32 devices in a mesh: gx: 8 (over z, x), gy: 2 (over y), gz: 2 (over core).
Axes of the slice: x: 2, y: 2, z: 4, core: 2. Of those that a mesh axis runs over, the one named last changes fastest.
Arguments:
- forward: float32 [19, 128, 32, 256], P(None, 'gx', 'gy', 'gz'), may hold values from 0.01 to 0.15
- adjoint: float32 [19, 128, 32, 256], P(None, 'gx', 'gy', 'gz'), may hold values from -1.2 to 1.2
- design: float32 [128, 32, 256], P('gx', 'gy', 'gz'), may hold values from 0 to 1
- mask: int32 [128, 32, 256], P('gx', 'gy', 'gz'), may hold values from 0 to 3
Outputs:
- adjoint_next: float32 [19, 128, 32, 256], P(None, 'gx', 'gy', 'gz')
- sensitivity: float32 [128, 32, 256], P('gx', 'gy', 'gz')
The draws below stay inside these ranges and needn't reach their ends.
All inputs are finite; a program needn't handle non-finite values.
Results may differ from the reference program's by a relative error of at most 0.0003.
Values sent between devices are 32-bit elements; how exact they have to be, the bound alone decides.
No kernel may reach another device: no remote copies, remote signals or barrier semaphores. Data moves between devices by JAX's collectives and lax.ppermute only.
A program may use at most 64 MiB of HBM per device.

```python
import math
import jax
import jax.numpy as jnp
from jax import lax

Q = 19
RADIUS = 8
NX = 128
NY = 32
NZ = 256


def touch_ends(array, rng, low, largest):
    spot = [jax.random.randint(jax.random.fold_in(rng, axis), (), 0, length) for axis, length in enumerate(array.shape)]
    longest = array.shape.index(max(array.shape))
    neighbour = spot[:longest] + [(spot[longest] + 1) % array.shape[longest]] + spot[longest + 1:]
    return array.at[tuple(spot)].set(low).at[tuple(neighbour)].set(largest)


def level_of(key, shape, pieces, smallest, largest):
    def one(dim, blocks):
        steps = jax.random.uniform(jax.random.fold_in(jax.random.fold_in(key, 6), dim), (blocks,), jnp.float32, smallest / len(pieces), largest / len(pieces))
        return jnp.repeat(jnp.exp(steps), shape[dim] // blocks).reshape((-1,) + (1,) * (len(shape) - dim - 1))

    loudness = one(*pieces[0])
    for cut in pieces[1:]:
        loudness = loudness * one(*cut)
    return loudness


def gaussian(own_key, shape, width, limit, split=(), dtype=jnp.bfloat16):
    array = jax.random.normal(own_key, shape, jnp.float32) * width
    if len(split) > 0:
        array = level_of(own_key, shape, split, -0.22, 0.18) * array
    return jnp.clip(array, min=-limit, max=limit).astype(dtype)


def setup_inputs(seed: int = 0) -> dict:
    streams_of = jax.random.split(jax.random.key(seed), 5)
    forward = jnp.clip(0.01 + 0.14 * jax.random.uniform(streams_of[0], (Q, NX, NY, NZ), jnp.float32) ** level_of(streams_of[0], (Q, NX, NY, NZ), ((1, 8), (2, 2), (3, 2)), -0.2, 0.2), 0.01, 0.15)
    adjoint = gaussian(streams_of[1], (Q, NX, NY, NZ), 0.2, 1.2, ((1, 8), (2, 2), (3, 2)), jnp.float32)
    design = jnp.clip(1.0 * jax.random.uniform(streams_of[2], (NX, NY, NZ), jnp.float32) ** level_of(streams_of[2], (NX, NY, NZ), ((0, 8), (1, 2), (2, 2)), -0.2, 0.2), 0.0, 1.0)
    mask = touch_ends(jax.random.randint(streams_of[3], (NX, NY, NZ), 0, 4), jax.random.fold_in(streams_of[3], 1), 0, 3).astype(jnp.int32)
    return dict(forward=forward, adjoint=adjoint, design=design, mask=mask)


velocity = [(0, 0, 0), (1, 0, 0), (-1, 0, 0), (0, 1, 0), (0, -1, 0), (0, 0, 1), (0, 0, -1),
            (1, 1, 0), (-1, -1, 0), (1, -1, 0), (-1, 1, 0), (1, 0, 1), (-1, 0, -1),
            (1, 0, -1), (-1, 0, 1), (0, 1, 1), (0, -1, -1), (0, 1, -1), (0, -1, 1)]
lattice_weight = [1.0 / 3.0] + [1.0 / 18.0] * 6 + [1.0 / 36.0] * 12
opposite = [0, 2, 1, 4, 3, 6, 5, 8, 7, 10, 9, 12, 11, 14, 13, 16, 15, 18, 17]
relax_rate = 1.25
sharpness = 64.0
threshold = 0.5
damping_max = 10.0
ramp_shape = 0.1


def tap_weights():
    spread_width = RADIUS / 2.0
    unscaled = [math.exp(-((k - RADIUS) ** 2) / (2.0 * spread_width * spread_width)) for k in range(2 * RADIUS + 1)]
    summed = sum(unscaled)
    return [v / summed for v in unscaled]


def filter_along(padded, along, length_out):
    weights = tap_weights()
    result = weights[0] * lax.slice_in_dim(padded, 0, length_out, axis=along)
    for k in range(1, 2 * RADIUS + 1):
        result = result + weights[k] * lax.slice_in_dim(padded, k, k + length_out, axis=along)
    return result


def smooth(field):
    for along in range(3):
        widths = [(0, 0), (0, 0), (0, 0)]
        widths[along] = (RADIUS, RADIUS)
        field = filter_along(jnp.pad(field, widths), along, field.shape[along])
    return field


def project(filtered):
    base = math.tanh(sharpness * threshold)
    denominator = base + math.tanh(sharpness * (1.0 - threshold))
    inner = jnp.tanh(sharpness * (filtered - threshold))
    physical = (base + inner) / denominator
    steep = sharpness * (1.0 - inner * inner) / denominator
    return physical, steep


def ramp(physical):
    damping = damping_max * ramp_shape * (1.0 - physical) / (ramp_shape + physical)
    slope = -damping_max * ramp_shape * (1.0 + ramp_shape) / ((ramp_shape + physical) * (ramp_shape + physical))
    return damping, slope


def weighted_sum(members, factors):
    result = None
    for member, factor in zip(members, factors):
        if factor == 0:
            continue
        addend = factor * member
        result = addend if result is None else result + addend
    return result


def collide(pulled, forward, mask, damping, slope):
    forward_list = [forward[q] for q in range(Q)]
    density = weighted_sum(forward_list, [1.0] * Q)
    vel = [weighted_sum(forward_list, [float(d[a]) for d in velocity]) / density for a in range(3)]
    speed_sq = vel[0] * vel[0] + vel[1] * vel[1] + vel[2] * vel[2]
    zeroth = weighted_sum(pulled, lattice_weight)
    first = [weighted_sum(pulled, [w * d[a] for w, d in zip(lattice_weight, velocity)]) for a in range(3)]
    second = [[weighted_sum(pulled, [w * d[a] * d[b] for w, d in zip(lattice_weight, velocity)]) for b in range(3)] for a in range(3)]
    quadric = None
    for a in range(3):
        for b in range(3):
            addend = vel[a] * vel[b] * second[a][b]
            quadric = addend if quadric is None else quadric + addend
    eq_scalar = zeroth * (1.0 + 1.5 * speed_sq) - 4.5 * quadric
    eq_vector = [3.0 * first[a] + 9.0 * (second[a][0] * vel[0] + second[a][1] * vel[1] + second[a][2] * vel[2]) - 3.0 * zeroth * vel[a] for a in range(3)]
    moment = [weighted_sum(pulled, [float(d[a]) for d in velocity]) for a in range(3)]
    source = slope * (speed_sq - (vel[0] * moment[0] + vel[1] * moment[1] + vel[2] * moment[2]))
    outputs = []
    for q in range(Q):
        step_dir = velocity[q]
        along_eq = eq_scalar
        along_vel = 0.0
        for a in range(3):
            if step_dir[a] != 0:
                along_eq = along_eq + step_dir[a] * eq_vector[a]
                along_vel = along_vel + step_dir[a] * vel[a]
        own = pulled[q]
        fluid = (1.0 - relax_rate) * own + relax_rate * along_eq + 2.0 * damping * (along_vel - speed_sq) / density
        solid = pulled[opposite[q]]
        value = jnp.where(mask == 0, fluid, jnp.where(mask == 1, solid, jnp.where(mask == 2, along_eq, eq_scalar)))
        outputs.append(value)
    return jnp.stack(outputs), source


def reference(forward, adjoint, design, mask):
    filtered = smooth(design)
    physical, steep = project(filtered)
    damping, slope = ramp(physical)
    padded = jnp.pad(adjoint, ((0, 0), (1, 1), (1, 1), (1, 1)))
    extent = adjoint.shape[1:]
    pulled = []
    for q in range(Q):
        step_dir = velocity[q]
        begin = (1 + step_dir[0], 1 + step_dir[1], 1 + step_dir[2])
        pulled.append(lax.slice(padded[q], begin, (begin[0] + extent[0], begin[1] + extent[1], begin[2] + extent[2])))
    adjoint_next, source = collide(pulled, forward, mask, damping, slope)
    sensitivity = smooth(steep * source)
    return adjoint_next, sensitivity
```

```python
import functools
import math

import jax
import jax.numpy as jnp
import numpy as np
from jax import lax
from jax.experimental import pallas as pl
from jax.experimental.pallas import tpu as pltpu
from jax.sharding import PartitionSpec as P

Q = 19
R = 8

velocity = [
    (0, 0, 0),
    (1, 0, 0),
    (-1, 0, 0),
    (0, 1, 0),
    (0, -1, 0),
    (0, 0, 1),
    (0, 0, -1),
    (1, 1, 0),
    (-1, -1, 0),
    (1, -1, 0),
    (-1, 1, 0),
    (1, 0, 1),
    (-1, 0, -1),
    (1, 0, -1),
    (-1, 0, 1),
    (0, 1, 1),
    (0, -1, -1),
    (0, 1, -1),
    (0, -1, 1),
]
relax_rate = 1.25
sharpness = 64.0
threshold = 0.5
damping_max = 10.0
ramp_shape = 0.1


def fields_of(axis, sign):
    plus = [q for q in range(Q) if velocity[q][axis] == 1]
    return plus if sign > 0 else [q + 1 if q % 2 else q - 1 for q in plus]


PLUS = [fields_of(a, 1) for a in range(3)]
MINUS = [fields_of(a, -1) for a in range(3)]


def tap_weights():
    spread_width = R / 2.0
    unscaled = [math.exp(-((k - R) ** 2) / (2.0 * spread_width * spread_width)) for k in range(2 * R + 1)]
    summed = sum(unscaled)
    return [v / summed for v in unscaled]


TAPS = tap_weights()


def band(length):
    out = np.zeros((3, length, length), np.float32)
    for i in range(length):
        for k in range(-R, R + 1):
            j = i + k
            if j < 0:
                out[1, j + length, i] = TAPS[k + R]
            elif j >= length:
                out[2, j - length, i] = TAPS[k + R]
            else:
                out[0, j, i] = TAPS[k + R]
    return out


def sides(parity, even, odd):
    zero = jnp.zeros_like(even)
    if odd is None:
        return jnp.where(parity == 0, zero, even), jnp.where(parity == 0, even, zero)
    return jnp.where(parity == 0, odd, even), jnp.where(parity == 0, even, odd)


def parity_of(axis):
    return lax.rem(lax.axis_index(axis), 2)


def exchange(axis, count, even, odd):
    got_odd = None
    if odd is not None:
        pairs = [(i, i + 1) for i in range(1, count - 1, 2)]
        got_odd = lax.ppermute(odd, axis, pairs + [(b, a) for a, b in pairs])
    pairs = [(i, i + 1) for i in range(0, count - 1, 2)]
    got_even = lax.ppermute(even, axis, pairs + [(b, a) for a, b in pairs])
    return got_even, got_odd


def vmem(count):
    return [pl.BlockSpec(memory_space=pltpu.VMEM)] * count


def f32(*shape):
    return jax.ShapeDtypeStruct(shape, jnp.float32)


def call(body, outs, args, specs=None, scratch=(), limit=16, flops=1e6, moved=1e6, **rest):
    return pl.pallas_call(
        body,
        out_shape=outs,
        in_specs=specs or vmem(len(args)),
        out_specs=rest.pop("out_specs", tuple(vmem(len(outs)))),
        scratch_shapes=list(scratch),
        compiler_params=pltpu.CompilerParams(vmem_limit_bytes=limit * 2**20),
        cost_estimate=pl.CostEstimate(flops=int(flops), bytes_accessed=int(moved), transcendentals=0),
        **rest,
    )(*args)


def filter_rows(load):
    total = TAPS[R] * load(R)
    for k in range(R):
        total = total + TAPS[k] * (load(k) + load(2 * R - k))
    return total


def dot(a, b):
    return jnp.dot(a, b, preferred_element_type=jnp.float32, precision=lax.Precision.HIGHEST)


def row_of(ref, at):
    return ref[pl.ds(at, 1), :]


class Pull:
    def __init__(self, adj, dims, py, y_even, y_odd, pz=None, z_even=None, z_odd=None):
        self.adj, self.dims = adj, dims
        self.py, self.y_even, self.y_odd = py, y_even, y_odd
        self.pz, self.z_even, self.z_odd = pz, z_even, z_odd
        X, Y, Z = dims
        self.row = lax.broadcasted_iota(jnp.int32, (Y, Z), 0)
        self.lane = lax.broadcasted_iota(jnp.int32, (Y, Z), 1)

    def along_y(self, q, x):
        X, Y, Z = self.dims
        here = self.adj[q, x]
        cy = velocity[q][1]
        if cy == 0:
            return here
        at = X * R + X * (PLUS if cy > 0 else MINUS)[1].index(q) + x
        even = row_of(self.y_even, at)
        odd = None if self.y_odd is None else row_of(self.y_odd, at)
        below, above = sides(self.py, even, odd)
        if cy > 0:
            return jnp.where(self.row == Y - 1, above, pltpu.roll(here, Y - 1, 0))
        return jnp.where(self.row == 0, below, pltpu.roll(here, 1, 0))

    def faces(self, x):
        even = self.z_even[x]
        odd = None if self.z_odd is None else self.z_odd[x]
        return sides(self.pz, even, odd)

    def both(self, q, x, faces):
        X, Y, Z = self.dims
        here = self.along_y(q, x)
        cz = velocity[q][2]
        if cz == 0:
            return here
        below, above = faces
        if cz > 0:
            j = PLUS[2].index(q)
            face = pltpu.roll(above, 4 - j, 1) if j != 4 else above
            return jnp.where(self.lane == Z - 1, face, pltpu.roll(here, Z - 1, 1))
        j = MINUS[2].index(q)
        face = pltpu.roll(below, Z - j, 1) if j else below
        return jnp.where(self.lane == 0, face, pltpu.roll(here, 1, 1))


def refs_of(refs, odd):
    even = next(refs)
    return even, (next(refs) if odd else None)


def pack_y(dims, many, adj, design, *rest):
    X, Y, Z = dims
    outs = rest[: 1 + many]
    tiles, sems = rest[1 + many :]
    py = parity_of("gy")

    def fill(n, out, up):
        names = (MINUS if up else PLUS)[1]
        first = Y - R if up else 0
        copies = [
            pltpu.make_async_copy(adj.at[q, :, pl.ds(first, R), :], tiles.at[n, j], sems.at[n, j])
            for j, q in enumerate(names)
        ]
        for c in copies:
            c.start()
        out[: X * R, :] = design[:, first : first + R, :].reshape(X * R, Z)
        for c in copies:
            c.wait()
        for j in range(5):
            out[X * R + X * j : X * R + X * (j + 1), :] = tiles[n, j, :, R - 1 if up else 0, :]

    for n, out in enumerate(outs):

        @pl.when(py == n)
        def _(n=n, out=out):
            fill(n, out, True)

        @pl.when(py != n)
        def _(n=n, out=out):
            fill(n, out, False)


def flow(forward, out):
    members = [forward[q] for q in range(Q)]
    rho = members[0]
    for q in range(1, Q):
        rho = rho + members[q]
    inverse = 1.0 / rho
    for a in range(3):
        total = None
        for q in range(1, Q, 2):
            c = velocity[q][a]
            if c == 0:
                continue
            term = members[q] - members[q + 1]
            term = term if c > 0 else -term
            total = term if total is None else total + term
        out[a] = total * inverse
    out[3] = inverse


def extend_y(dims, pad, own, py, even, odd):
    X, Y, Z = dims
    below, above = sides(py, even, odd)
    pad[:, :R, :] = below
    pad[:, R : R + Y, :] = own
    pad[:, R + Y :, :] = above


def filter_y(dims, pad, store, step=2):
    X, Y, Z = dims
    for x in range(0, X, step):
        store(x, filter_rows(lambda k: pad[x : x + step, k : k + Y, :]))


def design_y(dims, many_y, many_z, adj, design, *rest):
    X, Y, Z = dims
    rest = iter(rest)
    y_even, y_odd = refs_of(rest, many_y)
    filtered = next(rest)
    outs = [next(rest) for _ in range(1 + many_z)]
    pad, held, sems = rest
    pz = parity_of("gz")
    py = parity_of("gy")

    def fetch(up, n):
        names = (MINUS if up else PLUS)[2]
        return [
            pltpu.make_async_copy(adj.at[q], held.at[n, j], sems.at[n, j]) for j, q in enumerate(names)
        ]

    for n, out in enumerate(outs):

        @pl.when(pz == n)
        def _(n=n):
            for c in fetch(True, n):
                c.start()

        @pl.when(pz != n)
        def _(n=n):
            for c in fetch(False, n):
                c.start()

    def halo(ref):
        return ref[: X * R, :].reshape(X, R, Z)

    extend_y(dims, pad, design[...], py, halo(y_even), None if y_odd is None else halo(y_odd))

    def store(x, value):
        filtered[x : x + value.shape[0]] = value

    filter_y(dims, pad, store)

    def fill(out, up, n):
        names = (MINUS if up else PLUS)[2]
        for c in fetch(up, n):
            c.wait()
        by_name = {q: held.at[n, j] for j, q in enumerate(names)}

        class Held:
            def __getitem__(self, at):
                return by_name[at[0]][at[1]]

        pull = Pull(Held(), dims, py, y_even, y_odd)

        def layer(x, _):
            value = filtered[x]
            for j, q in enumerate(names):
                slot = j if up else Z - 5 + j
                shift = (slot - (Z - 1 if up else 0)) % Z
                value = jnp.where(pull.lane == slot, pltpu.roll(pull.along_y(q, x), shift, 1), value)
            out[x] = value
            return 0

        lax.fori_loop(0, X, layer, 0, unroll=2)

    for n, out in enumerate(outs):

        @pl.when(pz == n)
        def _(n=n, out=out):
            fill(out, True, n)

        @pl.when(pz != n)
        def _(n=n, out=out):
            fill(out, False, n)


def signed(terms):
    total = None
    for sign, value in terms:
        value = value if sign > 0 else -value
        total = value if total is None else total + value
    return total


def moment_of(values):
    return [
        signed([(velocity[q][a], v) for q, v in values.items() if velocity[q][a] != 0]) for a in range(3)
    ]


def filter_z(weights, own, pz, even, odd):
    value = dot(own, weights[0]) + dot(even, jnp.where(pz == 0, weights[2], weights[1]))
    if odd is not None:
        value = value + dot(odd, jnp.where(pz == 0, weights[1], weights[2]))
    return value


def pack_x(dims, many_x, many_y, many_z, adj, weights, filtered_y, flow_ref, *rest):
    X, Y, Z = dims
    rest = iter(rest)
    y_even, y_odd = refs_of(rest, many_y)
    z_even, z_odd = refs_of(rest, many_z)
    outs = [next(rest) for _ in range(1 + many_x)]
    factor = next(rest)
    local, rising, falling, sems = rest
    px, py, pz = parity_of("gx"), parity_of("gy"), parity_of("gz")
    part = X // 4
    copies = [
        pltpu.make_async_copy(
            adj.at[:, pl.ds(i * part, part)], local.at[:, pl.ds(i * part, part)], sems.at[i]
        )
        for i in range(4)
    ]
    for c in copies:
        c.start()
    smooth = filter_z(
        weights,
        filtered_y[...].reshape(X * Y, Z),
        pz,
        z_even[...].reshape(X * Y, Z),
        None if z_odd is None else z_odd[...].reshape(X * Y, Z),
    )
    for out in outs:
        out[: X * Y, :] = smooth
    pull = Pull(local, dims, py, y_even, y_odd, pz, z_even, z_odd)

    def layer(x, _):
        faces = pull.faces(x)
        groups = {}
        for q in range(1, Q):
            groups.setdefault(velocity[q][0], {})[q] = pull.both(q, x, faces)
        level = moment_of(groups[0])
        up = moment_of(groups[1])
        down = moment_of(groups[-1])
        for a in range(3):
            rising[a, x] = up[a]
            falling[a, x + 2] = down[a]
        vel = [flow_ref[a, x] for a in range(3)]
        factor[x] = vel[0] * vel[0] + vel[1] * vel[1] + vel[2] * vel[2] - vel[1] * level[1] - vel[2] * level[2]
        return 0

    zero = jnp.zeros((Y, Z), jnp.float32)
    for a in range(3):
        rising[a, X] = zero
        falling[a, 1] = zero
    for i, c in enumerate(copies):
        c.wait()
        lax.fori_loop(i * part, (i + 1) * part, layer, 0)

    def finish(x, _):
        total = factor[x]
        for a in range(3):
            total = total - flow_ref[a, x] * (rising[a, x + 1] + falling[a, x + 1])
        factor[x] = total
        return 0

    lax.fori_loop(0, X, finish, 0, unroll=4)

    def fill(out, up):
        names = (MINUS if up else PLUS)[0]
        edge = X - 1 if up else 0
        at = X * Y
        first = X - R if up else 0
        out[at : at + R * Y, :] = factor[first : first + R].reshape(R * Y, Z)
        at += R * Y
        faces = pull.faces(edge)
        for q in names:
            out[at : at + Y, :] = pull.both(q, edge, faces)
            at += Y
        for a in range(3):
            out[at : at + Y, :] = flow_ref[a, edge]
            at += Y

    for n, out in enumerate(outs):

        @pl.when(px == n)
        def _(out=out):
            fill(out, True)

        @pl.when(px != n)
        def _(out=out):
            fill(out, False)


def project(filtered):
    base = math.tanh(sharpness * threshold)
    denominator = base + math.tanh(sharpness * (1.0 - threshold))
    inner = jnp.tanh(sharpness * (filtered - threshold))
    physical = (base + inner) * (1.0 / denominator)
    steep = (sharpness / denominator) * (1.0 - inner * inner)
    inverse = 1.0 / (ramp_shape + physical)
    return physical, steep, inverse


def source(dims, many_x, many_y, factor, flow_ref, *rest):
    X, Y, Z = dims
    rest = iter(rest)
    own_even, own_odd = refs_of(rest, many_x)
    x_even, x_odd = refs_of(rest, many_x)
    result, damp = next(rest), next(rest)
    outs = [next(rest) for _ in range(1 + many_y)]
    layers, ext = rest
    px, py = parity_of("gx"), parity_of("gy")
    size = X * Y
    g_at, u_at, v_at = size, size + R * Y, size + R * Y + 5 * Y

    def got(at, count):
        return sides(px, x_even[at : at + count, :], None if x_odd is None else x_odd[at : at + count, :])

    def own(at, count):
        return sides(px, own_even[at : at + count, :], None if own_odd is None else own_odd[at : at + count, :])

    below, above = got(0, size)
    layers[:X] = below.reshape(X, Y, Z)
    layers[X : 2 * X] = own_even[:size, :].reshape(X, Y, Z)
    layers[2 * X :] = above.reshape(X, Y, Z)

    below, above = got(g_at, R * Y)
    ext[:R] = below.reshape(R, Y, Z)
    ext[R : R + X] = factor[...]
    ext[R + X :] = above.reshape(R, Y, Z)

    def face_moment(block, names):
        return moment_of({q: block[j * Y : (j + 1) * Y] for j, q in enumerate(names)})

    def less(at, vel, moment):
        ext[at] = ext[at] - (vel[0] * moment[0] + vel[1] * moment[1] + vel[2] * moment[2])

    got_low, got_high = got(u_at, 5 * Y)
    own_low, own_high = own(u_at, 5 * Y)
    vel_low, vel_high = got(v_at, 3 * Y)
    less(R - 1, [vel_low[a * Y : (a + 1) * Y] for a in range(3)], face_moment(own_low, PLUS[0]))
    less(R, [flow_ref[a, 0] for a in range(3)], face_moment(got_low, MINUS[0]))
    less(R + X - 1, [flow_ref[a, X - 1] for a in range(3)], face_moment(got_high, PLUS[0]))
    less(R + X, [vel_high[a * Y : (a + 1) * Y] for a in range(3)], face_moment(own_high, MINUS[0]))

    slope = -damping_max * ramp_shape * (1.0 + ramp_shape)
    base = X - 2 * R

    def layer(e, _):
        smooth = filter_rows(lambda k: layers[base + e + k])
        physical, steep, inverse = project(smooth)
        ext[e] = (slope * steep) * (inverse * inverse) * ext[e]

        @pl.when((e >= R) & (e < R + X))
        def _():
            damp[e - R] = (2.0 * damping_max * ramp_shape) * (1.0 - physical) * inverse

        return 0

    lax.fori_loop(0, X + 2 * R, layer, 0, unroll=2)

    def last(x, _):
        result[x] = filter_rows(lambda k: ext[x + k])
        return 0

    lax.fori_loop(0, X, last, 0, unroll=2)
    for n, out in enumerate(outs):

        @pl.when(py == n)
        def _(out=out):
            out[...] = result[:, Y - R :, :]

        @pl.when(py != n)
        def _(out=out):
            out[...] = result[:, :R, :]


def smooth_y(dims, many_y, own, *rest):
    rest = iter(rest)
    y_even, y_odd = refs_of(rest, many_y)
    result, pad = rest
    extend_y(dims, pad, own[...], parity_of("gy"), y_even[...], None if y_odd is None else y_odd[...])

    def store(x, value):
        result[x : x + value.shape[0]] = value

    filter_y(dims, pad, store)


def smooth_z(dims, many_z, weights, own, *rest):
    X, Y, Z = dims
    rest = iter(rest)
    z_even, z_odd = refs_of(rest, many_z)
    (result,) = rest
    value = filter_z(
        weights,
        own[...].reshape(X * Y, Z),
        parity_of("gz"),
        z_even[...].reshape(X * Y, Z),
        None if z_odd is None else z_odd[...].reshape(X * Y, Z),
    )
    result[...] = value.reshape(X, Y, Z)


def collide(dims, many_x, many_y, many_z, step, adj, flow_ref, damp, mask, *rest):
    X, Y, Z = dims
    rest = iter(rest)
    y_even, y_odd = refs_of(rest, many_y)
    z_even, z_odd = refs_of(rest, many_z)
    x_even, x_odd = refs_of(rest, many_x)
    (out,) = rest
    px, py, pz = parity_of("gx"), parity_of("gy"), parity_of("gz")
    pull = Pull(adj, dims, py, y_even, y_odd, pz, z_even, z_odd)
    begin = pl.program_id(0) * step
    u_at = X * Y + R * Y

    def layer(i, _):
        x = begin + i
        around = {c: pull.faces(jnp.clip(x + c, 0, X - 1)) for c in (-1, 0, 1)}
        pulled = []
        for q in range(Q):
            cx = velocity[q][0]
            value = pull.both(q, jnp.clip(x + cx, 0, X - 1), around[cx])
            if cx != 0:
                at = u_at + Y * (PLUS if cx > 0 else MINUS)[0].index(q)
                below, above = sides(
                    px, x_even[at : at + Y, :], None if x_odd is None else x_odd[at : at + Y, :]
                )
                value = jnp.where(x == (X - 1 if cx > 0 else 0), above if cx > 0 else below, value)
            pulled.append(value)
        vel = [flow_ref[a, x] for a in range(3)]
        inverse = flow_ref[3, x]
        speed_sq = vel[0] * vel[0] + vel[1] * vel[1] + vel[2] * vel[2]
        plus = {q: pulled[q] + pulled[q + 1] for q in range(1, Q, 2)}
        minus = {q: pulled[q] - pulled[q + 1] for q in range(1, Q, 2)}
        axes = (1, 3, 5)
        straight = plus[1] + plus[3] + plus[5]
        slanted = plus[7] + plus[9] + plus[11] + plus[13] + plus[15] + plus[17]
        zeroth = (1.0 / 3.0) * pulled[0] + (1.0 / 18.0) * straight + (1.0 / 36.0) * slanted
        first, diagonal = [], []
        for a in range(3):
            terms = [(velocity[q][a], minus[q]) for q in range(7, Q, 2) if velocity[q][a] != 0]
            first.append((1.0 / 18.0) * minus[axes[a]] + (1.0 / 36.0) * signed(terms))
            both = [(1, plus[q]) for q in range(7, Q, 2) if velocity[q][a] != 0]
            diagonal.append((1.0 / 18.0) * plus[axes[a]] + (1.0 / 36.0) * signed(both))
        xy = (1.0 / 36.0) * (plus[7] - plus[9])
        xz = (1.0 / 36.0) * (plus[11] - plus[13])
        yz = (1.0 / 36.0) * (plus[15] - plus[17])
        turned = [
            diagonal[0] * vel[0] + xy * vel[1] + xz * vel[2],
            xy * vel[0] + diagonal[1] * vel[1] + yz * vel[2],
            xz * vel[0] + yz * vel[1] + diagonal[2] * vel[2],
        ]
        quadric = vel[0] * turned[0] + vel[1] * turned[1] + vel[2] * turned[2]
        eq_scalar = zeroth * (1.0 + 1.5 * speed_sq) - 4.5 * quadric
        eq_vector = [3.0 * first[a] + 9.0 * turned[a] - 3.0 * zeroth * vel[a] for a in range(3)]
        label = mask[x]
        drag = damp[x] * inverse
        fluid, solid, inlet = label == 0, label == 1, label == 2
        zero = jnp.zeros_like(drag)
        keep = jnp.where(fluid, 1.0 - relax_rate, zero)
        bounce = jnp.where(solid, 1.0, zero)
        level = jnp.where(fluid, relax_rate * eq_scalar - drag * speed_sq, jnp.where(solid, zero, eq_scalar))
        tilt = [
            jnp.where(fluid, relax_rate * eq_vector[a] + drag * vel[a], jnp.where(inlet, eq_vector[a], zero))
            for a in range(3)
        ]
        out[0, i] = (keep + bounce) * pulled[0] + level
        for q in range(1, Q, 2):
            lean = signed([(velocity[q][a], tilt[a]) for a in range(3) if velocity[q][a] != 0])
            out[q, i] = keep * pulled[q] + bounce * pulled[q + 1] + (level + lean)
            out[q + 1, i] = keep * pulled[q + 1] + bounce * pulled[q] + (level - lean)
        return 0

    lax.fori_loop(0, step, layer, 0)


def local(counts, forward, adjoint, design, mask):
    many_x, many_y, many_z = (int(n > 2) for n in counts)
    nx, ny, nz = counts
    dims = design.shape
    X, Y, Z = dims
    weights = jnp.asarray(band(Z))
    any_space = pl.BlockSpec(memory_space=pl.ANY)
    cells = X * Y * Z
    some = lambda pair: [v for v in pair if v is not None]
    pair = lambda items: (items[0], items[1] if len(items) > 1 else None)
    dma = pltpu.SemaphoreType.DMA

    y_rows = X * R + 5 * X
    to_y = call(
        functools.partial(pack_y, dims, many_y),
        [f32(y_rows, Z)] * (1 + many_y),
        (adjoint, design),
        [any_space] + vmem(1),
        [pltpu.VMEM((1 + many_y, 5, X, R, Z), jnp.float32), dma((1 + many_y, 5))],
        limit=4,
        name="pack_y",
    )
    got_y = some(exchange("gy", ny, *pair(to_y)))

    step = 4
    flow_values = call(
        flow,
        f32(4, X, Y, Z),
        (forward,),
        [pl.BlockSpec((Q, step, Y, Z), lambda i: (0, i, 0, 0))],
        out_specs=pl.BlockSpec((4, step, Y, Z), lambda i: (0, i, 0, 0)),
        grid=(X // step,),
        flops=40 * cells,
        moved=23 * 4 * cells,
        name="flow",
    )

    to_z = call(
        functools.partial(design_y, dims, many_y, many_z),
        [f32(X, Y, Z)] * (2 + many_z),
        (adjoint, design, *got_y),
        [any_space] + vmem(1 + len(got_y)),
        [
            pltpu.VMEM((X, Y + 2 * R, Z), jnp.float32),
            pltpu.VMEM((1 + many_z, 5, X, Y, Z), jnp.float32),
            dma((1 + many_z, 5)),
        ],
        limit=8,
        name="design_y",
    )
    filtered_y = to_z[0]
    got_z = some(exchange("gz", nz, *pair(to_z[1:])))

    x_rows = X * Y + R * Y + 8 * Y
    *to_x, factor = call(
        functools.partial(pack_x, dims, many_x, many_y, many_z),
        [f32(x_rows, Z)] * (1 + many_x) + [f32(X, Y, Z)],
        (adjoint, weights, filtered_y, flow_values, *got_y, *got_z),
        [any_space] + vmem(3 + len(got_y) + len(got_z)),
        [
            pltpu.VMEM((Q, X, Y, Z), jnp.float32),
            pltpu.VMEM((3, X + 2, Y, Z), jnp.float32),
            pltpu.VMEM((3, X + 2, Y, Z), jnp.float32),
            dma((4,)),
        ],
        limit=16,
        name="pack_x",
    )
    got_x = some(exchange("gx", nx, *pair(to_x)))

    result, damp, *to_y = call(
        functools.partial(source, dims, many_x, many_y),
        [f32(X, Y, Z), f32(X, Y, Z)] + [f32(X, R, Z)] * (1 + many_y),
        (factor, flow_values, *to_x, *got_x),
        None,
        [pltpu.VMEM((3 * X, Y, Z), jnp.float32), pltpu.VMEM((X + 2 * R, Y, Z), jnp.float32)],
        limit=8,
        name="source",
    )
    got_y2 = some(exchange("gy", ny, *pair(to_y)))

    whole = pl.BlockSpec(memory_space=pltpu.VMEM)
    adjoint_next = call(
        functools.partial(collide, dims, many_x, many_y, many_z, step),
        f32(Q, X, Y, Z),
        (adjoint, flow_values, damp, mask, *got_y, *got_z, *got_x),
        [whole] * (4 + len(got_y) + len(got_z) + len(got_x)),
        out_specs=pl.BlockSpec((Q, step, Y, Z), lambda i: (0, i, 0, 0)),
        grid=(X // step,),
        limit=16,
        flops=300 * cells,
        moved=44 * 4 * cells,
        name="collide",
    )

    (filtered_xy,) = call(
        functools.partial(smooth_y, dims, many_y),
        [f32(X, Y, Z)],
        (result, *got_y2),
        None,
        [pltpu.VMEM((X, Y + 2 * R, Z), jnp.float32)],
        limit=4,
        name="smooth_y",
    )
    got_z2 = some(exchange("gz", nz, filtered_xy, filtered_xy if many_z else None))
    (sensitivity,) = call(
        functools.partial(smooth_z, dims, many_z),
        [f32(X, Y, Z)],
        (weights, filtered_xy, *got_z2),
        limit=4,
        name="smooth_z",
    )
    return adjoint_next, sensitivity


def solution(mesh):
    counts = tuple(mesh.shape[a] for a in ("gx", "gy", "gz"))
    populations, field = P(None, "gx", "gy", "gz"), P("gx", "gy", "gz")
    return jax.shard_map(
        functools.partial(local, counts),
        mesh=mesh,
        in_specs=(populations, populations, field, field),
        out_specs=(populations, field),
        check_vma=False,
    )
```

```python
import functools
import math

import jax
import jax.numpy as jnp
import numpy as np
from jax import lax
from jax.experimental import pallas as pl
from jax.experimental.pallas import tpu as pltpu
from jax.sharding import PartitionSpec as P

Q = 19
R = 8

velocity = [
    (0, 0, 0),
    (1, 0, 0),
    (-1, 0, 0),
    (0, 1, 0),
    (0, -1, 0),
    (0, 0, 1),
    (0, 0, -1),
    (1, 1, 0),
    (-1, -1, 0),
    (1, -1, 0),
    (-1, 1, 0),
    (1, 0, 1),
    (-1, 0, -1),
    (1, 0, -1),
    (-1, 0, 1),
    (0, 1, 1),
    (0, -1, -1),
    (0, 1, -1),
    (0, -1, 1),
]
relax_rate = 1.25
sharpness = 64.0
threshold = 0.5
damping_max = 10.0
ramp_shape = 0.1


def fields_of(axis, sign):
    plus = [q for q in range(Q) if velocity[q][axis] == 1]
    return plus if sign > 0 else [q + 1 if q % 2 else q - 1 for q in plus]


PLUS = [fields_of(a, 1) for a in range(3)]
MINUS = [fields_of(a, -1) for a in range(3)]


def tap_weights():
    spread_width = R / 2.0
    unscaled = [math.exp(-((k - R) ** 2) / (2.0 * spread_width * spread_width)) for k in range(2 * R + 1)]
    summed = sum(unscaled)
    return [v / summed for v in unscaled]


TAPS = tap_weights()


def band(length):
    out = np.zeros((3, length, length), np.float32)
    for i in range(length):
        for k in range(-R, R + 1):
            j = i + k
            if j < 0:
                out[1, j + length, i] = TAPS[k + R]
            elif j >= length:
                out[2, j - length, i] = TAPS[k + R]
            else:
                out[0, j, i] = TAPS[k + R]
    return out


def sides(parity, even, odd):
    zero = jnp.zeros_like(even)
    if odd is None:
        return jnp.where(parity == 0, zero, even), jnp.where(parity == 0, even, zero)
    return jnp.where(parity == 0, odd, even), jnp.where(parity == 0, even, odd)


def parity_of(axis):
    return lax.rem(lax.axis_index(axis), 2)


def exchange(axis, count, even, odd):
    got_odd = None
    if odd is not None:
        pairs = [(i, i + 1) for i in range(1, count - 1, 2)]
        got_odd = lax.ppermute(odd, axis, pairs + [(b, a) for a, b in pairs])
    pairs = [(i, i + 1) for i in range(0, count - 1, 2)]
    got_even = lax.ppermute(even, axis, pairs + [(b, a) for a, b in pairs])
    return got_even, got_odd


def vmem(count):
    return [pl.BlockSpec(memory_space=pltpu.VMEM)] * count


def in_hbm(array):
    return pltpu.with_memory_space_constraint(array, pltpu.HBM)


def f32(*shape):
    return jax.ShapeDtypeStruct(shape, jnp.float32)


def call(body, outs, args, specs=None, scratch=(), limit=16, flops=1e6, moved=1e6, **rest):
    return pl.pallas_call(
        body,
        out_shape=outs,
        in_specs=specs or vmem(len(args)),
        out_specs=rest.pop("out_specs", tuple(vmem(len(outs)))),
        scratch_shapes=list(scratch),
        compiler_params=pltpu.CompilerParams(vmem_limit_bytes=limit * 2**20),
        cost_estimate=pl.CostEstimate(flops=int(flops), bytes_accessed=int(moved), transcendentals=0),
        **rest,
    )(*args)


def filter_rows(load):
    total = TAPS[R] * load(R)
    for k in range(R):
        total = total + TAPS[k] * (load(k) + load(2 * R - k))
    return total


def dot(a, b):
    return jnp.dot(a, b, preferred_element_type=jnp.float32, precision=lax.Precision.HIGHEST)


def row_of(ref, at):
    return ref[pl.ds(at, 1), :]


class Pull:
    def __init__(self, adj, dims, py, y_even, y_odd, pz=None, z_even=None, z_odd=None):
        self.adj, self.dims = adj, dims
        self.py, self.y_even, self.y_odd = py, y_even, y_odd
        self.pz, self.z_even, self.z_odd = pz, z_even, z_odd
        X, Y, Z = dims
        self.row = lax.broadcasted_iota(jnp.int32, (Y, Z), 0)
        self.lane = lax.broadcasted_iota(jnp.int32, (Y, Z), 1)

    def along_y(self, q, x):
        X, Y, Z = self.dims
        here = self.adj[q, x]
        cy = velocity[q][1]
        if cy == 0:
            return here
        at = X * R + X * (PLUS if cy > 0 else MINUS)[1].index(q) + x
        even = row_of(self.y_even, at)
        odd = None if self.y_odd is None else row_of(self.y_odd, at)
        below, above = sides(self.py, even, odd)
        if cy > 0:
            return jnp.where(self.row == Y - 1, above, pltpu.roll(here, Y - 1, 0))
        return jnp.where(self.row == 0, below, pltpu.roll(here, 1, 0))

    def faces(self, x):
        even = self.z_even[x]
        odd = None if self.z_odd is None else self.z_odd[x]
        return sides(self.pz, even, odd)

    def both(self, q, x, faces):
        X, Y, Z = self.dims
        here = self.along_y(q, x)
        cz = velocity[q][2]
        if cz == 0:
            return here
        below, above = faces
        if cz > 0:
            j = PLUS[2].index(q)
            face = pltpu.roll(above, 4 - j, 1) if j != 4 else above
            return jnp.where(self.lane == Z - 1, face, pltpu.roll(here, Z - 1, 1))
        j = MINUS[2].index(q)
        face = pltpu.roll(below, Z - j, 1) if j else below
        return jnp.where(self.lane == 0, face, pltpu.roll(here, 1, 1))


def refs_of(refs, odd):
    even = next(refs)
    return even, (next(refs) if odd else None)


def pack_y(dims, many, adj, design, *rest):
    X, Y, Z = dims
    outs = rest[: 1 + many]
    kept, tiles, sems, kept_sem = rest[1 + many :]
    py = parity_of("gy")
    keep = pltpu.make_async_copy(design, kept, kept_sem)
    keep.start()

    def copies(n, up):
        names = (MINUS if up else PLUS)[1]
        first = Y - R if up else 0
        return [
            pltpu.make_async_copy(adj.at[q, :, pl.ds(first, R), :], tiles.at[n, j], sems.at[n, j])
            for j, q in enumerate(names)
        ]

    def start(n, out, up):
        for c in copies(n, up):
            c.start()

    def fill(n, out, up):
        first = Y - R if up else 0
        out[: X * R, :] = kept[:, first : first + R, :].reshape(X * R, Z)
        for c in copies(n, up):
            c.wait()
        for j in range(5):
            out[X * R + X * j : X * R + X * (j + 1), :] = tiles[n, j, :, R - 1 if up else 0, :]

    def each(act):
        for n, out in enumerate(outs):
            pl.when(py == n)(functools.partial(act, n, out, True))
            pl.when(py != n)(functools.partial(act, n, out, False))

    each(start)
    keep.wait()
    each(fill)


def prepare(dims, many_z, ahead, forward, adj, *rest):
    X, Y, Z = dims
    rest = iter(rest)
    flow_ref, factor = next(rest), next(rest)
    outs = [next(rest) for _ in range(1 + many_z)]
    rising, falling, members_ref, sems = rest
    pz = parity_of("gz")
    part = X // 4
    copies = [
        pltpu.make_async_copy(
            forward.at[:, pl.ds(i * part, part)], members_ref.at[:, pl.ds(i * part, part)], sems.at[i]
        )
        for i in range(4)
    ]
    for c in copies:
        c.start()
    row = lax.broadcasted_iota(jnp.int32, (Y, Z), 0)
    lane = lax.broadcasted_iota(jnp.int32, (Y, Z), 1)
    zero = jnp.zeros((Y, Z), jnp.float32)

    def along_y(q, x):
        here, cy = adj[q, x], velocity[q][1]
        if cy == 0:
            return here
        return jnp.where(row == (Y - 1 if cy > 0 else 0), zero, pltpu.roll(here, (-cy) % Y, 0))

    def both(q, x):
        here, cz = along_y(q, x), velocity[q][2]
        if cz == 0:
            return here
        return jnp.where(lane == (Z - 1 if cz > 0 else 0), zero, pltpu.roll(here, (-cz) % Z, 1))

    def layer(x, _):
        members = [members_ref[q, x] for q in range(Q)]
        inverse = 1.0 / sum(members[1:], members[0])
        vel = [
            signed([(velocity[q][a], members[q] - members[q + 1]) for q in range(1, Q, 2) if velocity[q][a] != 0])
            * inverse
            for a in range(3)
        ]
        for a in range(3):
            flow_ref[a, x] = vel[a]
        flow_ref[3, x] = inverse
        groups = {}
        for q in range(1, Q):
            groups.setdefault(velocity[q][0], {})[q] = both(q, x)
        level, up, down = moment_of(groups[0]), moment_of(groups[1]), moment_of(groups[-1])
        for a in range(3):
            rising[a, x] = up[a]
            falling[a, x + 2] = down[a]
        factor[x] = vel[0] * vel[0] + vel[1] * vel[1] + vel[2] * vel[2] - vel[1] * level[1] - vel[2] * level[2]
        return 0

    for a in range(3):
        rising[a, X] = zero
        falling[a, 1] = zero
    for i, c in enumerate(copies):
        c.wait()
        lax.fori_loop(i * part, (i + 1) * part, layer, 0)

    def finish(x, _):
        total = factor[x]
        for a in range(3):
            total = total - flow_ref[a, x] * (rising[a, x + 1] + falling[a, x + 1])
        factor[x] = total
        return 0

    lax.fori_loop(0, X, finish, 0, unroll=4)

    def fill(out, up):
        names = (MINUS if up else PLUS)[2]

        def face(x, _):
            value = zero
            for j, q in enumerate(names):
                slot = slot_of(Z, up, j)
                value = jnp.where(lane == slot, pltpu.roll(along_y(q, x), shift_of(Z, up, j), 1), value)
            out[x] = value
            return 0

        lax.fori_loop(0, X, face, 0, unroll=2)

    for n, out in enumerate(outs):
        pl.when(pz == n)(functools.partial(fill, out, True))
        pl.when(pz != n)(functools.partial(fill, out, False))


def slot_of(Z, up, j):
    return j if up else Z - 5 + j


def shift_of(Z, up, j):
    return (slot_of(Z, up, j) - (Z - 1 if up else 0)) % Z


def extend_y(dims, pad, own, py, even, odd):
    X, Y, Z = dims
    below, above = sides(py, even, odd)
    pad[:, :R, :] = below
    pad[:, R : R + Y, :] = own
    pad[:, R + Y :, :] = above


def filter_y(dims, pad, store, step=2):
    X, Y, Z = dims
    for x in range(0, X, step):
        store(x, filter_rows(lambda k: pad[x : x + step, k : k + Y, :]))


def design_y(dims, many_y, many_z, design, *rest):
    X, Y, Z = dims
    rest = iter(rest)
    faces = [next(rest) for _ in range(1 + many_z)]
    y_even, y_odd = refs_of(rest, many_y)
    filtered = next(rest)
    outs = [next(rest) for _ in range(1 + many_z)]
    pad, edges = rest
    pz = parity_of("gz")
    py = parity_of("gy")

    def halo(ref):
        return ref[: X * R, :].reshape(X, R, Z)

    extend_y(dims, pad, design[...], py, halo(y_even), None if y_odd is None else halo(y_odd))

    def store(x, value):
        filtered[x : x + value.shape[0]] = value

    filter_y(dims, pad, store)
    row = lax.broadcasted_iota(jnp.int32, (Y, Z), 0)
    lane = lax.broadcasted_iota(jnp.int32, (Y, Z), 1)

    def fill(out, face, up):
        names = (MINUS if up else PLUS)[2]
        slanted = [(j, q) for j, q in enumerate(names) if velocity[q][1] != 0]
        for i, (j, q) in enumerate(slanted):
            edges[i] = pltpu.roll(rows_of(dims, py, y_even, y_odd, q), shift_of(Z, up, j), 1)
        first, last = slot_of(Z, up, 0), slot_of(Z, up, 4)

        def layer(x, _):
            value = jnp.where((lane >= first) & (lane <= last), face[x], filtered[x])
            for i, (j, q) in enumerate(slanted):
                at = (row == (Y - 1 if velocity[q][1] > 0 else 0)) & (lane == slot_of(Z, up, j))
                value = jnp.where(at, edges[i, pl.ds(x, 1), :], value)
            out[x] = value
            return 0

        lax.fori_loop(0, X, layer, 0, unroll=4)

    for n, (out, face) in enumerate(zip(outs, faces)):
        pl.when(pz == n)(functools.partial(fill, out, face, True))
        pl.when(pz != n)(functools.partial(fill, out, face, False))


def rows_of(dims, py, even, odd, q):
    X, Y, Z = dims
    above = velocity[q][1] > 0
    at = X * R + X * (PLUS if above else MINUS)[1].index(q)
    return sides(py, even[at : at + X, :], None if odd is None else odd[at : at + X, :])[int(above)]


def signed(terms):
    total = None
    for sign, value in terms:
        value = value if sign > 0 else -value
        total = value if total is None else total + value
    return total


def moment_of(values):
    return [
        signed([(velocity[q][a], v) for q, v in values.items() if velocity[q][a] != 0]) for a in range(3)
    ]


def halo_z(weights, pz, even, odd):
    value = dot(even, jnp.where(pz == 0, weights[2], weights[1]))
    if odd is not None:
        value = value + dot(odd, jnp.where(pz == 0, weights[1], weights[2]))
    return value


def flat(dims, ref):
    X, Y, Z = dims
    return None if ref is None else ref[...].reshape(X * Y, Z)


def own_z(dims, weights, field, out):
    out[...] = dot(flat(dims, field), weights[0])


def factor_y(dims, many_y, weights, filtered_y, flow_ref, factor, *rest):
    X, Y, Z = dims
    rest = iter(rest)
    y_even, y_odd = refs_of(rest, many_y)
    smooth, out = rest
    smooth[...] = dot(flat(dims, filtered_y), weights[0])
    out[...] = factor[...]
    py = parity_of("gy")
    row = lax.broadcasted_iota(jnp.int32, (X, Z), 0)
    lane = lax.broadcasted_iota(jnp.int32, (X, Z), 1)
    for edge, names in ((0, MINUS[1]), (Y - 1, PLUS[1])):
        values = {}
        for q in names:
            value = rows_of(dims, py, y_even, y_odd, q)
            cx, _, cz = velocity[q]
            if cx != 0:
                value = jnp.where(row == (X - 1 if cx > 0 else 0), 0.0, pltpu.roll(value, (-cx) % X, 0))
            if cz != 0:
                value = jnp.where(lane == (Z - 1 if cz > 0 else 0), 0.0, pltpu.roll(value, (-cz) % Z, 1))
            values[q] = value
        moment = moment_of(values)
        total = factor[:, edge, :]
        for a in range(3):
            total = total - flow_ref[a, :, edge, :] * moment[a]
        out[:, edge, :] = total


def pack_x(dims, many_x, many_y, many_z, adj, weights, smooth, factor_in, flow_ref, *rest):
    X, Y, Z = dims
    rest = iter(rest)
    y_even, y_odd = refs_of(rest, many_y)
    z_even, z_odd = refs_of(rest, many_z)
    outs = [next(rest) for _ in range(1 + many_x)]
    (factor,) = rest
    px, py, pz = parity_of("gx"), parity_of("gy"), parity_of("gz")
    value = smooth[...] + halo_z(weights, pz, flat(dims, z_even), flat(dims, z_odd))
    for out in outs:
        out[: X * Y, :] = value
    lane = lax.broadcasted_iota(jnp.int32, (Y, Z), 1)
    factor[...] = factor_in[...]

    def correct(ref, above):
        names = (PLUS if above else MINUS)[2]
        edge = Z - 1 if above else 0
        zero = jnp.zeros((Y, Z), jnp.float32)

        def layer(x, _):
            values = {}
            for j, q in enumerate(names):
                cx = velocity[q][0]
                face = ref[jnp.clip(x + cx, 0, X - 1)] if cx else ref[x]
                shift = (edge - slot_of(Z, not above, j)) % Z
                face = pltpu.roll(face, shift, 1) if shift else face
                if cx != 0:
                    face = jnp.where(x == (X - 1 if cx > 0 else 0), zero, face)
                values[q] = face
            moment = moment_of(values)
            change = flow_ref[0, x] * moment[0] + flow_ref[1, x] * moment[1] + flow_ref[2, x] * moment[2]
            factor[x] = factor[x] - jnp.where(lane == edge, change, zero)
            return 0

        lax.fori_loop(0, X, layer, 0, unroll=4)

    for n, ref in enumerate([z_even, z_odd][: 1 + many_z]):
        pl.when(pz == n)(functools.partial(correct, ref, True))
        pl.when(pz != n)(functools.partial(correct, ref, False))

    pull = Pull(adj, dims, py, y_even, y_odd, pz, z_even, z_odd)

    def fill(out, up):
        names = (MINUS if up else PLUS)[0]
        edge = X - 1 if up else 0
        at = X * Y
        first = X - R if up else 0
        out[at : at + R * Y, :] = factor[first : first + R].reshape(R * Y, Z)
        at += R * Y
        faces = pull.faces(edge)
        for q in names:
            out[at : at + Y, :] = pull.both(q, edge, faces)
            at += Y
        for a in range(3):
            out[at : at + Y, :] = flow_ref[a, edge]
            at += Y

    for n, out in enumerate(outs):
        pl.when(px == n)(functools.partial(fill, out, True))
        pl.when(px != n)(functools.partial(fill, out, False))


def project(filtered):
    base = math.tanh(sharpness * threshold)
    denominator = base + math.tanh(sharpness * (1.0 - threshold))
    inner = jnp.tanh(sharpness * (filtered - threshold))
    physical = (base + inner) * (1.0 / denominator)
    steep = (sharpness / denominator) * (1.0 - inner * inner)
    inverse = 1.0 / (ramp_shape + physical)
    return physical, steep, inverse


def source(dims, many_x, many_y, factor, flow_ref, *rest):
    X, Y, Z = dims
    rest = iter(rest)
    own_even, own_odd = refs_of(rest, many_x)
    x_even, x_odd = refs_of(rest, many_x)
    result, damp = next(rest), next(rest)
    outs = [next(rest) for _ in range(1 + many_y)]
    layers, ext = rest
    px, py = parity_of("gx"), parity_of("gy")
    size = X * Y
    g_at, u_at, v_at = size, size + R * Y, size + R * Y + 5 * Y

    def got(at, count):
        return sides(px, x_even[at : at + count, :], None if x_odd is None else x_odd[at : at + count, :])

    def own(at, count):
        return sides(px, own_even[at : at + count, :], None if own_odd is None else own_odd[at : at + count, :])

    below, above = got(0, size)
    layers[:X] = below.reshape(X, Y, Z)
    layers[X : 2 * X] = own_even[:size, :].reshape(X, Y, Z)
    layers[2 * X :] = above.reshape(X, Y, Z)

    below, above = got(g_at, R * Y)
    ext[:R] = below.reshape(R, Y, Z)
    ext[R : R + X] = factor[...]
    ext[R + X :] = above.reshape(R, Y, Z)

    def face_moment(block, names):
        return moment_of({q: block[j * Y : (j + 1) * Y] for j, q in enumerate(names)})

    def less(at, vel, moment):
        ext[at] = ext[at] - (vel[0] * moment[0] + vel[1] * moment[1] + vel[2] * moment[2])

    got_low, got_high = got(u_at, 5 * Y)
    own_low, own_high = own(u_at, 5 * Y)
    vel_low, vel_high = got(v_at, 3 * Y)
    less(R - 1, [vel_low[a * Y : (a + 1) * Y] for a in range(3)], face_moment(own_low, PLUS[0]))
    less(R, [flow_ref[a, 0] for a in range(3)], face_moment(got_low, MINUS[0]))
    less(R + X - 1, [flow_ref[a, X - 1] for a in range(3)], face_moment(got_high, PLUS[0]))
    less(R + X, [vel_high[a * Y : (a + 1) * Y] for a in range(3)], face_moment(own_high, MINUS[0]))

    slope = -damping_max * ramp_shape * (1.0 + ramp_shape)
    base = X - 2 * R

    def layer(e, _):
        smooth = filter_rows(lambda k: layers[base + e + k])
        physical, steep, inverse = project(smooth)
        ext[e] = (slope * steep) * (inverse * inverse) * ext[e]

        @pl.when((e >= R) & (e < R + X))
        def _():
            damp[e - R] = (2.0 * damping_max * ramp_shape) * (1.0 - physical) * inverse

        return 0

    lax.fori_loop(0, X + 2 * R, layer, 0, unroll=4)

    def last(x, _):
        result[x] = filter_rows(lambda k: ext[x + k])
        return 0

    lax.fori_loop(0, X, last, 0, unroll=4)
    for n, out in enumerate(outs):

        @pl.when(py == n)
        def _(out=out):
            out[...] = result[:, Y - R :, :]

        @pl.when(py != n)
        def _(out=out):
            out[...] = result[:, :R, :]


def smooth_y(dims, many_y, ahead, own, *rest):
    rest = iter(rest)
    y_even, y_odd = refs_of(rest, many_y)
    result, pad = rest
    extend_y(dims, pad, own[...], parity_of("gy"), y_even[...], None if y_odd is None else y_odd[...])

    def store(x, value):
        result[x : x + value.shape[0]] = value

    filter_y(dims, pad, store)


def smooth_z(dims, many_z, weights, own, *rest):
    rest = iter(rest)
    z_even, z_odd = refs_of(rest, many_z)
    (result,) = rest
    value = own[...] + halo_z(weights, parity_of("gz"), flat(dims, z_even), flat(dims, z_odd))
    result[...] = value.reshape(dims)


def collide(dims, many_x, many_y, many_z, step, adj, flow_ref, damp, mask, *rest):
    X, Y, Z = dims
    rest = iter(rest)
    y_even, y_odd = refs_of(rest, many_y)
    z_even, z_odd = refs_of(rest, many_z)
    x_even, x_odd = refs_of(rest, many_x)
    (out,) = rest
    px, py, pz = parity_of("gx"), parity_of("gy"), parity_of("gz")
    pull = Pull(adj, dims, py, y_even, y_odd, pz, z_even, z_odd)
    begin = pl.program_id(0) * step
    u_at = X * Y + R * Y

    def layer(i, _):
        x = begin + i
        around = {c: pull.faces(jnp.clip(x + c, 0, X - 1)) for c in (-1, 0, 1)}
        pulled = []
        for q in range(Q):
            cx = velocity[q][0]
            value = pull.both(q, jnp.clip(x + cx, 0, X - 1), around[cx])
            if cx != 0:
                at = u_at + Y * (PLUS if cx > 0 else MINUS)[0].index(q)
                below, above = sides(
                    px, x_even[at : at + Y, :], None if x_odd is None else x_odd[at : at + Y, :]
                )
                value = jnp.where(x == (X - 1 if cx > 0 else 0), above if cx > 0 else below, value)
            pulled.append(value)
        vel = [flow_ref[a, x] for a in range(3)]
        inverse = flow_ref[3, x]
        speed_sq = vel[0] * vel[0] + vel[1] * vel[1] + vel[2] * vel[2]
        plus = {q: pulled[q] + pulled[q + 1] for q in range(1, Q, 2)}
        minus = {q: pulled[q] - pulled[q + 1] for q in range(1, Q, 2)}
        axes = (1, 3, 5)
        straight = plus[1] + plus[3] + plus[5]
        slanted = plus[7] + plus[9] + plus[11] + plus[13] + plus[15] + plus[17]
        zeroth = (1.0 / 3.0) * pulled[0] + (1.0 / 18.0) * straight + (1.0 / 36.0) * slanted
        first, diagonal = [], []
        for a in range(3):
            terms = [(velocity[q][a], minus[q]) for q in range(7, Q, 2) if velocity[q][a] != 0]
            first.append((1.0 / 18.0) * minus[axes[a]] + (1.0 / 36.0) * signed(terms))
            both = [(1, plus[q]) for q in range(7, Q, 2) if velocity[q][a] != 0]
            diagonal.append((1.0 / 18.0) * plus[axes[a]] + (1.0 / 36.0) * signed(both))
        xy = (1.0 / 36.0) * (plus[7] - plus[9])
        xz = (1.0 / 36.0) * (plus[11] - plus[13])
        yz = (1.0 / 36.0) * (plus[15] - plus[17])
        turned = [
            diagonal[0] * vel[0] + xy * vel[1] + xz * vel[2],
            xy * vel[0] + diagonal[1] * vel[1] + yz * vel[2],
            xz * vel[0] + yz * vel[1] + diagonal[2] * vel[2],
        ]
        quadric = vel[0] * turned[0] + vel[1] * turned[1] + vel[2] * turned[2]
        eq_scalar = zeroth * (1.0 + 1.5 * speed_sq) - 4.5 * quadric
        eq_vector = [3.0 * first[a] + 9.0 * turned[a] - 3.0 * zeroth * vel[a] for a in range(3)]
        label = mask[x]
        drag = damp[x] * inverse
        fluid, solid, inlet = label == 0, label == 1, label == 2
        zero = jnp.zeros_like(drag)
        keep = jnp.where(fluid, 1.0 - relax_rate, zero)
        bounce = jnp.where(solid, 1.0, zero)
        level = jnp.where(fluid, relax_rate * eq_scalar - drag * speed_sq, jnp.where(solid, zero, eq_scalar))
        tilt = [
            jnp.where(fluid, relax_rate * eq_vector[a] + drag * vel[a], jnp.where(inlet, eq_vector[a], zero))
            for a in range(3)
        ]
        out[0, i] = (keep + bounce) * pulled[0] + level
        for q in range(1, Q, 2):
            lean = signed([(velocity[q][a], tilt[a]) for a in range(3) if velocity[q][a] != 0])
            out[q, i] = keep * pulled[q] + bounce * pulled[q + 1] + (level + lean)
            out[q + 1, i] = keep * pulled[q + 1] + bounce * pulled[q] + (level - lean)
        return 0

    lax.fori_loop(0, step, layer, 0)


def local(counts, forward, adjoint, design, mask):
    many_x, many_y, many_z = (int(n > 2) for n in counts)
    nx, ny, nz = counts
    dims = design.shape
    X, Y, Z = dims
    weights = jnp.asarray(band(Z))
    hbm = pl.BlockSpec(memory_space=pltpu.HBM)
    cells = X * Y * Z
    some = lambda pair: [v for v in pair if v is not None]
    pair = lambda items: (items[0], items[1] if len(items) > 1 else None)
    dma = pltpu.SemaphoreType.DMA

    y_rows = X * R + 5 * X
    *to_y, design = call(
        functools.partial(pack_y, dims, many_y),
        [f32(y_rows, Z)] * (1 + many_y) + [f32(X, Y, Z)],
        (in_hbm(adjoint), in_hbm(design)),
        [hbm, hbm],
        [pltpu.VMEM((1 + many_y, 5, X, R, Z), jnp.float32), dma((1 + many_y, 5)), dma],
        limit=4,
        name="pack_y",
    )
    got_y = some(exchange("gy", ny, *pair(to_y)))

    flow_values, factor, *faces = call(
        functools.partial(prepare, dims, many_z),
        [f32(4, X, Y, Z)] + [f32(X, Y, Z)] * (2 + many_z),
        (to_y[0], in_hbm(forward), adjoint),
        vmem(1) + [hbm] + vmem(1),
        [pltpu.VMEM((3, X + 2, Y, Z), jnp.float32)] * 2 + [pltpu.VMEM((Q, X, Y, Z), jnp.float32), dma((4,))],
        limit=16,
        flops=200 * cells,
        moved=44 * 4 * cells,
        name="prepare",
    )

    filtered_y, *to_z = call(
        functools.partial(design_y, dims, many_y, many_z),
        [f32(X, Y, Z)] * (2 + many_z),
        (design, *faces, *got_y),
        None,
        [pltpu.VMEM((X, Y + 2 * R, Z), jnp.float32), pltpu.VMEM((2, X, Z), jnp.float32)],
        limit=8,
        name="design_y",
    )
    got_z = some(exchange("gz", nz, *pair(to_z)))

    smooth, factor = call(
        functools.partial(factor_y, dims, many_y),
        [f32(X * Y, Z), f32(X, Y, Z)],
        (weights, filtered_y, flow_values, factor, *got_y),
        limit=8,
        flops=200 * cells,
        name="factor_y",
    )

    x_rows = X * Y + R * Y + 8 * Y
    *to_x, factor = call(
        functools.partial(pack_x, dims, many_x, many_y, many_z),
        [f32(x_rows, Z)] * (1 + many_x) + [f32(X, Y, Z)],
        (adjoint, weights, smooth, factor, flow_values, *got_y, *got_z),
        limit=16,
        name="pack_x",
    )
    got_x = some(exchange("gx", nx, *pair(to_x)))

    result, damp, *to_y = call(
        functools.partial(source, dims, many_x, many_y),
        [f32(X, Y, Z), f32(X, Y, Z)] + [f32(X, R, Z)] * (1 + many_y),
        (factor, flow_values, *to_x, *got_x),
        None,
        [pltpu.VMEM((3 * X, Y, Z), jnp.float32), pltpu.VMEM((X + 2 * R, Y, Z), jnp.float32)],
        limit=8,
        name="source",
    )
    got_y2 = some(exchange("gy", ny, *pair(to_y)))

    step = 4
    whole = pl.BlockSpec(memory_space=pltpu.VMEM)
    adjoint_next = call(
        functools.partial(collide, dims, many_x, many_y, many_z, step),
        f32(Q, X, Y, Z),
        (adjoint, flow_values, damp, mask, *got_y, *got_z, *got_x),
        [whole] * (4 + len(got_y) + len(got_z) + len(got_x)),
        out_specs=pl.BlockSpec((Q, step, Y, Z), lambda i: (0, i, 0, 0)),
        grid=(X // step,),
        limit=16,
        flops=300 * cells,
        moved=44 * 4 * cells,
        name="collide",
    )

    (filtered_xy,) = call(
        functools.partial(smooth_y, dims, many_y),
        [f32(X, Y, Z)],
        (in_hbm(adjoint_next), result, *got_y2),
        [hbm] + vmem(1 + len(got_y2)),
        [pltpu.VMEM((X, Y + 2 * R, Z), jnp.float32)],
        limit=4,
        name="smooth_y",
    )
    got_z2 = some(exchange("gz", nz, filtered_xy, filtered_xy if many_z else None))
    (own,) = call(
        functools.partial(own_z, dims),
        [f32(X * Y, Z)],
        (weights, filtered_xy),
        limit=4,
        flops=200 * cells,
        name="own_z",
    )
    (sensitivity,) = call(
        functools.partial(smooth_z, dims, many_z),
        [f32(X, Y, Z)],
        (weights, own, *got_z2),
        limit=4,
        name="smooth_z",
    )
    return adjoint_next, sensitivity


def solution(mesh):
    counts = tuple(mesh.shape[a] for a in ("gx", "gy", "gz"))
    populations, field = P(None, "gx", "gy", "gz"), P("gx", "gy", "gz")
    return jax.shard_map(
        functools.partial(local, counts),
        mesh=mesh,
        in_specs=(populations, populations, field, field),
        out_specs=(populations, field),
        check_vma=False,
    )
```

```python
import functools
import math

import jax
import jax.numpy as jnp
import numpy as np
from jax import lax
from jax.experimental import pallas as pl
from jax.experimental.pallas import tpu as pltpu
from jax.sharding import PartitionSpec as P

Q = 19
R = 8

velocity = [
    (0, 0, 0),
    (1, 0, 0),
    (-1, 0, 0),
    (0, 1, 0),
    (0, -1, 0),
    (0, 0, 1),
    (0, 0, -1),
    (1, 1, 0),
    (-1, -1, 0),
    (1, -1, 0),
    (-1, 1, 0),
    (1, 0, 1),
    (-1, 0, -1),
    (1, 0, -1),
    (-1, 0, 1),
    (0, 1, 1),
    (0, -1, -1),
    (0, 1, -1),
    (0, -1, 1),
]
relax_rate = 1.25
sharpness = 64.0
threshold = 0.5
damping_max = 10.0
ramp_shape = 0.1


def fields_of(axis, sign):
    plus = [q for q in range(Q) if velocity[q][axis] == 1]
    return plus if sign > 0 else [q + 1 if q % 2 else q - 1 for q in plus]


PLUS = [fields_of(a, 1) for a in range(3)]
MINUS = [fields_of(a, -1) for a in range(3)]


def tap_weights():
    spread_width = R / 2.0
    unscaled = [math.exp(-((k - R) ** 2) / (2.0 * spread_width * spread_width)) for k in range(2 * R + 1)]
    summed = sum(unscaled)
    return [v / summed for v in unscaled]


TAPS = tap_weights()


def band(length):
    out = np.zeros((3, length, length), np.float32)
    for i in range(length):
        for k in range(-R, R + 1):
            j = i + k
            if j < 0:
                out[1, j + length, i] = TAPS[k + R]
            elif j >= length:
                out[2, j - length, i] = TAPS[k + R]
            else:
                out[0, j, i] = TAPS[k + R]
    return out


def packed_band(dims):
    X, Y, Z = dims
    out = np.zeros((2, 2, Z, Z), np.float32)
    for above_x in range(2):
        for above_z in range(2):
            for e in range(X):
                for i in range(X):
                    for z in range(R):
                        for j in range(R):
                            kx = i - e + 2 * R * above_x
                            kz = j - z + 2 * R * above_z
                            if 0 <= kx <= 2 * R and 0 <= kz <= 2 * R:
                                out[above_x, above_z, i * R + j, e * R + z] = TAPS[kx] * TAPS[kz]
    return out.reshape(4, Z, Z)


def sides(parity, even, odd):
    zero = jnp.zeros_like(even)
    if odd is None:
        return jnp.where(parity == 0, zero, even), jnp.where(parity == 0, even, zero)
    return jnp.where(parity == 0, odd, even), jnp.where(parity == 0, even, odd)


def parity_of(axis):
    return lax.rem(lax.axis_index(axis), 2)


def swap(array, axis, count, first):
    pairs = [(i, i + 1) for i in range(first, count - 1, 2)]
    return lax.ppermute(array, axis, pairs + [(b, a) for a, b in pairs])


def relay(array, axis, count):
    pairs = [(i + 2, i) for i in range(1, count - 2, 2)] + [(i - 2, i) for i in range(2, count, 2)]
    return lax.ppermute(array, axis, pairs)


def exchange(axis, count, even, odd):
    return swap(even, axis, count, 0), (None if odd is None else swap(odd, axis, count, 1))


def vmem(count):
    return [pl.BlockSpec(memory_space=pltpu.VMEM)] * count


def in_hbm(array):
    return pltpu.with_memory_space_constraint(array, pltpu.HBM)


def f32(*shape):
    return jax.ShapeDtypeStruct(shape, jnp.float32)


def call(body, outs, args, specs=None, scratch=(), limit=16, flops=1e6, moved=1e6, **rest):
    return pl.pallas_call(
        body,
        out_shape=outs,
        in_specs=specs or vmem(len(args)),
        out_specs=rest.pop("out_specs", tuple(vmem(len(outs)))),
        scratch_shapes=list(scratch),
        compiler_params=pltpu.CompilerParams(vmem_limit_bytes=limit * 2**20),
        cost_estimate=pl.CostEstimate(flops=int(flops), bytes_accessed=int(moved), transcendentals=0),
        **rest,
    )(*args)


def filter_rows(load):
    total = TAPS[R] * load(R)
    for k in range(R):
        total = total + TAPS[k] * (load(k) + load(2 * R - k))
    return total


def dot(a, b):
    return jnp.dot(a, b, preferred_element_type=jnp.float32, precision=lax.Precision.HIGHEST)


def row_of(ref, at):
    return ref[pl.ds(at, 1), :]


class Pull:
    def __init__(self, adj, dims, py, y_even, y_odd, pz=None, z_even=None, z_odd=None):
        self.adj, self.dims = adj, dims
        self.py, self.y_even, self.y_odd = py, y_even, y_odd
        self.pz, self.z_even, self.z_odd = pz, z_even, z_odd
        X, Y, Z = dims
        self.row = lax.broadcasted_iota(jnp.int32, (Y, Z), 0)
        self.lane = lax.broadcasted_iota(jnp.int32, (Y, Z), 1)

    def along_y(self, q, x):
        X, Y, Z = self.dims
        here = self.adj[q, x]
        cy = velocity[q][1]
        if cy == 0:
            return here
        at = X * R + X * (PLUS if cy > 0 else MINUS)[1].index(q) + x
        even = row_of(self.y_even, at)
        odd = None if self.y_odd is None else row_of(self.y_odd, at)
        below, above = sides(self.py, even, odd)
        if cy > 0:
            return jnp.where(self.row == Y - 1, above, pltpu.roll(here, Y - 1, 0))
        return jnp.where(self.row == 0, below, pltpu.roll(here, 1, 0))

    def faces(self, x):
        even = self.z_even[x]
        odd = None if self.z_odd is None else self.z_odd[x]
        return sides(self.pz, even, odd)

    def both(self, q, x, faces):
        X, Y, Z = self.dims
        here = self.along_y(q, x)
        cz = velocity[q][2]
        if cz == 0:
            return here
        below, above = faces
        if cz > 0:
            j = PLUS[2].index(q)
            face = pltpu.roll(above, 4 - j, 1) if j != 4 else above
            return jnp.where(self.lane == Z - 1, face, pltpu.roll(here, Z - 1, 1))
        j = MINUS[2].index(q)
        face = pltpu.roll(below, Z - j, 1) if j else below
        return jnp.where(self.lane == 0, face, pltpu.roll(here, 1, 1))


def refs_of(refs, odd):
    even = next(refs)
    return even, (next(refs) if odd else None)


def pack_y(dims, many, adj, design, *rest):
    X, Y, Z = dims
    outs = rest[: 1 + many]
    kept, tiles, sems, kept_sem = rest[1 + many :]
    py = parity_of("gy")
    keep = pltpu.make_async_copy(design, kept, kept_sem)
    keep.start()

    def copies(n, up):
        names = (MINUS if up else PLUS)[1]
        first = Y - R if up else 0
        return [
            pltpu.make_async_copy(adj.at[q, :, pl.ds(first, R), :], tiles.at[n, j], sems.at[n, j])
            for j, q in enumerate(names)
        ]

    def start(n, out, up):
        for c in copies(n, up):
            c.start()

    def fill(n, out, up):
        first = Y - R if up else 0
        out[: X * R, :] = kept[:, first : first + R, :].reshape(X * R, Z)
        for c in copies(n, up):
            c.wait()
        for j in range(5):
            out[X * R + X * j : X * R + X * (j + 1), :] = tiles[n, j, :, R - 1 if up else 0, :]

    def each(act):
        for n, out in enumerate(outs):
            pl.when(py == n)(functools.partial(act, n, out, True))
            pl.when(py != n)(functools.partial(act, n, out, False))

    each(start)
    keep.wait()
    each(fill)


def prepare(dims, many_z, ahead, forward, adj, *rest):
    X, Y, Z = dims
    rest = iter(rest)
    flow_ref, factor = next(rest), next(rest)
    outs = [next(rest) for _ in range(1 + many_z)]
    rising, falling, members_ref, sems = rest
    pz = parity_of("gz")
    part = X // 4
    copies = [
        pltpu.make_async_copy(
            forward.at[:, pl.ds(i * part, part)], members_ref.at[:, pl.ds(i * part, part)], sems.at[i]
        )
        for i in range(4)
    ]
    for c in copies:
        c.start()
    row = lax.broadcasted_iota(jnp.int32, (Y, Z), 0)
    lane = lax.broadcasted_iota(jnp.int32, (Y, Z), 1)
    zero = jnp.zeros((Y, Z), jnp.float32)

    def along_y(q, x):
        here, cy = adj[q, x], velocity[q][1]
        if cy == 0:
            return here
        return jnp.where(row == (Y - 1 if cy > 0 else 0), zero, pltpu.roll(here, (-cy) % Y, 0))

    def both(q, x):
        here, cz = along_y(q, x), velocity[q][2]
        if cz == 0:
            return here
        return jnp.where(lane == (Z - 1 if cz > 0 else 0), zero, pltpu.roll(here, (-cz) % Z, 1))

    def layer(x, _):
        members = [members_ref[q, x] for q in range(Q)]
        inverse = 1.0 / sum(members[1:], members[0])
        vel = [
            signed([(velocity[q][a], members[q] - members[q + 1]) for q in range(1, Q, 2) if velocity[q][a] != 0])
            * inverse
            for a in range(3)
        ]
        for a in range(3):
            flow_ref[a, x] = vel[a]
        flow_ref[3, x] = inverse
        groups = {}
        for q in range(1, Q):
            groups.setdefault(velocity[q][0], {})[q] = both(q, x)
        level, up, down = moment_of(groups[0]), moment_of(groups[1]), moment_of(groups[-1])
        for a in range(3):
            rising[a, x] = up[a]
            falling[a, x + 2] = down[a]
        factor[x] = vel[0] * vel[0] + vel[1] * vel[1] + vel[2] * vel[2] - vel[1] * level[1] - vel[2] * level[2]
        return 0

    for a in range(3):
        rising[a, X] = zero
        falling[a, 1] = zero
    for i, c in enumerate(copies):
        c.wait()
        lax.fori_loop(i * part, (i + 1) * part, layer, 0)

    def finish(x, _):
        total = factor[x]
        for a in range(3):
            total = total - flow_ref[a, x] * (rising[a, x + 1] + falling[a, x + 1])
        factor[x] = total
        return 0

    lax.fori_loop(0, X, finish, 0, unroll=4)

    def fill(out, up):
        names = (MINUS if up else PLUS)[2]

        def face(x, _):
            value = zero
            for j, q in enumerate(names):
                slot = slot_of(Z, up, j)
                value = jnp.where(lane == slot, pltpu.roll(along_y(q, x), shift_of(Z, up, j), 1), value)
            out[x] = value
            return 0

        lax.fori_loop(0, X, face, 0, unroll=2)

    for n, out in enumerate(outs):
        pl.when(pz == n)(functools.partial(fill, out, True))
        pl.when(pz != n)(functools.partial(fill, out, False))


def slot_of(Z, up, j):
    return j if up else Z - 5 + j


def shift_of(Z, up, j):
    return (slot_of(Z, up, j) - (Z - 1 if up else 0)) % Z


def extend_y(dims, pad, own, py, even, odd):
    X, Y, Z = dims
    below, above = sides(py, even, odd)
    pad[:, :R, :] = below
    pad[:, R : R + Y, :] = own
    pad[:, R + Y :, :] = above


def filter_y(dims, pad, store, step=2):
    X, Y, Z = dims
    for x in range(0, X, step):
        store(x, filter_rows(lambda k: pad[x : x + step, k : k + Y, :]))


def design_y(dims, many_y, many_z, design, *rest):
    X, Y, Z = dims
    rest = iter(rest)
    faces = [next(rest) for _ in range(1 + many_z)]
    y_even, y_odd = refs_of(rest, many_y)
    filtered = next(rest)
    outs = [next(rest) for _ in range(1 + many_z)]
    pad, edges = rest
    pz = parity_of("gz")
    py = parity_of("gy")

    def halo(ref):
        return ref[: X * R, :].reshape(X, R, Z)

    extend_y(dims, pad, design[...], py, halo(y_even), None if y_odd is None else halo(y_odd))

    def store(x, value):
        filtered[x : x + value.shape[0]] = value

    filter_y(dims, pad, store)
    row = lax.broadcasted_iota(jnp.int32, (Y, Z), 0)
    lane = lax.broadcasted_iota(jnp.int32, (Y, Z), 1)

    def fill(out, face, up):
        names = (MINUS if up else PLUS)[2]
        slanted = [(j, q) for j, q in enumerate(names) if velocity[q][1] != 0]
        for i, (j, q) in enumerate(slanted):
            edges[i] = pltpu.roll(rows_of(dims, py, y_even, y_odd, q), shift_of(Z, up, j), 1)
        first, last = slot_of(Z, up, 0), slot_of(Z, up, 4)

        def layer(x, _):
            value = jnp.where((lane >= first) & (lane <= last), face[x], filtered[x])
            for i, (j, q) in enumerate(slanted):
                at = (row == (Y - 1 if velocity[q][1] > 0 else 0)) & (lane == slot_of(Z, up, j))
                value = jnp.where(at, edges[i, pl.ds(x, 1), :], value)
            out[x] = value
            return 0

        lax.fori_loop(0, X, layer, 0, unroll=True)

    for n, (out, face) in enumerate(zip(outs, faces)):
        pl.when(pz == n)(functools.partial(fill, out, face, True))
        pl.when(pz != n)(functools.partial(fill, out, face, False))


def rows_of(dims, py, even, odd, q):
    X, Y, Z = dims
    above = velocity[q][1] > 0
    at = X * R + X * (PLUS if above else MINUS)[1].index(q)
    return sides(py, even[at : at + X, :], None if odd is None else odd[at : at + X, :])[int(above)]


def signed(terms):
    total = None
    for sign, value in terms:
        value = value if sign > 0 else -value
        total = value if total is None else total + value
    return total


def moment_of(values):
    return [
        signed([(velocity[q][a], v) for q, v in values.items() if velocity[q][a] != 0]) for a in range(3)
    ]


def halo_z(weights, pz, even, odd):
    value = dot(even, jnp.where(pz == 0, weights[2], weights[1]))
    if odd is not None:
        value = value + dot(odd, jnp.where(pz == 0, weights[1], weights[2]))
    return value


def flat(dims, ref):
    X, Y, Z = dims
    return None if ref is None else ref[...].reshape(X * Y, Z)


def own_z(dims, weights, field, out):
    out[...] = dot(flat(dims, field), weights[0])


def factor_y(dims, many_y, weights, filtered_y, flow_ref, factor, *rest):
    X, Y, Z = dims
    rest = iter(rest)
    y_even, y_odd = refs_of(rest, many_y)
    smooth, out, again = rest
    again[...] = filtered_y[...]
    smooth[...] = dot(flat(dims, filtered_y), weights[0])
    out[...] = factor[...]
    py = parity_of("gy")
    row = lax.broadcasted_iota(jnp.int32, (X, Z), 0)
    lane = lax.broadcasted_iota(jnp.int32, (X, Z), 1)
    for edge, names in ((0, MINUS[1]), (Y - 1, PLUS[1])):
        values = {}
        for q in names:
            value = rows_of(dims, py, y_even, y_odd, q)
            cx, _, cz = velocity[q]
            if cx != 0:
                value = jnp.where(row == (X - 1 if cx > 0 else 0), 0.0, pltpu.roll(value, (-cx) % X, 0))
            if cz != 0:
                value = jnp.where(lane == (Z - 1 if cz > 0 else 0), 0.0, pltpu.roll(value, (-cz) % Z, 1))
            values[q] = value
        moment = moment_of(values)
        total = factor[:, edge, :]
        for a in range(3):
            total = total - flow_ref[a, :, edge, :] * moment[a]
        out[:, edge, :] = total


def faces_x(dims, out, up, factor, flow_ref, pull):
    X, Y, Z = dims
    names = (MINUS if up else PLUS)[0]
    edge = X - 1 if up else 0
    first = X - R if up else 0
    at = R * Y
    out[:at, :] = factor[first : first + R].reshape(R * Y, Z)
    faces = pull.faces(edge)
    for q in names:
        out[at : at + Y, :] = pull.both(q, edge, faces)
        at += Y
    for a in range(3):
        out[at : at + Y, :] = flow_ref[a, edge]
        at += Y


def pack_halo(dims, pz, refs, out):
    X, Y, Z = dims
    lane = lax.broadcasted_iota(jnp.int32, (Y, Z), 1)
    for n, ref in enumerate(refs):
        value = jnp.zeros((Y, Z), jnp.float32)
        for x in range(X):
            there = (lane >= R * x) & (lane < R * (x + 1))
            value = jnp.where(there, pltpu.roll(ref[x], lanes_x(dims, pz, n, x), 1), value)
        out[(R + 8 + n) * Y : (R + 9 + n) * Y, :] = value


def pack_odd(dims, many_y, many_z, adj, ahead, factor, flow_ref, *rest):
    X, Y, Z = dims
    rest = iter(rest)
    y_even, y_odd = refs_of(rest, many_y)
    z_even, z_odd = refs_of(rest, many_z)
    (out,) = rest
    px = parity_of("gx")
    pz = parity_of("gz")
    out[(R + 8) * Y :, :] = ahead[(R + 8) * Y :, :]
    pull = Pull(adj, dims, parity_of("gy"), y_even, y_odd, pz, z_even, z_odd)
    pl.when(px == 1)(lambda: faces_x(dims, out, True, factor, flow_ref, pull))
    pl.when(px != 1)(lambda: faces_x(dims, out, False, factor, flow_ref, pull))


def pack_x(dims, many_y, many_z, adj, weights, smooth, factor_in, flow_ref, *rest):
    X, Y, Z = dims
    rest = iter(rest)
    y_even, y_odd = refs_of(rest, many_y)
    z_even, z_odd = refs_of(rest, many_z)
    out, whole, factor = rest
    px, py, pz = parity_of("gx"), parity_of("gy"), parity_of("gz")
    value = smooth[...] + halo_z(weights, pz, flat(dims, z_even), flat(dims, z_odd))
    whole[...] = value
    pack_halo(dims, pz, [z_even, z_odd][: 1 + many_z], out)
    lane = lax.broadcasted_iota(jnp.int32, (Y, Z), 1)
    factor[...] = factor_in[...]

    def correct(ref, above):
        names = (PLUS if above else MINUS)[2]
        edge = Z - 1 if above else 0
        zero = jnp.zeros((Y, Z), jnp.float32)

        def layer(x, _):
            values = {}
            for j, q in enumerate(names):
                cx = velocity[q][0]
                face = ref[jnp.clip(x + cx, 0, X - 1)] if cx else ref[x]
                shift = (edge - slot_of(Z, not above, j)) % Z
                face = pltpu.roll(face, shift, 1) if shift else face
                if cx != 0:
                    face = jnp.where(x == (X - 1 if cx > 0 else 0), zero, face)
                values[q] = face
            moment = moment_of(values)
            change = flow_ref[0, x] * moment[0] + flow_ref[1, x] * moment[1] + flow_ref[2, x] * moment[2]
            factor[x] = factor[x] - jnp.where(lane == edge, change, zero)
            return 0

        lax.fori_loop(0, X, layer, 0, unroll=True)

    for n, ref in enumerate([z_even, z_odd][: 1 + many_z]):
        pl.when(pz == n)(functools.partial(correct, ref, True))
        pl.when(pz != n)(functools.partial(correct, ref, False))

    pull = Pull(adj, dims, py, y_even, y_odd, pz, z_even, z_odd)

    pl.when(px == 0)(lambda: faces_x(dims, out, True, factor, flow_ref, pull))
    pl.when(px != 0)(lambda: faces_x(dims, out, False, factor, flow_ref, pull))


def project(filtered):
    base = math.tanh(sharpness * threshold)
    denominator = base + math.tanh(sharpness * (1.0 - threshold))
    inner = jnp.tanh(sharpness * (filtered - threshold))
    physical = (base + inner) * (1.0 / denominator)
    steep = (sharpness / denominator) * (1.0 - inner * inner)
    inverse = 1.0 / (ramp_shape + physical)
    return physical, steep, inverse


def taps_of(X, above, e):
    shift = 2 * R + (X if above else -X) - e
    return [(TAPS[i + shift], i) for i in range(X) if 0 <= i + shift <= 2 * R]


def add_side(dims, base, layers, at, out, above):
    X, Y, Z = dims
    for e in range(X + 2 * R):
        total = base[e]
        for tap, i in taps_of(X, above, e):
            total = total + tap * layers[at + i * Y : at + (i + 1) * Y, :]
        out[e] = total


def lanes_x(dims, pz, n, x):
    Z = dims[2]
    return jnp.where(pz == n, (R * x) % Z, (R * x + R) % Z)


def source(dims, many_x, many_y, many_z, weights, partial, factor, flow_ref, *rest):
    X, Y, Z = dims
    rest = iter(rest)
    own_even, own_odd = refs_of(rest, many_x)
    x_even, x_odd = refs_of(rest, many_x)
    result, damp = next(rest), next(rest)
    outs = [next(rest) for _ in range(1 + many_y)]
    smooth, ext = rest
    px, py, pz = parity_of("gx"), parity_of("gy"), parity_of("gz")
    u_at, v_at, d_at = R * Y, R * Y + 5 * Y, R * Y + 8 * Y

    def got(at, count):
        return sides(px, x_even[at : at + count, :], None if x_odd is None else x_odd[at : at + count, :])

    def own(at, count):
        return sides(px, own_even[at : at + count, :], None if own_odd is None else own_odd[at : at + count, :])

    smooth[...] = partial[...]
    lane = lax.broadcasted_iota(jnp.int32, (Y, Z), 1)
    for odd, ref in enumerate([x_even, x_odd][: 1 + many_x]):
        above_x = jnp.where(px == odd, 1, 0)
        for n in range(1 + many_z):
            above_z = jnp.where(pz == n, 1, 0)
            value = dot(ref[d_at + n * Y : d_at + (n + 1) * Y, :], weights[2 * above_x + above_z])
            first = (Z - R) * above_z
            there = (lane >= first) & (lane < first + R)
            for e in range(X):
                at = e + X * above_x
                moved = pltpu.roll(value, lax.rem(first + Z - R * e, Z), 1)
                smooth[at] = smooth[at] + jnp.where(there, moved, 0.0)
    low, high = got(0, R * Y)
    ext[:R] = low.reshape(R, Y, Z)
    ext[R : R + X] = factor[...]
    ext[R + X :] = high.reshape(R, Y, Z)

    def face_moment(block, names):
        return moment_of({q: block[j * Y : (j + 1) * Y] for j, q in enumerate(names)})

    def less(at, vel, moment):
        ext[at] = ext[at] - (vel[0] * moment[0] + vel[1] * moment[1] + vel[2] * moment[2])

    got_low, got_high = got(u_at, 5 * Y)
    own_low, own_high = own(u_at, 5 * Y)
    vel_low, vel_high = got(v_at, 3 * Y)
    less(R - 1, [vel_low[a * Y : (a + 1) * Y] for a in range(3)], face_moment(own_low, PLUS[0]))
    less(R, [flow_ref[a, 0] for a in range(3)], face_moment(got_low, MINUS[0]))
    less(R + X - 1, [flow_ref[a, X - 1] for a in range(3)], face_moment(got_high, PLUS[0]))
    less(R + X, [vel_high[a * Y : (a + 1) * Y] for a in range(3)], face_moment(own_high, MINUS[0]))

    slope = -damping_max * ramp_shape * (1.0 + ramp_shape)
    for e in range(X + 2 * R):
        physical, steep, inverse = project(smooth[e])
        ext[e] = (slope * steep) * (inverse * inverse) * ext[e]
        if R <= e < R + X:
            damp[e - R] = (2.0 * damping_max * ramp_shape) * (1.0 - physical) * inverse

    for x in range(X):
        result[x] = filter_rows(lambda k: ext[x + k])
    for n, out in enumerate(outs):

        @pl.when(py == n)
        def _(out=out):
            out[...] = result[:, Y - R :, :]

        @pl.when(py != n)
        def _(out=out):
            out[...] = result[:, :R, :]


def smooth_y(dims, many_y, ahead, own, *rest):
    rest = iter(rest)
    y_even, y_odd = refs_of(rest, many_y)
    result, pad = rest
    extend_y(dims, pad, own[...], parity_of("gy"), y_even[...], None if y_odd is None else y_odd[...])

    def store(x, value):
        result[x : x + value.shape[0]] = value

    filter_y(dims, pad, store)


def smooth_z(dims, many_z, weights, own, *rest):
    rest = iter(rest)
    z_even, z_odd = refs_of(rest, many_z)
    (result,) = rest
    value = own[...] + halo_z(weights, parity_of("gz"), flat(dims, z_even), flat(dims, z_odd))
    result[...] = value.reshape(dims)


def relax(pulled, vel, speed_sq, label, drag, store):
    plus = {q: pulled[q] + pulled[q + 1] for q in range(1, Q, 2)}
    minus = {q: pulled[q] - pulled[q + 1] for q in range(1, Q, 2)}
    axes = (1, 3, 5)
    straight = plus[1] + plus[3] + plus[5]
    slanted = plus[7] + plus[9] + plus[11] + plus[13] + plus[15] + plus[17]
    zeroth = (1.0 / 3.0) * pulled[0] + (1.0 / 18.0) * straight + (1.0 / 36.0) * slanted
    first, diagonal = [], []
    for a in range(3):
        terms = [(velocity[q][a], minus[q]) for q in range(7, Q, 2) if velocity[q][a] != 0]
        first.append((1.0 / 18.0) * minus[axes[a]] + (1.0 / 36.0) * signed(terms))
        both = [(1, plus[q]) for q in range(7, Q, 2) if velocity[q][a] != 0]
        diagonal.append((1.0 / 18.0) * plus[axes[a]] + (1.0 / 36.0) * signed(both))
    xy = (1.0 / 36.0) * (plus[7] - plus[9])
    xz = (1.0 / 36.0) * (plus[11] - plus[13])
    yz = (1.0 / 36.0) * (plus[15] - plus[17])
    turned = [
        diagonal[0] * vel[0] + xy * vel[1] + xz * vel[2],
        xy * vel[0] + diagonal[1] * vel[1] + yz * vel[2],
        xz * vel[0] + yz * vel[1] + diagonal[2] * vel[2],
    ]
    quadric = vel[0] * turned[0] + vel[1] * turned[1] + vel[2] * turned[2]
    eq_scalar = zeroth * (1.0 + 1.5 * speed_sq) - 4.5 * quadric
    eq_vector = [3.0 * first[a] + 9.0 * turned[a] - 3.0 * zeroth * vel[a] for a in range(3)]
    fluid, solid, inlet = label == 0, label == 1, label == 2
    zero = jnp.zeros_like(eq_scalar)
    keep = jnp.where(fluid, 1.0 - relax_rate, zero)
    bounce = jnp.where(solid, 1.0, zero)
    level = relax_rate * eq_scalar
    tilt = [relax_rate * v for v in eq_vector]
    if drag is not None:
        level = level - drag * speed_sq
        tilt = [t + drag * v for t, v in zip(tilt, vel)]
    level = jnp.where(fluid, level, jnp.where(solid, zero, eq_scalar))
    tilt = [jnp.where(fluid, t, jnp.where(inlet, v, zero)) for t, v in zip(tilt, eq_vector)]
    store(0, (keep + bounce) * pulled[0] + level)
    for q in range(1, Q, 2):
        lean = lean_of(q, tilt)
        store(q, keep * pulled[q] + bounce * pulled[q + 1] + (level + lean))
        store(q + 1, keep * pulled[q + 1] + bounce * pulled[q] + (level - lean))


def lean_of(q, vector):
    return signed([(velocity[q][a], vector[a]) for a in range(3) if velocity[q][a] != 0])


def square(vel):
    return vel[0] * vel[0] + vel[1] * vel[1] + vel[2] * vel[2]


def far_x(dims, odd, weights, partial, beyond, out, smooth):
    X, Y, Z = dims
    smooth[...] = dot(flat(dims, beyond), weights[0])
    px = parity_of("gx")
    pl.when(px == odd)(lambda: add_side(dims, partial, smooth, 0, out, True))
    pl.when(px != odd)(lambda: add_side(dims, partial, smooth, 0, out, False))


def beside_x(dims, many_y, many_z, adj, flow_ref, mask, own, *rest):
    X, Y, Z = dims
    rest = iter(rest)
    y_even, y_odd = refs_of(rest, many_y)
    z_even, z_odd = refs_of(rest, many_z)
    partial, base = rest
    for e in range(X + 2 * R):
        terms = [(i - e + 2 * R, i * Y) for i in range(X) if 0 <= i - e + 2 * R <= 2 * R]
        partial[e] = sum(TAPS[k] * own[at : at + Y, :] for k, at in terms)
    pull = Pull(adj, dims, parity_of("gy"), y_even, y_odd, parity_of("gz"), z_even, z_odd)

    def layer(x, _):
        around = {c: pull.faces(x + c) for c in (-1, 0, 1)}
        pulled = [pull.both(q, x + velocity[q][0], around[velocity[q][0]]) for q in range(Q)]
        vel = [flow_ref[a, x] for a in range(3)]

        def store(q, value):
            base[q, x] = value

        relax(pulled, vel, square(vel), mask[x], None, store)
        return 0

    lax.fori_loop(1, X - 1, layer, 0)


def collide(dims, many_x, many_y, many_z, step, adj, base, flow_ref, damp, mask, *rest):
    X, Y, Z = dims
    rest = iter(rest)
    y_even, y_odd = refs_of(rest, many_y)
    z_even, z_odd = refs_of(rest, many_z)
    x_even, x_odd = refs_of(rest, many_x)
    (out,) = rest
    px, py, pz = parity_of("gx"), parity_of("gy"), parity_of("gz")
    pull = Pull(adj, dims, py, y_even, y_odd, pz, z_even, z_odd)
    begin = pl.program_id(0) * step
    u_at = R * Y

    def layer(i, _):
        x = begin + i
        vel = [flow_ref[a, x] for a in range(3)]
        drag = jnp.where(mask[x] == 0, damp[x] * flow_ref[3, x], 0.0)
        level = drag * square(vel)
        tilt = [drag * v for v in vel]
        out[0, i] = base[0, x] - level
        for q in range(1, Q, 2):
            lean = lean_of(q, tilt)
            out[q, i] = base[q, x] + (lean - level)
            out[q + 1, i] = base[q + 1, x] - (lean + level)
        return 0

    def edge(x, i, toward):
        around = {c: pull.faces(x + c) for c in (0, -toward)}
        pulled = []
        for q in range(Q):
            cx = velocity[q][0]
            if cx == toward:
                at = u_at + Y * (PLUS if cx > 0 else MINUS)[0].index(q)
                both = sides(px, x_even[at : at + Y, :], None if x_odd is None else x_odd[at : at + Y, :])
                pulled.append(both[int(cx > 0)])
            else:
                pulled.append(pull.both(q, x + cx, around[cx]))
        vel = [flow_ref[a, x] for a in range(3)]

        def store(q, value):
            out[q, i] = value

        relax(pulled, vel, square(vel), mask[x], damp[x] * flow_ref[3, x], store)

    lax.fori_loop(0, step, layer, 0, unroll=2)
    pl.when(pl.program_id(0) == 0)(lambda: edge(0, 0, -1))
    pl.when(pl.program_id(0) == X // step - 1)(lambda: edge(X - 1, step - 1, 1))


def local(counts, forward, adjoint, design, mask):
    many_x, many_y, many_z = (int(n > 2) for n in counts)
    nx, ny, nz = counts
    dims = design.shape
    X, Y, Z = dims
    weights = jnp.asarray(band(Z))
    hbm = pl.BlockSpec(memory_space=pltpu.HBM)
    cells = X * Y * Z
    some = lambda pair: [v for v in pair if v is not None]
    pair = lambda items: (items[0], items[1] if len(items) > 1 else None)
    dma = pltpu.SemaphoreType.DMA

    y_rows = X * R + 5 * X
    *to_y, design = call(
        functools.partial(pack_y, dims, many_y),
        [f32(y_rows, Z)] * (1 + many_y) + [f32(X, Y, Z)],
        (in_hbm(adjoint), in_hbm(design)),
        [hbm, hbm],
        [pltpu.VMEM((1 + many_y, 5, X, R, Z), jnp.float32), dma((1 + many_y, 5)), dma],
        limit=4,
        name="pack_y",
    )
    got_y = some(exchange("gy", ny, *pair(to_y)))

    flow_values, factor, *faces = call(
        functools.partial(prepare, dims, many_z),
        [f32(4, X, Y, Z)] + [f32(X, Y, Z)] * (2 + many_z),
        (to_y[0], in_hbm(forward), adjoint),
        vmem(1) + [hbm] + vmem(1),
        [pltpu.VMEM((3, X + 2, Y, Z), jnp.float32)] * 2 + [pltpu.VMEM((Q, X, Y, Z), jnp.float32), dma((4,))],
        limit=16,
        flops=200 * cells,
        moved=44 * 4 * cells,
        name="prepare",
    )

    filtered_y, *to_z = call(
        functools.partial(design_y, dims, many_y, many_z),
        [f32(X, Y, Z)] * (2 + many_z),
        (design, *faces, *got_y),
        None,
        [pltpu.VMEM((X, Y + 2 * R, Z), jnp.float32), pltpu.VMEM((2, X, Z), jnp.float32)],
        limit=8,
        name="design_y",
    )
    got_z = some(exchange("gz", nz, *pair(to_z)))

    smooth, factor, beyond = call(
        functools.partial(factor_y, dims, many_y),
        [f32(X * Y, Z), f32(X, Y, Z), f32(X, Y, Z)],
        (weights, filtered_y, flow_values, factor, *got_y),
        limit=8,
        flops=200 * cells,
        name="factor_y",
    )
    beyond = swap(beyond, "gx", nx, 0)

    x_rows = R * Y + 8 * Y
    even, smooth, factor = call(
        functools.partial(pack_x, dims, many_y, many_z),
        [f32(x_rows + (1 + many_z) * Y, Z), f32(X * Y, Z), f32(X, Y, Z)],
        (adjoint, weights, smooth, factor, flow_values, *got_y, *got_z),
        limit=16,
        name="pack_x",
    )
    to_x = [even]
    if many_x:
        to_x += call(
            functools.partial(pack_odd, dims, many_y, many_z),
            [f32(x_rows + (1 + many_z) * Y, Z)],
            (adjoint, even, factor, flow_values, *got_y, *got_z),
            limit=16,
            name="pack_odd",
        )
    got_x = some(exchange("gx", nx, *pair(to_x)))

    partial, base = call(
        functools.partial(beside_x, dims, many_y, many_z),
        [f32(X + 2 * R, Y, Z), f32(Q, X, Y, Z)],
        (adjoint, flow_values, mask, smooth, *got_y, *got_z),
        limit=16,
        flops=100000 * cells,
        moved=1000,
        name="beside_x",
    )
    for odd, layers in enumerate([beyond] + ([relay(beyond, "gx", nx)] if many_x else [])):
        (partial,) = call(
            functools.partial(far_x, dims, odd),
            [f32(X + 2 * R, Y, Z)],
            (weights, partial, layers),
            None,
            [pltpu.VMEM((X * Y, Z), jnp.float32)],
            limit=8,
            flops=1000,
            moved=1000,
            name="far_odd" if odd else "far_even",
        )

    result, damp, *to_y = call(
        functools.partial(source, dims, many_x, many_y, many_z),
        [f32(X, Y, Z), f32(X, Y, Z)] + [f32(X, R, Z)] * (1 + many_y),
        (jnp.asarray(packed_band(dims)), partial, factor, flow_values, *to_x, *got_x),
        None,
        [pltpu.VMEM((X + 2 * R, Y, Z), jnp.float32)] * 2,
        limit=8,
        name="source",
    )
    got_y2 = some(exchange("gy", ny, *pair(to_y)))

    step = 4
    whole = pl.BlockSpec(memory_space=pltpu.VMEM)
    adjoint_next = call(
        functools.partial(collide, dims, many_x, many_y, many_z, step),
        f32(Q, X, Y, Z),
        (adjoint, base, flow_values, damp, mask, *got_y, *got_z, *got_x),
        [whole] * (5 + len(got_y) + len(got_z) + len(got_x)),
        out_specs=pl.BlockSpec((Q, step, Y, Z), lambda i: (0, i, 0, 0)),
        grid=(X // step,),
        limit=16,
        flops=300 * cells,
        moved=44 * 4 * cells,
        name="collide",
    )

    (filtered_xy,) = call(
        functools.partial(smooth_y, dims, many_y),
        [f32(X, Y, Z)],
        (in_hbm(adjoint_next), result, *got_y2),
        [hbm] + vmem(1 + len(got_y2)),
        [pltpu.VMEM((X, Y + 2 * R, Z), jnp.float32)],
        limit=4,
        name="smooth_y",
    )
    got_z2 = some(exchange("gz", nz, filtered_xy, filtered_xy if many_z else None))
    (own,) = call(
        functools.partial(own_z, dims),
        [f32(X * Y, Z)],
        (weights, filtered_xy),
        limit=4,
        flops=200 * cells,
        name="own_z",
    )
    (sensitivity,) = call(
        functools.partial(smooth_z, dims, many_z),
        [f32(X, Y, Z)],
        (weights, own, *got_z2),
        limit=4,
        name="smooth_z",
    )
    return adjoint_next, sensitivity


def solution(mesh):
    counts = tuple(mesh.shape[a] for a in ("gx", "gy", "gz"))
    populations, field = P(None, "gx", "gy", "gz"), P("gx", "gy", "gz")
    return jax.shard_map(
        functools.partial(local, counts),
        mesh=mesh,
        in_specs=(populations, populations, field, field),
        out_specs=(populations, field),
        check_vma=False,
    )
```

```python
import functools
import math

import jax
import jax.numpy as jnp
import numpy as np
from jax import lax
from jax.experimental import pallas as pl
from jax.experimental.pallas import tpu as pltpu
from jax.sharding import PartitionSpec as P

Q = 19
R = 8

velocity = [
    (0, 0, 0),
    (1, 0, 0),
    (-1, 0, 0),
    (0, 1, 0),
    (0, -1, 0),
    (0, 0, 1),
    (0, 0, -1),
    (1, 1, 0),
    (-1, -1, 0),
    (1, -1, 0),
    (-1, 1, 0),
    (1, 0, 1),
    (-1, 0, -1),
    (1, 0, -1),
    (-1, 0, 1),
    (0, 1, 1),
    (0, -1, -1),
    (0, 1, -1),
    (0, -1, 1),
]
relax_rate = 1.25
sharpness = 64.0
threshold = 0.5
damping_max = 10.0
ramp_shape = 0.1


def fields_of(axis, sign):
    plus = [q for q in range(Q) if velocity[q][axis] == 1]
    return plus if sign > 0 else [q + 1 if q % 2 else q - 1 for q in plus]


PLUS = [fields_of(a, 1) for a in range(3)]
MINUS = [fields_of(a, -1) for a in range(3)]


def tap_weights():
    spread_width = R / 2.0
    unscaled = [math.exp(-((k - R) ** 2) / (2.0 * spread_width * spread_width)) for k in range(2 * R + 1)]
    summed = sum(unscaled)
    return [v / summed for v in unscaled]


TAPS = tap_weights()


def band(length):
    out = np.zeros((3, length, length), np.float32)
    for i in range(length):
        for k in range(-R, R + 1):
            j = i + k
            if j < 0:
                out[1, j + length, i] = TAPS[k + R]
            elif j >= length:
                out[2, j - length, i] = TAPS[k + R]
            else:
                out[0, j, i] = TAPS[k + R]
    return out


def packed_band(dims):
    X, Y, Z = dims
    out = np.zeros((2, 2, Z, Z), np.float32)
    for above_x in range(2):
        for above_z in range(2):
            for e in range(X):
                for i in range(X):
                    for z in range(R):
                        for j in range(R):
                            kx = i - e + 2 * R * above_x
                            kz = j - z + 2 * R * above_z
                            if 0 <= kx <= 2 * R and 0 <= kz <= 2 * R:
                                out[above_x, above_z, i * R + j, e * R + z] = TAPS[kx] * TAPS[kz]
    return out.reshape(4, Z, Z)


def sides(parity, even, odd):
    zero = jnp.zeros_like(even)
    if odd is None:
        return jnp.where(parity == 0, zero, even), jnp.where(parity == 0, even, zero)
    return jnp.where(parity == 0, odd, even), jnp.where(parity == 0, even, odd)


def parity_of(axis):
    return lax.rem(lax.axis_index(axis), 2)


def swap(array, axis, count, first):
    pairs = [(i, i + 1) for i in range(first, count - 1, 2)]
    return lax.ppermute(array, axis, pairs + [(b, a) for a, b in pairs])


def relay(array, axis, count):
    pairs = [(i + 2, i) for i in range(1, count - 2, 2)] + [(i - 2, i) for i in range(2, count, 2)]
    return lax.ppermute(array, axis, pairs)


def exchange(axis, count, even, odd):
    return swap(even, axis, count, 0), (None if odd is None else swap(odd, axis, count, 1))


def vmem(count):
    return [pl.BlockSpec(memory_space=pltpu.VMEM)] * count


def in_hbm(array):
    return pltpu.with_memory_space_constraint(array, pltpu.HBM)


def f32(*shape):
    return jax.ShapeDtypeStruct(shape, jnp.float32)


def call(body, outs, args, specs=None, scratch=(), limit=16, flops=1e6, moved=1e6, **rest):
    return pl.pallas_call(
        body,
        out_shape=outs,
        in_specs=specs or vmem(len(args)),
        out_specs=rest.pop("out_specs", tuple(vmem(len(outs)))),
        scratch_shapes=list(scratch),
        compiler_params=pltpu.CompilerParams(vmem_limit_bytes=limit * 2**20),
        cost_estimate=pl.CostEstimate(flops=int(flops), bytes_accessed=int(moved), transcendentals=0),
        **rest,
    )(*args)


def filter_rows(load):
    total = TAPS[R] * load(R)
    for k in range(R):
        total = total + TAPS[k] * (load(k) + load(2 * R - k))
    return total


def dot(a, b):
    return jnp.dot(a, b, preferred_element_type=jnp.float32, precision=lax.Precision.HIGHEST)


def row_of(ref, at):
    return ref[pl.ds(at, 1), :]


class Pull:
    def __init__(self, adj, dims, py, y_even, y_odd, pz=None, z_even=None, z_odd=None):
        self.adj, self.dims = adj, dims
        self.py, self.y_even, self.y_odd = py, y_even, y_odd
        self.pz, self.z_even, self.z_odd = pz, z_even, z_odd
        X, Y, Z = dims
        self.row = lax.broadcasted_iota(jnp.int32, (Y, Z), 0)
        self.lane = lax.broadcasted_iota(jnp.int32, (Y, Z), 1)

    def along_y(self, q, x):
        X, Y, Z = self.dims
        here = self.adj[q, x]
        cy = velocity[q][1]
        if cy == 0:
            return here
        at = X * R + X * (PLUS if cy > 0 else MINUS)[1].index(q) + x
        even = row_of(self.y_even, at)
        odd = None if self.y_odd is None else row_of(self.y_odd, at)
        below, above = sides(self.py, even, odd)
        if cy > 0:
            return jnp.where(self.row == Y - 1, above, pltpu.roll(here, Y - 1, 0))
        return jnp.where(self.row == 0, below, pltpu.roll(here, 1, 0))

    def faces(self, x):
        even = self.z_even[x]
        odd = None if self.z_odd is None else self.z_odd[x]
        return sides(self.pz, even, odd)

    def both(self, q, x, faces):
        X, Y, Z = self.dims
        here = self.along_y(q, x)
        cz = velocity[q][2]
        if cz == 0:
            return here
        below, above = faces
        if cz > 0:
            j = PLUS[2].index(q)
            face = pltpu.roll(above, 4 - j, 1) if j != 4 else above
            return jnp.where(self.lane == Z - 1, face, pltpu.roll(here, Z - 1, 1))
        j = MINUS[2].index(q)
        face = pltpu.roll(below, Z - j, 1) if j else below
        return jnp.where(self.lane == 0, face, pltpu.roll(here, 1, 1))


def refs_of(refs, odd):
    even = next(refs)
    return even, (next(refs) if odd else None)


def pack_y(dims, many, adj, design, *rest):
    X, Y, Z = dims
    outs = rest[: 1 + many]
    kept, tiles, sems, kept_sem = rest[1 + many :]
    py = parity_of("gy")
    keep = pltpu.make_async_copy(design, kept, kept_sem)
    keep.start()

    def copies(n, up):
        names = (MINUS if up else PLUS)[1]
        first = Y - R if up else 0
        return [
            pltpu.make_async_copy(adj.at[q, :, pl.ds(first, R), :], tiles.at[n, j], sems.at[n, j])
            for j, q in enumerate(names)
        ]

    def start(n, out, up):
        for c in copies(n, up):
            c.start()

    def fill(n, out, up):
        first = Y - R if up else 0
        out[: X * R, :] = kept[:, first : first + R, :].reshape(X * R, Z)
        for c in copies(n, up):
            c.wait()
        for j in range(5):
            out[X * R + X * j : X * R + X * (j + 1), :] = tiles[n, j, :, R - 1 if up else 0, :]

    def each(act):
        for n, out in enumerate(outs):
            pl.when(py == n)(functools.partial(act, n, out, True))
            pl.when(py != n)(functools.partial(act, n, out, False))

    each(start)
    keep.wait()
    each(fill)


def prepare(dims, many_z, ahead, forward, adj, *rest):
    X, Y, Z = dims
    rest = iter(rest)
    flow_ref, factor = next(rest), next(rest)
    outs = [next(rest) for _ in range(1 + many_z)]
    rising, falling, straight, members_ref, sems = rest
    pz = parity_of("gz")
    part = X // 4
    copies = [
        pltpu.make_async_copy(
            forward.at[:, pl.ds(i * part, part)], members_ref.at[:, pl.ds(i * part, part)], sems.at[i]
        )
        for i in range(4)
    ]
    for c in copies:
        c.start()
    row = lax.broadcasted_iota(jnp.int32, (Y, Z), 0)
    lane = lax.broadcasted_iota(jnp.int32, (Y, Z), 1)
    zero = jnp.zeros((Y, Z), jnp.float32)

    def along_y(q, x):
        here, cy = adj[q, x], velocity[q][1]
        if cy == 0:
            return here
        return jnp.where(row == (Y - 1 if cy > 0 else 0), zero, pltpu.roll(here, (-cy) % Y, 0))

    def both(q, x):
        here, cz = along_y(q, x), velocity[q][2]
        if cz == 0:
            return here
        return jnp.where(lane == (Z - 1 if cz > 0 else 0), zero, pltpu.roll(here, (-cz) % Z, 1))

    for a in range(3):
        rising[a, X] = zero
        falling[a, 1] = zero

    def moments(x, _):
        groups = {}
        for q in range(1, Q):
            groups.setdefault(velocity[q][0], {})[q] = both(q, x)
        level, up, down = moment_of(groups[0]), moment_of(groups[1]), moment_of(groups[-1])
        for a in range(3):
            rising[a, x] = up[a]
            falling[a, x + 2] = down[a]
        for a in range(1, 3):
            straight[a - 1, x] = level[a]
        return 0

    def layer(x, _):
        members = [members_ref[q, x] for q in range(Q)]
        inverse = 1.0 / sum(members[1:], members[0])
        total = None
        for a in range(3):
            terms = [(velocity[q][a], members[q] - members[q + 1]) for q in range(1, Q, 2) if velocity[q][a] != 0]
            vel = signed(terms) * inverse
            flow_ref[a, x] = vel
            moment = rising[a, x + 1] + falling[a, x + 1]
            if a > 0:
                moment = moment + straight[a - 1, x]
            term = vel * (vel - moment)
            total = term if total is None else total + term
        flow_ref[3, x] = inverse
        factor[x] = total
        return 0

    def fill(out, up):
        names = (MINUS if up else PLUS)[2]

        def face(x, _):
            value = zero
            for j, q in enumerate(names):
                slot = slot_of(Z, up, j)
                value = jnp.where(lane == slot, pltpu.roll(along_y(q, x), shift_of(Z, up, j), 1), value)
            out[x] = value
            return 0

        lax.fori_loop(0, X, face, 0, unroll=2)

    lax.fori_loop(0, X, moments, 0, unroll=2)
    for n, out in enumerate(outs):
        pl.when(pz == n)(functools.partial(fill, out, True))
        pl.when(pz != n)(functools.partial(fill, out, False))
    for i, c in enumerate(copies):
        c.wait()
        lax.fori_loop(i * part, (i + 1) * part, layer, 0, unroll=2)


def slot_of(Z, up, j):
    return j if up else Z - 5 + j


def shift_of(Z, up, j):
    return (slot_of(Z, up, j) - (Z - 1 if up else 0)) % Z


def extend_y(dims, pad, own, py, even, odd):
    X, Y, Z = dims
    below, above = sides(py, even, odd)
    pad[:, :R, :] = below
    pad[:, R : R + Y, :] = own
    pad[:, R + Y :, :] = above


def filter_y(dims, pad, store, step=2):
    X, Y, Z = dims
    for x in range(0, X, step):
        store(x, filter_rows(lambda k: pad[x : x + step, k : k + Y, :]))


def design_y(dims, many_y, many_z, design, *rest):
    X, Y, Z = dims
    rest = iter(rest)
    faces = [next(rest) for _ in range(1 + many_z)]
    y_even, y_odd = refs_of(rest, many_y)
    filtered = next(rest)
    outs = [next(rest) for _ in range(1 + many_z)]
    pad, edges = rest
    pz = parity_of("gz")
    py = parity_of("gy")

    def halo(ref):
        return ref[: X * R, :].reshape(X, R, Z)

    extend_y(dims, pad, design[...], py, halo(y_even), None if y_odd is None else halo(y_odd))

    def store(x, value):
        filtered[x : x + value.shape[0]] = value

    filter_y(dims, pad, store)
    row = lax.broadcasted_iota(jnp.int32, (Y, Z), 0)
    lane = lax.broadcasted_iota(jnp.int32, (Y, Z), 1)

    def fill(out, face, up):
        names = (MINUS if up else PLUS)[2]
        slanted = [(j, q) for j, q in enumerate(names) if velocity[q][1] != 0]
        for i, (j, q) in enumerate(slanted):
            edges[i] = pltpu.roll(rows_of(dims, py, y_even, y_odd, q), shift_of(Z, up, j), 1)
        first, last = slot_of(Z, up, 0), slot_of(Z, up, 4)

        def layer(x, _):
            value = jnp.where((lane >= first) & (lane <= last), face[x], filtered[x])
            for i, (j, q) in enumerate(slanted):
                at = (row == (Y - 1 if velocity[q][1] > 0 else 0)) & (lane == slot_of(Z, up, j))
                value = jnp.where(at, edges[i, pl.ds(x, 1), :], value)
            out[x] = value
            return 0

        lax.fori_loop(0, X, layer, 0, unroll=True)

    for n, (out, face) in enumerate(zip(outs, faces)):
        pl.when(pz == n)(functools.partial(fill, out, face, True))
        pl.when(pz != n)(functools.partial(fill, out, face, False))


def rows_of(dims, py, even, odd, q):
    X, Y, Z = dims
    above = velocity[q][1] > 0
    at = X * R + X * (PLUS if above else MINUS)[1].index(q)
    return sides(py, even[at : at + X, :], None if odd is None else odd[at : at + X, :])[int(above)]


def signed(terms):
    total = None
    for sign, value in terms:
        value = value if sign > 0 else -value
        total = value if total is None else total + value
    return total


def moment_of(values):
    return [
        signed([(velocity[q][a], v) for q, v in values.items() if velocity[q][a] != 0]) for a in range(3)
    ]


def halo_z(weights, pz, even, odd):
    value = dot(even, jnp.where(pz == 0, weights[2], weights[1]))
    if odd is not None:
        value = value + dot(odd, jnp.where(pz == 0, weights[1], weights[2]))
    return value


def flat(dims, ref):
    X, Y, Z = dims
    return None if ref is None else ref[...].reshape(X * Y, Z)


def own_z(dims, weights, field, out):
    out[...] = dot(flat(dims, field), weights[0])


def factor_y(dims, many_y, weights, filtered_y, flow_ref, factor, *rest):
    X, Y, Z = dims
    rest = iter(rest)
    y_even, y_odd = refs_of(rest, many_y)
    smooth, out = rest
    smooth[...] = dot(flat(dims, filtered_y), weights[0])
    out[...] = factor[...]
    py = parity_of("gy")
    row = lax.broadcasted_iota(jnp.int32, (X, Z), 0)
    lane = lax.broadcasted_iota(jnp.int32, (X, Z), 1)
    for edge, names in ((0, MINUS[1]), (Y - 1, PLUS[1])):
        values = {}
        for q in names:
            value = rows_of(dims, py, y_even, y_odd, q)
            cx, _, cz = velocity[q]
            if cx != 0:
                value = jnp.where(row == (X - 1 if cx > 0 else 0), 0.0, pltpu.roll(value, (-cx) % X, 0))
            if cz != 0:
                value = jnp.where(lane == (Z - 1 if cz > 0 else 0), 0.0, pltpu.roll(value, (-cz) % Z, 1))
            values[q] = value
        moment = moment_of(values)
        total = factor[:, edge, :]
        for a in range(3):
            total = total - flow_ref[a, :, edge, :] * moment[a]
        out[:, edge, :] = total


def faces_x(dims, out, up, factor, flow_ref, pull):
    X, Y, Z = dims
    names = (MINUS if up else PLUS)[0]
    edge = X - 1 if up else 0
    first = X - R if up else 0
    at = R * Y
    out[:at, :] = factor[first : first + R].reshape(R * Y, Z)
    faces = pull.faces(edge)
    for q in names:
        out[at : at + Y, :] = pull.both(q, edge, faces)
        at += Y
    for a in range(3):
        out[at : at + Y, :] = flow_ref[a, edge]
        at += Y


def pack_halo(dims, pz, refs, out):
    X, Y, Z = dims
    lane = lax.broadcasted_iota(jnp.int32, (Y, Z), 1)
    for n, ref in enumerate(refs):
        value = jnp.zeros((Y, Z), jnp.float32)
        for x in range(X):
            there = (lane >= R * x) & (lane < R * (x + 1))
            value = jnp.where(there, pltpu.roll(ref[x], lanes_x(dims, pz, n, x), 1), value)
        out[(R + 8 + n) * Y : (R + 9 + n) * Y, :] = value


def pack_odd(dims, many_y, many_z, adj, ahead, factor, flow_ref, *rest):
    X, Y, Z = dims
    rest = iter(rest)
    y_even, y_odd = refs_of(rest, many_y)
    z_even, z_odd = refs_of(rest, many_z)
    (out,) = rest
    px = parity_of("gx")
    pz = parity_of("gz")
    out[(R + 8) * Y :, :] = ahead[(R + 8) * Y :, :]
    pull = Pull(adj, dims, parity_of("gy"), y_even, y_odd, pz, z_even, z_odd)
    pl.when(px == 1)(lambda: faces_x(dims, out, True, factor, flow_ref, pull))
    pl.when(px != 1)(lambda: faces_x(dims, out, False, factor, flow_ref, pull))


def pack_x(dims, many_y, many_z, adj, weights, smooth, factor_in, flow_ref, *rest):
    X, Y, Z = dims
    rest = iter(rest)
    y_even, y_odd = refs_of(rest, many_y)
    z_even, z_odd = refs_of(rest, many_z)
    out, whole, factor = rest
    px, py, pz = parity_of("gx"), parity_of("gy"), parity_of("gz")
    value = smooth[...] + halo_z(weights, pz, flat(dims, z_even), flat(dims, z_odd))
    whole[...] = value
    pack_halo(dims, pz, [z_even, z_odd][: 1 + many_z], out)
    lane = lax.broadcasted_iota(jnp.int32, (Y, Z), 1)
    factor[...] = factor_in[...]

    def correct(ref, above):
        names = (PLUS if above else MINUS)[2]
        edge = Z - 1 if above else 0
        zero = jnp.zeros((Y, Z), jnp.float32)

        def layer(x, _):
            values = {}
            for j, q in enumerate(names):
                cx = velocity[q][0]
                face = ref[jnp.clip(x + cx, 0, X - 1)] if cx else ref[x]
                shift = (edge - slot_of(Z, not above, j)) % Z
                face = pltpu.roll(face, shift, 1) if shift else face
                if cx != 0:
                    face = jnp.where(x == (X - 1 if cx > 0 else 0), zero, face)
                values[q] = face
            moment = moment_of(values)
            change = flow_ref[0, x] * moment[0] + flow_ref[1, x] * moment[1] + flow_ref[2, x] * moment[2]
            factor[x] = factor[x] - jnp.where(lane == edge, change, zero)
            return 0

        lax.fori_loop(0, X, layer, 0, unroll=True)

    for n, ref in enumerate([z_even, z_odd][: 1 + many_z]):
        pl.when(pz == n)(functools.partial(correct, ref, True))
        pl.when(pz != n)(functools.partial(correct, ref, False))

    pull = Pull(adj, dims, py, y_even, y_odd, pz, z_even, z_odd)

    pl.when(px == 0)(lambda: faces_x(dims, out, True, factor, flow_ref, pull))
    pl.when(px != 0)(lambda: faces_x(dims, out, False, factor, flow_ref, pull))


def project(filtered):
    base = math.tanh(sharpness * threshold)
    denominator = base + math.tanh(sharpness * (1.0 - threshold))
    inner = jnp.tanh(sharpness * (filtered - threshold))
    physical = (base + inner) * (1.0 / denominator)
    steep = (sharpness / denominator) * (1.0 - inner * inner)
    inverse = 1.0 / (ramp_shape + physical)
    return physical, steep, inverse


def taps_of(X, above, e):
    shift = 2 * R + (X if above else -X) - e
    return [(TAPS[i + shift], i) for i in range(X) if 0 <= i + shift <= 2 * R]


def add_side(dims, base, layers, at, out, above):
    X, Y, Z = dims
    for e in range(X + 2 * R):
        total = base[e]
        for tap, i in taps_of(X, above, e):
            total = total + tap * layers[at + i * Y : at + (i + 1) * Y, :]
        out[e] = total


def lanes_x(dims, pz, n, x):
    Z = dims[2]
    return jnp.where(pz == n, (R * x) % Z, (R * x + R) % Z)


def half_source(dims, above, near, many_z, pz, weights, partial, relayed, factor, flow_ref, own, got, smooth, ext, damp, base, result):
    X, Y, Z = dims
    if near:
        layers = range(2 * R, X + 2 * R) if above else range(X)
    else:
        layers = range(X, X + 2 * R) if above else range(2 * R)
    u_at, v_at, d_at = R * Y, R * Y + 5 * Y, R * Y + 8 * Y
    for e in layers:
        total = partial[e]
        if relayed is not None:
            for tap, i in taps_of(X, above, e):
                total = total + tap * relayed[i * Y : (i + 1) * Y, :]
        smooth[e] = total
        if R <= e < R + X:
            ext[e] = factor[e - R]
        elif got is None:
            ext[e] = jnp.zeros((Y, Z), jnp.float32)
        else:
            at = (e - R - X if above else e) * Y
            ext[e] = got[at : at + Y, :]
    if got is not None:
        lane = lax.broadcasted_iota(jnp.int32, (Y, Z), 1)
        for n in range(1 + many_z):
            above_z = jnp.where(pz == n, 1, 0)
            value = dot(got[d_at + n * Y : d_at + (n + 1) * Y, :], weights[2 * int(above) + above_z])
            first = (Z - R) * above_z
            there = (lane >= first) & (lane < first + R)
            for i in range(X):
                e = i + X * int(above)
                moved = pltpu.roll(value, lax.rem(first + Z - R * i, Z), 1)
                smooth[e] = smooth[e] + jnp.where(there, moved, 0.0)

        def moment(ref, names):
            return moment_of({q: ref[u_at + j * Y : u_at + (j + 1) * Y, :] for j, q in enumerate(names)})

        def less(e, vel, m):
            ext[e] = ext[e] - (vel[0] * m[0] + vel[1] * m[1] + vel[2] * m[2])

        inner, outer = (R + X - 1, R + X) if above else (R, R - 1)
        there, here = (PLUS[0], MINUS[0]) if above else (MINUS[0], PLUS[0])
        less(inner, [flow_ref[a, inner - R] for a in range(3)], moment(got, there))
        less(outer, [got[v_at + a * Y : v_at + (a + 1) * Y, :] for a in range(3)], moment(own, here))
    slope = -damping_max * ramp_shape * (1.0 + ramp_shape)
    for e in layers:
        physical, steep, inverse = project(smooth[e])
        ext[e] = (slope * steep) * (inverse * inverse) * ext[e]
        if R <= e < R + X:
            damp[e - R] = (2.0 * damping_max * ramp_shape) * (1.0 - physical) * inverse
    for x in range(X):
        terms = [TAPS[e - x] * ext[e] for e in layers if 0 <= e - x <= 2 * R]
        if base is not None:
            terms = [base[x]] + terms
        result[x] = sum(terms[1:], terms[0]) if terms else jnp.zeros((Y, Z), jnp.float32)


def near_x(dims, many_z, weights, partial, factor, flow_ref, own, got, result, damp, smooth, ext):
    px, pz = parity_of("gx"), parity_of("gz")
    for parity in range(2):
        pl.when(px == parity)(
            functools.partial(
                half_source, dims, parity == 0, True, many_z, pz, weights, partial, None, factor, flow_ref,
                own, got, smooth, ext, damp, None, result,
            )
        )


def source(dims, many_x, many_y, many_z, weights, partial, factor, flow_ref, near, near_damp, *rest):
    X, Y, Z = dims
    rest = iter(rest)
    own, got, relayed = (next(rest), next(rest), next(rest)) if many_x else (None, None, None)
    result, damp = next(rest), next(rest)
    outs = [next(rest) for _ in range(1 + many_y)]
    smooth, ext = rest
    px, py, pz = parity_of("gx"), parity_of("gy"), parity_of("gz")
    damp[...] = near_damp[...]
    for parity in range(2):
        pl.when(px == parity)(
            functools.partial(
                half_source, dims, parity == 1, False, many_z, pz, weights, partial, relayed, factor, flow_ref,
                own, got, smooth, ext, damp, near, result,
            )
        )
    for n, out in enumerate(outs):

        @pl.when(py == n)
        def _(out=out):
            out[...] = result[:, Y - R :, :]

        @pl.when(py != n)
        def _(out=out):
            out[...] = result[:, :R, :]


def smooth_y(dims, many_y, ahead, own, *rest):
    rest = iter(rest)
    y_even, y_odd = refs_of(rest, many_y)
    result, pad = rest
    extend_y(dims, pad, own[...], parity_of("gy"), y_even[...], None if y_odd is None else y_odd[...])

    def store(x, value):
        result[x : x + value.shape[0]] = value

    filter_y(dims, pad, store)


def smooth_z(dims, many_z, weights, own, *rest):
    rest = iter(rest)
    z_even, z_odd = refs_of(rest, many_z)
    (result,) = rest
    value = own[...] + halo_z(weights, parity_of("gz"), flat(dims, z_even), flat(dims, z_odd))
    result[...] = value.reshape(dims)


def relax(pulled, vel, speed_sq, label, drag, store):
    plus = {q: pulled[q] + pulled[q + 1] for q in range(1, Q, 2)}
    minus = {q: pulled[q] - pulled[q + 1] for q in range(1, Q, 2)}
    axes = (1, 3, 5)
    straight = plus[1] + plus[3] + plus[5]
    slanted = plus[7] + plus[9] + plus[11] + plus[13] + plus[15] + plus[17]
    zeroth = (1.0 / 3.0) * pulled[0] + (1.0 / 18.0) * straight + (1.0 / 36.0) * slanted
    first, diagonal = [], []
    for a in range(3):
        terms = [(velocity[q][a], minus[q]) for q in range(7, Q, 2) if velocity[q][a] != 0]
        first.append((1.0 / 18.0) * minus[axes[a]] + (1.0 / 36.0) * signed(terms))
        both = [(1, plus[q]) for q in range(7, Q, 2) if velocity[q][a] != 0]
        diagonal.append((1.0 / 18.0) * plus[axes[a]] + (1.0 / 36.0) * signed(both))
    xy = (1.0 / 36.0) * (plus[7] - plus[9])
    xz = (1.0 / 36.0) * (plus[11] - plus[13])
    yz = (1.0 / 36.0) * (plus[15] - plus[17])
    turned = [
        diagonal[0] * vel[0] + xy * vel[1] + xz * vel[2],
        xy * vel[0] + diagonal[1] * vel[1] + yz * vel[2],
        xz * vel[0] + yz * vel[1] + diagonal[2] * vel[2],
    ]
    quadric = vel[0] * turned[0] + vel[1] * turned[1] + vel[2] * turned[2]
    eq_scalar = zeroth * (1.0 + 1.5 * speed_sq) - 4.5 * quadric
    eq_vector = [3.0 * first[a] + 9.0 * turned[a] - 3.0 * zeroth * vel[a] for a in range(3)]
    fluid, solid, inlet = label == 0, label == 1, label == 2
    zero = jnp.zeros_like(eq_scalar)
    keep = jnp.where(fluid, 1.0 - relax_rate, zero)
    bounce = jnp.where(solid, 1.0, zero)
    level = relax_rate * eq_scalar
    tilt = [relax_rate * v for v in eq_vector]
    if drag is not None:
        level = level - drag * speed_sq
        tilt = [t + drag * v for t, v in zip(tilt, vel)]
    level = jnp.where(fluid, level, jnp.where(solid, zero, eq_scalar))
    tilt = [jnp.where(fluid, t, jnp.where(inlet, v, zero)) for t, v in zip(tilt, eq_vector)]
    store(0, (keep + bounce) * pulled[0] + level)
    for q in range(1, Q, 2):
        lean = lean_of(q, tilt)
        store(q, keep * pulled[q] + bounce * pulled[q + 1] + (level + lean))
        store(q + 1, keep * pulled[q + 1] + bounce * pulled[q] + (level - lean))


def lean_of(q, vector):
    return signed([(velocity[q][a], vector[a]) for a in range(3) if velocity[q][a] != 0])


def square(vel):
    return vel[0] * vel[0] + vel[1] * vel[1] + vel[2] * vel[2]


def far_x(dims, partial, beyond, out):
    px = parity_of("gx")
    pl.when(px == 0)(lambda: add_side(dims, partial, beyond, 0, out, True))
    pl.when(px != 0)(lambda: add_side(dims, partial, beyond, 0, out, False))


def beside_x(dims, many_y, many_z, adj, flow_ref, mask, own, *rest):
    X, Y, Z = dims
    rest = iter(rest)
    y_even, y_odd = refs_of(rest, many_y)
    z_even, z_odd = refs_of(rest, many_z)
    partial, base = rest
    for e in range(X + 2 * R):
        terms = [(i - e + 2 * R, i * Y) for i in range(X) if 0 <= i - e + 2 * R <= 2 * R]
        partial[e] = sum(TAPS[k] * own[at : at + Y, :] for k, at in terms)
    pull = Pull(adj, dims, parity_of("gy"), y_even, y_odd, parity_of("gz"), z_even, z_odd)

    def layer(x, _):
        around = {c: pull.faces(x + c) for c in (-1, 0, 1)}
        pulled = [pull.both(q, x + velocity[q][0], around[velocity[q][0]]) for q in range(Q)]
        vel = [flow_ref[a, x] for a in range(3)]

        def store(q, value):
            base[q, x] = value

        relax(pulled, vel, square(vel), mask[x], None, store)
        return 0

    lax.fori_loop(1, X - 1, layer, 0)


def collide(dims, many_x, many_y, many_z, step, adj, base, flow_ref, damp, mask, *rest):
    X, Y, Z = dims
    rest = iter(rest)
    y_even, y_odd = refs_of(rest, many_y)
    z_even, z_odd = refs_of(rest, many_z)
    x_even, x_odd = refs_of(rest, many_x)
    (out,) = rest
    px, py, pz = parity_of("gx"), parity_of("gy"), parity_of("gz")
    pull = Pull(adj, dims, py, y_even, y_odd, pz, z_even, z_odd)
    begin = pl.program_id(0) * step
    u_at = R * Y

    def layer(i, _):
        x = begin + i
        vel = [flow_ref[a, x] for a in range(3)]
        drag = jnp.where(mask[x] == 0, damp[x] * flow_ref[3, x], 0.0)
        level = drag * square(vel)
        tilt = [drag * v for v in vel]
        out[0, i] = base[0, x] - level
        for q in range(1, Q, 2):
            lean = lean_of(q, tilt)
            out[q, i] = base[q, x] + (lean - level)
            out[q + 1, i] = base[q + 1, x] - (lean + level)
        return 0

    def edge(x, i, toward):
        around = {c: pull.faces(x + c) for c in (0, -toward)}
        pulled = []
        for q in range(Q):
            cx = velocity[q][0]
            if cx == toward:
                at = u_at + Y * (PLUS if cx > 0 else MINUS)[0].index(q)
                both = sides(px, x_even[at : at + Y, :], None if x_odd is None else x_odd[at : at + Y, :])
                pulled.append(both[int(cx > 0)])
            else:
                pulled.append(pull.both(q, x + cx, around[cx]))
        vel = [flow_ref[a, x] for a in range(3)]

        def store(q, value):
            out[q, i] = value

        relax(pulled, vel, square(vel), mask[x], damp[x] * flow_ref[3, x], store)

    lax.fori_loop(0, step, layer, 0, unroll=2)
    pl.when(pl.program_id(0) == 0)(lambda: edge(0, 0, -1))
    pl.when(pl.program_id(0) == X // step - 1)(lambda: edge(X - 1, step - 1, 1))


def local(counts, forward, adjoint, design, mask):
    many_x, many_y, many_z = (int(n > 2) for n in counts)
    nx, ny, nz = counts
    dims = design.shape
    X, Y, Z = dims
    weights = jnp.asarray(band(Z))
    hbm = pl.BlockSpec(memory_space=pltpu.HBM)
    cells = X * Y * Z
    some = lambda pair: [v for v in pair if v is not None]
    pair = lambda items: (items[0], items[1] if len(items) > 1 else None)
    dma = pltpu.SemaphoreType.DMA

    y_rows = X * R + 5 * X
    *to_y, design = call(
        functools.partial(pack_y, dims, many_y),
        [f32(y_rows, Z)] * (1 + many_y) + [f32(X, Y, Z)],
        (in_hbm(adjoint), in_hbm(design)),
        [hbm, hbm],
        [pltpu.VMEM((1 + many_y, 5, X, R, Z), jnp.float32), dma((1 + many_y, 5)), dma],
        limit=4,
        name="pack_y",
    )
    got_y = some(exchange("gy", ny, *pair(to_y)))

    flow_values, factor, *faces = call(
        functools.partial(prepare, dims, many_z),
        [f32(4, X, Y, Z)] + [f32(X, Y, Z)] * (2 + many_z),
        (to_y[0], in_hbm(forward), adjoint),
        vmem(1) + [hbm] + vmem(1),
        [pltpu.VMEM((3, X + 2, Y, Z), jnp.float32)] * 2
        + [pltpu.VMEM((2, X, Y, Z), jnp.float32), pltpu.VMEM((Q, X, Y, Z), jnp.float32), dma((4,))],
        limit=16,
        flops=200 * cells,
        moved=44 * 4 * cells,
        name="prepare",
    )

    filtered_y, *to_z = call(
        functools.partial(design_y, dims, many_y, many_z),
        [f32(X, Y, Z)] * (2 + many_z),
        (design, *faces, *got_y),
        None,
        [pltpu.VMEM((X, Y + 2 * R, Z), jnp.float32), pltpu.VMEM((2, X, Z), jnp.float32)],
        limit=8,
        name="design_y",
    )
    got_z = some(exchange("gz", nz, *pair(to_z)))

    smooth, factor = call(
        functools.partial(factor_y, dims, many_y),
        [f32(X * Y, Z), f32(X, Y, Z)],
        (weights, filtered_y, flow_values, factor, *got_y),
        limit=8,
        flops=200 * cells,
        name="factor_y",
    )
    beyond = swap(smooth, "gx", nx, 0)

    x_rows = R * Y + 8 * Y
    even, smooth, factor = call(
        functools.partial(pack_x, dims, many_y, many_z),
        [f32(x_rows + (1 + many_z) * Y, Z), f32(X * Y, Z), f32(X, Y, Z)],
        (adjoint, weights, smooth, factor, flow_values, *got_y, *got_z),
        limit=16,
        name="pack_x",
    )
    to_x = [even]
    if many_x:
        to_x += call(
            functools.partial(pack_odd, dims, many_y, many_z),
            [f32(x_rows + (1 + many_z) * Y, Z)],
            (adjoint, even, factor, flow_values, *got_y, *got_z),
            limit=16,
            name="pack_odd",
        )
    got_x = some(exchange("gx", nx, *pair(to_x)))

    partial, base = call(
        functools.partial(beside_x, dims, many_y, many_z),
        [f32(X + 2 * R, Y, Z), f32(Q, X, Y, Z)],
        (adjoint, flow_values, mask, smooth, *got_y, *got_z),
        limit=16,
        flops=100000 * cells,
        moved=1000,
        name="beside_x",
    )
    (partial,) = call(
        functools.partial(far_x, dims),
        [f32(X + 2 * R, Y, Z)],
        (partial, beyond),
        limit=8,
        flops=1000,
        moved=1000,
        name="far_x",
    )
    relayed = [relay(beyond, "gx", nx)] if many_x else []

    packed = jnp.asarray(packed_band(dims))
    extended = pltpu.VMEM((X + 2 * R, Y, Z), jnp.float32)
    near, near_damp = call(
        functools.partial(near_x, dims, many_z),
        [f32(X, Y, Z), f32(X, Y, Z)],
        (packed, partial, factor, flow_values, to_x[0], got_x[0]),
        None,
        [extended] * 2,
        limit=8,
        flops=1000,
        moved=1000,
        name="near_x",
    )
    result, damp, *to_y = call(
        functools.partial(source, dims, many_x, many_y, many_z),
        [f32(X, Y, Z), f32(X, Y, Z)] + [f32(X, R, Z)] * (1 + many_y),
        (packed, partial, factor, flow_values, near, near_damp, *to_x[1:], *got_x[1:], *relayed),
        None,
        [extended] * 2,
        limit=8,
        name="source",
    )
    got_y2 = some(exchange("gy", ny, *pair(to_y)))

    step = 4
    whole = pl.BlockSpec(memory_space=pltpu.VMEM)
    adjoint_next = call(
        functools.partial(collide, dims, many_x, many_y, many_z, step),
        f32(Q, X, Y, Z),
        (adjoint, base, flow_values, damp, mask, *got_y, *got_z, *got_x),
        [whole] * (5 + len(got_y) + len(got_z) + len(got_x)),
        out_specs=pl.BlockSpec((Q, step, Y, Z), lambda i: (0, i, 0, 0)),
        grid=(X // step,),
        limit=16,
        flops=300 * cells,
        moved=44 * 4 * cells,
        name="collide",
    )

    (filtered_xy,) = call(
        functools.partial(smooth_y, dims, many_y),
        [f32(X, Y, Z)],
        (in_hbm(adjoint_next), result, *got_y2),
        [hbm] + vmem(1 + len(got_y2)),
        [pltpu.VMEM((X, Y + 2 * R, Z), jnp.float32)],
        limit=4,
        name="smooth_y",
    )
    got_z2 = some(exchange("gz", nz, filtered_xy, filtered_xy if many_z else None))
    (own,) = call(
        functools.partial(own_z, dims),
        [f32(X * Y, Z)],
        (weights, filtered_xy),
        limit=4,
        flops=200 * cells,
        name="own_z",
    )
    (sensitivity,) = call(
        functools.partial(smooth_z, dims, many_z),
        [f32(X, Y, Z)],
        (weights, own, *got_z2),
        limit=4,
        name="smooth_z",
    )
    return adjoint_next, sensitivity


def solution(mesh):
    counts = tuple(mesh.shape[a] for a in ("gx", "gy", "gz"))
    populations, field = P(None, "gx", "gy", "gz"), P("gx", "gy", "gz")
    return jax.shard_map(
        functools.partial(local, counts),
        mesh=mesh,
        in_specs=(populations, populations, field, field),
        out_specs=(populations, field),
        check_vma=False,
    )
```

```python
import functools
import math

import jax
import jax.numpy as jnp
import numpy as np
from jax import lax
from jax.experimental import pallas as pl
from jax.experimental.pallas import tpu as pltpu
from jax.sharding import PartitionSpec as P

Q = 19
R = 8

velocity = [
    (0, 0, 0),
    (1, 0, 0),
    (-1, 0, 0),
    (0, 1, 0),
    (0, -1, 0),
    (0, 0, 1),
    (0, 0, -1),
    (1, 1, 0),
    (-1, -1, 0),
    (1, -1, 0),
    (-1, 1, 0),
    (1, 0, 1),
    (-1, 0, -1),
    (1, 0, -1),
    (-1, 0, 1),
    (0, 1, 1),
    (0, -1, -1),
    (0, 1, -1),
    (0, -1, 1),
]
relax_rate = 1.25
sharpness = 64.0
threshold = 0.5
damping_max = 10.0
ramp_shape = 0.1


def fields_of(axis, sign):
    plus = [q for q in range(Q) if velocity[q][axis] == 1]
    return plus if sign > 0 else [q + 1 if q % 2 else q - 1 for q in plus]


PLUS = [fields_of(a, 1) for a in range(3)]
MINUS = [fields_of(a, -1) for a in range(3)]


def tap_weights():
    spread_width = R / 2.0
    unscaled = [math.exp(-((k - R) ** 2) / (2.0 * spread_width * spread_width)) for k in range(2 * R + 1)]
    summed = sum(unscaled)
    return [v / summed for v in unscaled]


TAPS = tap_weights()


def band(length):
    out = np.zeros((3, length, length), np.float32)
    for i in range(length):
        for k in range(-R, R + 1):
            j = i + k
            if j < 0:
                out[1, j + length, i] = TAPS[k + R]
            elif j >= length:
                out[2, j - length, i] = TAPS[k + R]
            else:
                out[0, j, i] = TAPS[k + R]
    return out


def packed_band(dims):
    X, Y, Z = dims
    out = np.zeros((2, 2, Z, Z), np.float32)
    for above_x in range(2):
        for above_z in range(2):
            for e in range(X):
                for i in range(X):
                    for z in range(R):
                        for j in range(R):
                            kx = i - e + 2 * R * above_x
                            kz = j - z + 2 * R * above_z
                            if 0 <= kx <= 2 * R and 0 <= kz <= 2 * R:
                                out[above_x, above_z, i * R + j, e * R + z] = TAPS[kx] * TAPS[kz]
    return out.reshape(4, Z, Z)


def packed_band_z(dims):
    X, Y, Z = dims
    out = np.zeros((2, Z, Z), np.float32)
    for above in range(2):
        for i in range(X):
            for z in range(R):
                for j in range(R):
                    k = j - z + 2 * R * above
                    if 0 <= k <= 2 * R:
                        out[above, i * R + j, i * R + z] = TAPS[k]
    return out


def sides(parity, even, odd):
    zero = jnp.zeros_like(even)
    if odd is None:
        return jnp.where(parity == 0, zero, even), jnp.where(parity == 0, even, zero)
    return jnp.where(parity == 0, odd, even), jnp.where(parity == 0, even, odd)


def parity_of(axis):
    return lax.rem(lax.axis_index(axis), 2)


def swap(array, axis, count, first):
    pairs = [(i, i + 1) for i in range(first, count - 1, 2)]
    return lax.ppermute(array, axis, pairs + [(b, a) for a, b in pairs])


def relay(array, axis, count):
    pairs = [(i + 2, i) for i in range(1, count - 2, 2)] + [(i - 2, i) for i in range(2, count, 2)]
    return lax.ppermute(array, axis, pairs)


def swap_corner(array, counts, first_y, first_z):
    ny, nz = counts
    pairs = []
    for a in range(first_y, ny - 1, 2):
        for c in range(first_z, nz - 1, 2):
            for d, e in ((c, c + 1), (c + 1, c)):
                pairs += [(a * nz + d, (a + 1) * nz + e), ((a + 1) * nz + e, a * nz + d)]
    return lax.ppermute(array, ("gy", "gz"), pairs)


def exchange(axis, count, even, odd):
    return swap(even, axis, count, 0), (None if odd is None else swap(odd, axis, count, 1))


def vmem(count):
    return [pl.BlockSpec(memory_space=pltpu.VMEM)] * count


def in_hbm(array):
    return pltpu.with_memory_space_constraint(array, pltpu.HBM)


def f32(*shape):
    return jax.ShapeDtypeStruct(shape, jnp.float32)


def call(body, outs, args, specs=None, scratch=(), limit=16, flops=1e6, moved=1e6, **rest):
    return pl.pallas_call(
        body,
        out_shape=outs,
        in_specs=specs or vmem(len(args)),
        out_specs=rest.pop("out_specs", tuple(vmem(len(outs)))),
        scratch_shapes=list(scratch),
        compiler_params=pltpu.CompilerParams(vmem_limit_bytes=limit * 2**20),
        cost_estimate=pl.CostEstimate(flops=int(flops), bytes_accessed=int(moved), transcendentals=0),
        **rest,
    )(*args)


def filter_rows(load):
    total = TAPS[R] * load(R)
    for k in range(R):
        total = total + TAPS[k] * (load(k) + load(2 * R - k))
    return total


def dot(a, b):
    return jnp.dot(a, b, preferred_element_type=jnp.float32, precision=lax.Precision.HIGHEST)


def row_of(ref, at):
    return ref[pl.ds(at, 1), :]


class Pull:
    def __init__(self, adj, dims, py, y_even, y_odd, pz=None, z_even=None, z_odd=None):
        self.adj, self.dims = adj, dims
        self.py, self.y_even, self.y_odd = py, y_even, y_odd
        self.pz, self.z_even, self.z_odd = pz, z_even, z_odd
        X, Y, Z = dims
        self.row = lax.broadcasted_iota(jnp.int32, (Y, Z), 0)
        self.lane = lax.broadcasted_iota(jnp.int32, (Y, Z), 1)

    def along_y(self, q, x):
        X, Y, Z = self.dims
        here = self.adj[q, x]
        cy = velocity[q][1]
        if cy == 0:
            return here
        at = X * R + X * (PLUS if cy > 0 else MINUS)[1].index(q) + x
        even = row_of(self.y_even, at)
        odd = None if self.y_odd is None else row_of(self.y_odd, at)
        below, above = sides(self.py, even, odd)
        if cy > 0:
            return jnp.where(self.row == Y - 1, above, pltpu.roll(here, Y - 1, 0))
        return jnp.where(self.row == 0, below, pltpu.roll(here, 1, 0))

    def faces(self, x):
        even = self.z_even[x]
        odd = None if self.z_odd is None else self.z_odd[x]
        return sides(self.pz, even, odd)

    def both(self, q, x, faces):
        X, Y, Z = self.dims
        here = self.along_y(q, x)
        cz = velocity[q][2]
        if cz == 0:
            return here
        below, above = faces
        if cz > 0:
            j = PLUS[2].index(q)
            face = pltpu.roll(above, 4 - j, 1) if j != 4 else above
            return jnp.where(self.lane == Z - 1, face, pltpu.roll(here, Z - 1, 1))
        j = MINUS[2].index(q)
        face = pltpu.roll(below, Z - j, 1) if j else below
        return jnp.where(self.lane == 0, face, pltpu.roll(here, 1, 1))


def refs_of(refs, odd):
    even = next(refs)
    return even, (next(refs) if odd else None)


def pack_y(dims, many, adj, design, *rest):
    X, Y, Z = dims
    outs = rest[: 1 + many]
    kept, tiles, sems, kept_sem = rest[1 + many :]
    py = parity_of("gy")
    keep = pltpu.make_async_copy(design, kept, kept_sem)
    keep.start()

    def copies(n, up):
        names = (MINUS if up else PLUS)[1]
        first = Y - R if up else 0
        return [
            pltpu.make_async_copy(adj.at[q, :, pl.ds(first, R), :], tiles.at[n, j], sems.at[n, j])
            for j, q in enumerate(names)
        ]

    def start(n, out, up):
        for c in copies(n, up):
            c.start()

    def fill(n, out, up):
        first = Y - R if up else 0
        out[: X * R, :] = kept[:, first : first + R, :].reshape(X * R, Z)
        for c in copies(n, up):
            c.wait()
        for j in range(5):
            out[X * R + X * j : X * R + X * (j + 1), :] = tiles[n, j, :, R - 1 if up else 0, :]

    def each(act):
        for n, out in enumerate(outs):
            pl.when(py == n)(functools.partial(act, n, out, True))
            pl.when(py != n)(functools.partial(act, n, out, False))

    each(start)
    keep.wait()
    each(fill)


def prepare(dims, many_z, ahead, forward, adj, *rest):
    X, Y, Z = dims
    rest = iter(rest)
    flow_ref, factor = next(rest), next(rest)
    outs = [next(rest) for _ in range(1 + many_z)]
    rising, falling, straight, members_ref, sems = rest
    pz = parity_of("gz")
    part = X // 4
    copies = [
        pltpu.make_async_copy(
            forward.at[:, pl.ds(i * part, part)], members_ref.at[:, pl.ds(i * part, part)], sems.at[i]
        )
        for i in range(4)
    ]
    for c in copies:
        c.start()
    row = lax.broadcasted_iota(jnp.int32, (Y, Z), 0)
    lane = lax.broadcasted_iota(jnp.int32, (Y, Z), 1)
    zero = jnp.zeros((Y, Z), jnp.float32)

    def along_y(q, x):
        here, cy = adj[q, x], velocity[q][1]
        if cy == 0:
            return here
        return jnp.where(row == (Y - 1 if cy > 0 else 0), zero, pltpu.roll(here, (-cy) % Y, 0))

    def both(q, x):
        here, cz = along_y(q, x), velocity[q][2]
        if cz == 0:
            return here
        return jnp.where(lane == (Z - 1 if cz > 0 else 0), zero, pltpu.roll(here, (-cz) % Z, 1))

    for a in range(3):
        rising[a, X] = zero
        falling[a, 1] = zero

    def moments(x, _):
        groups = {}
        for q in range(1, Q):
            groups.setdefault(velocity[q][0], {})[q] = both(q, x)
        level, up, down = moment_of(groups[0]), moment_of(groups[1]), moment_of(groups[-1])
        for a in range(3):
            rising[a, x] = up[a]
            falling[a, x + 2] = down[a]
        for a in range(1, 3):
            straight[a - 1, x] = level[a]
        return 0

    def layer(x, _):
        members = [members_ref[q, x] for q in range(Q)]
        inverse = 1.0 / sum(members[1:], members[0])
        total = None
        for a in range(3):
            terms = [(velocity[q][a], members[q] - members[q + 1]) for q in range(1, Q, 2) if velocity[q][a] != 0]
            vel = signed(terms) * inverse
            flow_ref[a, x] = vel
            moment = rising[a, x + 1] + falling[a, x + 1]
            if a > 0:
                moment = moment + straight[a - 1, x]
            term = vel * (vel - moment)
            total = term if total is None else total + term
        flow_ref[3, x] = inverse
        factor[x] = total
        return 0

    def fill(out, up):
        names = (MINUS if up else PLUS)[2]

        def face(x, _):
            value = zero
            for j, q in enumerate(names):
                slot = slot_of(Z, up, j)
                value = jnp.where(lane == slot, pltpu.roll(along_y(q, x), shift_of(Z, up, j), 1), value)
            out[x] = value
            return 0

        lax.fori_loop(0, X, face, 0, unroll=2)

    lax.fori_loop(0, X, moments, 0, unroll=2)
    for n, out in enumerate(outs):
        pl.when(pz == n)(functools.partial(fill, out, True))
        pl.when(pz != n)(functools.partial(fill, out, False))
    for i, c in enumerate(copies):
        c.wait()
        lax.fori_loop(i * part, (i + 1) * part, layer, 0, unroll=2)


def slot_of(Z, up, j):
    return j if up else Z - 5 + j


def shift_of(Z, up, j):
    return (slot_of(Z, up, j) - (Z - 1 if up else 0)) % Z


def extend_y(dims, pad, own, py, even, odd):
    X, Y, Z = dims
    below, above = sides(py, even, odd)
    pad[:, :R, :] = below
    pad[:, R : R + Y, :] = own
    pad[:, R + Y :, :] = above


def filter_y(dims, pad, store, step=2):
    X, Y, Z = dims
    for x in range(0, X, step):
        store(x, filter_rows(lambda k: pad[x : x + step, k : k + Y, :]))


def design_y(dims, many_y, many_z, design, *rest):
    X, Y, Z = dims
    rest = iter(rest)
    faces = [next(rest) for _ in range(1 + many_z)]
    y_even, y_odd = refs_of(rest, many_y)
    filtered = next(rest)
    outs = [next(rest) for _ in range(1 + many_z)]
    pad, edges = rest
    pz = parity_of("gz")
    py = parity_of("gy")

    def halo(ref):
        return ref[: X * R, :].reshape(X, R, Z)

    extend_y(dims, pad, design[...], py, halo(y_even), None if y_odd is None else halo(y_odd))

    def store(x, value):
        filtered[x : x + value.shape[0]] = value

    filter_y(dims, pad, store)
    row = lax.broadcasted_iota(jnp.int32, (Y, Z), 0)
    lane = lax.broadcasted_iota(jnp.int32, (Y, Z), 1)

    def fill(out, face, up):
        names = (MINUS if up else PLUS)[2]
        slanted = [(j, q) for j, q in enumerate(names) if velocity[q][1] != 0]
        for i, (j, q) in enumerate(slanted):
            edges[i] = pltpu.roll(rows_of(dims, py, y_even, y_odd, q), shift_of(Z, up, j), 1)
        first, last = slot_of(Z, up, 0), slot_of(Z, up, 4)

        def layer(x, _):
            value = jnp.where((lane >= first) & (lane <= last), face[x], filtered[x])
            for i, (j, q) in enumerate(slanted):
                at = (row == (Y - 1 if velocity[q][1] > 0 else 0)) & (lane == slot_of(Z, up, j))
                value = jnp.where(at, edges[i, pl.ds(x, 1), :], value)
            out[x] = value
            return 0

        lax.fori_loop(0, X, layer, 0, unroll=True)

    for n, (out, face) in enumerate(zip(outs, faces)):
        pl.when(pz == n)(functools.partial(fill, out, face, True))
        pl.when(pz != n)(functools.partial(fill, out, face, False))


def rows_of(dims, py, even, odd, q):
    X, Y, Z = dims
    above = velocity[q][1] > 0
    at = X * R + X * (PLUS if above else MINUS)[1].index(q)
    return sides(py, even[at : at + X, :], None if odd is None else odd[at : at + X, :])[int(above)]


def signed(terms):
    total = None
    for sign, value in terms:
        value = value if sign > 0 else -value
        total = value if total is None else total + value
    return total


def moment_of(values):
    return [
        signed([(velocity[q][a], v) for q, v in values.items() if velocity[q][a] != 0]) for a in range(3)
    ]


def halo_z(weights, pz, even, odd):
    value = dot(even, jnp.where(pz == 0, weights[2], weights[1]))
    if odd is not None:
        value = value + dot(odd, jnp.where(pz == 0, weights[1], weights[2]))
    return value


def flat(dims, ref):
    X, Y, Z = dims
    return None if ref is None else ref[...].reshape(X * Y, Z)


def own_z(dims, weights, field, out):
    out[...] = dot(flat(dims, field), weights[0])


def factor_y(dims, many_y, weights, filtered_y, flow_ref, factor, *rest):
    X, Y, Z = dims
    rest = iter(rest)
    y_even, y_odd = refs_of(rest, many_y)
    smooth, out = rest
    smooth[...] = dot(flat(dims, filtered_y), weights[0])
    out[...] = factor[...]
    py = parity_of("gy")
    row = lax.broadcasted_iota(jnp.int32, (X, Z), 0)
    lane = lax.broadcasted_iota(jnp.int32, (X, Z), 1)
    for edge, names in ((0, MINUS[1]), (Y - 1, PLUS[1])):
        values = {}
        for q in names:
            value = rows_of(dims, py, y_even, y_odd, q)
            cx, _, cz = velocity[q]
            if cx != 0:
                value = jnp.where(row == (X - 1 if cx > 0 else 0), 0.0, pltpu.roll(value, (-cx) % X, 0))
            if cz != 0:
                value = jnp.where(lane == (Z - 1 if cz > 0 else 0), 0.0, pltpu.roll(value, (-cz) % Z, 1))
            values[q] = value
        moment = moment_of(values)
        total = factor[:, edge, :]
        for a in range(3):
            total = total - flow_ref[a, :, edge, :] * moment[a]
        out[:, edge, :] = total


def faces_x(dims, out, up, factor, flow_ref, pull):
    X, Y, Z = dims
    names = (MINUS if up else PLUS)[0]
    edge = X - 1 if up else 0
    first = X - R if up else 0
    at = R * Y
    out[:at, :] = factor[first : first + R].reshape(R * Y, Z)
    faces = pull.faces(edge)
    for q in names:
        out[at : at + Y, :] = pull.both(q, edge, faces)
        at += Y
    for a in range(3):
        out[at : at + Y, :] = flow_ref[a, edge]
        at += Y


def pack_halo(dims, pz, refs, out):
    X, Y, Z = dims
    lane = lax.broadcasted_iota(jnp.int32, (Y, Z), 1)
    for n, ref in enumerate(refs):
        value = jnp.zeros((Y, Z), jnp.float32)
        for x in range(X):
            there = (lane >= R * x) & (lane < R * (x + 1))
            value = jnp.where(there, pltpu.roll(ref[x], lanes_x(dims, pz, n, x), 1), value)
        out[(R + 8 + n) * Y : (R + 9 + n) * Y, :] = value


def pack_odd(dims, many_y, many_z, adj, ahead, factor, flow_ref, *rest):
    X, Y, Z = dims
    rest = iter(rest)
    y_even, y_odd = refs_of(rest, many_y)
    z_even, z_odd = refs_of(rest, many_z)
    (out,) = rest
    px = parity_of("gx")
    pz = parity_of("gz")
    out[(R + 8) * Y :, :] = ahead[(R + 8) * Y :, :]
    pull = Pull(adj, dims, parity_of("gy"), y_even, y_odd, pz, z_even, z_odd)
    pl.when(px == 1)(lambda: faces_x(dims, out, True, factor, flow_ref, pull))
    pl.when(px != 1)(lambda: faces_x(dims, out, False, factor, flow_ref, pull))


def pack_x(dims, many_y, many_z, adj, weights, smooth, factor_in, flow_ref, *rest):
    X, Y, Z = dims
    rest = iter(rest)
    y_even, y_odd = refs_of(rest, many_y)
    z_even, z_odd = refs_of(rest, many_z)
    out, whole, factor = rest
    px, py, pz = parity_of("gx"), parity_of("gy"), parity_of("gz")
    value = smooth[...] + halo_z(weights, pz, flat(dims, z_even), flat(dims, z_odd))
    whole[...] = value
    pack_halo(dims, pz, [z_even, z_odd][: 1 + many_z], out)
    lane = lax.broadcasted_iota(jnp.int32, (Y, Z), 1)
    factor[...] = factor_in[...]

    def correct(ref, above):
        names = (PLUS if above else MINUS)[2]
        edge = Z - 1 if above else 0
        zero = jnp.zeros((Y, Z), jnp.float32)

        def layer(x, _):
            values = {}
            for j, q in enumerate(names):
                cx = velocity[q][0]
                face = ref[jnp.clip(x + cx, 0, X - 1)] if cx else ref[x]
                shift = (edge - slot_of(Z, not above, j)) % Z
                face = pltpu.roll(face, shift, 1) if shift else face
                if cx != 0:
                    face = jnp.where(x == (X - 1 if cx > 0 else 0), zero, face)
                values[q] = face
            moment = moment_of(values)
            change = flow_ref[0, x] * moment[0] + flow_ref[1, x] * moment[1] + flow_ref[2, x] * moment[2]
            factor[x] = factor[x] - jnp.where(lane == edge, change, zero)
            return 0

        lax.fori_loop(0, X, layer, 0, unroll=True)

    for n, ref in enumerate([z_even, z_odd][: 1 + many_z]):
        pl.when(pz == n)(functools.partial(correct, ref, True))
        pl.when(pz != n)(functools.partial(correct, ref, False))

    pull = Pull(adj, dims, py, y_even, y_odd, pz, z_even, z_odd)

    pl.when(px == 0)(lambda: faces_x(dims, out, True, factor, flow_ref, pull))
    pl.when(px != 0)(lambda: faces_x(dims, out, False, factor, flow_ref, pull))


def project(filtered):
    base = math.tanh(sharpness * threshold)
    denominator = base + math.tanh(sharpness * (1.0 - threshold))
    inner = jnp.tanh(sharpness * (filtered - threshold))
    physical = (base + inner) * (1.0 / denominator)
    steep = (sharpness / denominator) * (1.0 - inner * inner)
    inverse = 1.0 / (ramp_shape + physical)
    return physical, steep, inverse


def taps_of(X, above, e):
    shift = 2 * R + (X if above else -X) - e
    return [(TAPS[i + shift], i) for i in range(X) if 0 <= i + shift <= 2 * R]


def add_side(dims, base, layers, at, out, above):
    X, Y, Z = dims
    for e in range(X + 2 * R):
        total = base[e]
        for tap, i in taps_of(X, above, e):
            total = total + tap * layers[at + i * Y : at + (i + 1) * Y, :]
        out[e] = total


def lanes_x(dims, pz, n, x):
    Z = dims[2]
    return jnp.where(pz == n, (R * x) % Z, (R * x + R) % Z)


def half_source(dims, above, near, many_z, pz, weights, partial, relayed, factor, flow_ref, own, got, smooth, ext, damp, base, result):
    X, Y, Z = dims
    if near:
        layers = range(2 * R, X + 2 * R) if above else range(X)
    else:
        layers = range(X, X + 2 * R) if above else range(2 * R)
    u_at, v_at, d_at = R * Y, R * Y + 5 * Y, R * Y + 8 * Y
    for e in layers:
        total = partial[e]
        if relayed is not None:
            for tap, i in taps_of(X, above, e):
                total = total + tap * relayed[i * Y : (i + 1) * Y, :]
        smooth[e] = total
        if R <= e < R + X:
            ext[e] = factor[e - R]
        elif got is None:
            ext[e] = jnp.zeros((Y, Z), jnp.float32)
        else:
            at = (e - R - X if above else e) * Y
            ext[e] = got[at : at + Y, :]
    if got is not None:
        lane = lax.broadcasted_iota(jnp.int32, (Y, Z), 1)
        for n in range(1 + many_z):
            above_z = jnp.where(pz == n, 1, 0)
            value = dot(got[d_at + n * Y : d_at + (n + 1) * Y, :], weights[3 + 2 * int(above) + above_z])
            first = (Z - R) * above_z
            there = (lane >= first) & (lane < first + R)
            for i in range(X):
                e = i + X * int(above)
                moved = pltpu.roll(value, lax.rem(first + Z - R * i, Z), 1)
                smooth[e] = smooth[e] + jnp.where(there, moved, 0.0)

        def moment(ref, names):
            return moment_of({q: ref[u_at + j * Y : u_at + (j + 1) * Y, :] for j, q in enumerate(names)})

        def less(e, vel, m):
            ext[e] = ext[e] - (vel[0] * m[0] + vel[1] * m[1] + vel[2] * m[2])

        inner, outer = (R + X - 1, R + X) if above else (R, R - 1)
        there, here = (PLUS[0], MINUS[0]) if above else (MINUS[0], PLUS[0])
        less(inner, [flow_ref[a, inner - R] for a in range(3)], moment(got, there))
        less(outer, [got[v_at + a * Y : v_at + (a + 1) * Y, :] for a in range(3)], moment(own, here))
    slope = -damping_max * ramp_shape * (1.0 + ramp_shape)
    for e in layers:
        physical, steep, inverse = project(smooth[e])
        ext[e] = (slope * steep) * (inverse * inverse) * ext[e]
        if R <= e < R + X:
            damp[e - R] = (2.0 * damping_max * ramp_shape) * (1.0 - physical) * inverse
    for x in range(X):
        terms = [TAPS[e - x] * ext[e] for e in layers if 0 <= e - x <= 2 * R]
        if base is not None:
            terms = [base[x]] + terms
        result[x] = sum(terms[1:], terms[0]) if terms else jnp.zeros((Y, Z), jnp.float32)


def near_x(dims, many_z, weights, partial, factor, flow_ref, own, got, result, damp, smooth, ext):
    px, pz = parity_of("gx"), parity_of("gz")
    for parity in range(2):
        pl.when(px == parity)(
            functools.partial(
                half_source, dims, parity == 0, True, many_z, pz, weights, partial, None, factor, flow_ref,
                own, got, smooth, ext, damp, None, result,
            )
        )


def source(dims, many_x, many_y, many_z, weights, partial, factor, flow_ref, near, near_damp, *rest):
    X, Y, Z = dims
    rest = iter(rest)
    own, got, relayed = (next(rest), next(rest), next(rest)) if many_x else (None, None, None)
    result, damp = next(rest), next(rest)
    outs = [next(rest) for _ in range(1 + many_y)]
    smooth, ext = rest
    px, py, pz = parity_of("gx"), parity_of("gy"), parity_of("gz")
    damp[...] = near_damp[...]
    for parity in range(2):
        pl.when(px == parity)(
            functools.partial(
                half_source, dims, parity == 1, False, many_z, pz, weights, partial, relayed, factor, flow_ref,
                own, got, smooth, ext, damp, near, result,
            )
        )
    for n, out in enumerate(outs):

        @pl.when(py == n)
        def _(out=out):
            out[...] = result[:, Y - R :, :]

        @pl.when(py != n)
        def _(out=out):
            out[...] = result[:, :R, :]


def pack_corner(dims, many_y, many_z, own, *outs):
    X, Y, Z = dims
    outs = iter(outs)
    to_z = [next(outs) for _ in range(1 + many_z)]
    py, pz = parity_of("gy"), parity_of("gz")
    lane = lax.broadcasted_iota(jnp.int32, (Y, Z), 1)
    for n, out in enumerate(to_z):
        value = jnp.zeros((Y, Z), jnp.float32)
        for x in range(X):
            shift = jnp.where(pz == n, (R * x + R) % Z, (R * x) % Z)
            there = (lane >= R * x) & (lane < R * (x + 1))
            value = jnp.where(there, pltpu.roll(own[x], shift, 1), value)
        out[...] = value
    for m in range(1 + many_y):
        for ref in to_z:
            next(outs)[...] = jnp.where(py == m, ref[Y - R :, :], ref[:R, :])


def smooth_yz(dims, many_y, ahead, weights, own, *rest):
    X, Y, Z = dims
    rest = iter(rest)
    rows = [next(rest) for _ in range(1 + many_y)]
    result, pad = rest
    rows = [dot(ref[...].reshape(X * R, Z), weights[0]).reshape(X, R, Z) for ref in rows]
    extend_y(dims, pad, own[...].reshape(X, Y, Z), parity_of("gy"), rows[0], rows[1] if many_y else None)

    def store(x, value):
        result[x : x + value.shape[0]] = value

    filter_y(dims, pad, store)


def add_halo(dims, many_y, many_z, weights, own, *rest):
    X, Y, Z = dims
    rest = iter(rest)
    sides_z = [next(rest) for _ in range(1 + many_z)]
    corners = [[next(rest) for _ in range(1 + many_z)] for _ in range(1 + many_y)]
    out, pad, result, sems = rest
    py, pz = parity_of("gy"), parity_of("gz")
    lane = lax.broadcasted_iota(jnp.int32, (Y, Z), 1)
    moved = []
    for n in range(1 + many_z):
        below, above = sides(py, corners[0][n][...], corners[1][n][...] if many_y else None)
        pad[:R, :] = below
        pad[R : R + Y, :] = sides_z[n][...]
        pad[R + Y :, :] = above
        side = jnp.where(pz == n, 1, 0)
        first = (Z - R) * side
        extra = dot(filter_rows(lambda k: pad[k : k + Y, :]), weights[7 + side])
        moved.append((extra, first, (lane >= first) & (lane < first + R)))
    part = X // 4
    copies = []
    for i in range(4):
        for x in range(i * part, (i + 1) * part):
            value = own[x]
            for extra, first, there in moved:
                value = value + jnp.where(there, pltpu.roll(extra, lax.rem(first + Z - R * x, Z), 1), 0.0)
            result[x] = value
        here = pl.ds(i * part, part)
        copies.append(pltpu.make_async_copy(result.at[here], out.at[here], sems.at[i]))
        copies[-1].start()
    for c in copies:
        c.wait()


def relax(pulled, vel, speed_sq, label, drag, store):
    plus = {q: pulled[q] + pulled[q + 1] for q in range(1, Q, 2)}
    minus = {q: pulled[q] - pulled[q + 1] for q in range(1, Q, 2)}
    axes = (1, 3, 5)
    straight = plus[1] + plus[3] + plus[5]
    slanted = plus[7] + plus[9] + plus[11] + plus[13] + plus[15] + plus[17]
    zeroth = (1.0 / 3.0) * pulled[0] + (1.0 / 18.0) * straight + (1.0 / 36.0) * slanted
    first, diagonal = [], []
    for a in range(3):
        terms = [(velocity[q][a], minus[q]) for q in range(7, Q, 2) if velocity[q][a] != 0]
        first.append((1.0 / 18.0) * minus[axes[a]] + (1.0 / 36.0) * signed(terms))
        both = [(1, plus[q]) for q in range(7, Q, 2) if velocity[q][a] != 0]
        diagonal.append((1.0 / 18.0) * plus[axes[a]] + (1.0 / 36.0) * signed(both))
    xy = (1.0 / 36.0) * (plus[7] - plus[9])
    xz = (1.0 / 36.0) * (plus[11] - plus[13])
    yz = (1.0 / 36.0) * (plus[15] - plus[17])
    turned = [
        diagonal[0] * vel[0] + xy * vel[1] + xz * vel[2],
        xy * vel[0] + diagonal[1] * vel[1] + yz * vel[2],
        xz * vel[0] + yz * vel[1] + diagonal[2] * vel[2],
    ]
    quadric = vel[0] * turned[0] + vel[1] * turned[1] + vel[2] * turned[2]
    eq_scalar = zeroth * (1.0 + 1.5 * speed_sq) - 4.5 * quadric
    eq_vector = [3.0 * first[a] + 9.0 * turned[a] - 3.0 * zeroth * vel[a] for a in range(3)]
    fluid, solid, inlet = label == 0, label == 1, label == 2
    zero = jnp.zeros_like(eq_scalar)
    keep = jnp.where(fluid, 1.0 - relax_rate, zero)
    bounce = jnp.where(solid, 1.0, zero)
    level = relax_rate * eq_scalar
    tilt = [relax_rate * v for v in eq_vector]
    if drag is not None:
        level = level - drag * speed_sq
        tilt = [t + drag * v for t, v in zip(tilt, vel)]
    level = jnp.where(fluid, level, jnp.where(solid, zero, eq_scalar))
    tilt = [jnp.where(fluid, t, jnp.where(inlet, v, zero)) for t, v in zip(tilt, eq_vector)]
    store(0, (keep + bounce) * pulled[0] + level)
    for q in range(1, Q, 2):
        lean = lean_of(q, tilt)
        store(q, keep * pulled[q] + bounce * pulled[q + 1] + (level + lean))
        store(q + 1, keep * pulled[q + 1] + bounce * pulled[q] + (level - lean))


def lean_of(q, vector):
    return signed([(velocity[q][a], vector[a]) for a in range(3) if velocity[q][a] != 0])


def square(vel):
    return vel[0] * vel[0] + vel[1] * vel[1] + vel[2] * vel[2]


def far_x(dims, partial, beyond, out):
    px = parity_of("gx")
    pl.when(px == 0)(lambda: add_side(dims, partial, beyond, 0, out, True))
    pl.when(px != 0)(lambda: add_side(dims, partial, beyond, 0, out, False))


def beside_x(dims, many_y, many_z, adj, flow_ref, mask, own, *rest):
    X, Y, Z = dims
    rest = iter(rest)
    y_even, y_odd = refs_of(rest, many_y)
    z_even, z_odd = refs_of(rest, many_z)
    partial, base = rest
    for e in range(X + 2 * R):
        terms = [(i - e + 2 * R, i * Y) for i in range(X) if 0 <= i - e + 2 * R <= 2 * R]
        partial[e] = sum(TAPS[k] * own[at : at + Y, :] for k, at in terms)
    pull = Pull(adj, dims, parity_of("gy"), y_even, y_odd, parity_of("gz"), z_even, z_odd)

    def layer(x, _):
        around = {c: pull.faces(x + c) for c in (-1, 0, 1)}
        pulled = [pull.both(q, x + velocity[q][0], around[velocity[q][0]]) for q in range(Q)]
        vel = [flow_ref[a, x] for a in range(3)]

        def store(q, value):
            base[q, x] = value

        relax(pulled, vel, square(vel), mask[x], None, store)
        return 0

    lax.fori_loop(1, X - 1, layer, 0)


def collide(dims, many_x, many_y, many_z, step, adj, base, flow_ref, damp, mask, *rest):
    X, Y, Z = dims
    rest = iter(rest)
    y_even, y_odd = refs_of(rest, many_y)
    z_even, z_odd = refs_of(rest, many_z)
    x_even, x_odd = refs_of(rest, many_x)
    target, out, sems = rest
    px, py, pz = parity_of("gx"), parity_of("gy"), parity_of("gz")
    pull = Pull(adj, dims, py, y_even, y_odd, pz, z_even, z_odd)
    u_at = R * Y

    def layer(x):
        vel = [flow_ref[a, x] for a in range(3)]
        drag = jnp.where(mask[x] == 0, damp[x] * flow_ref[3, x], 0.0)
        level = drag * square(vel)
        tilt = [drag * v for v in vel]
        out[0, x] = base[0, x] - level
        for q in range(1, Q, 2):
            lean = lean_of(q, tilt)
            out[q, x] = base[q, x] + (lean - level)
            out[q + 1, x] = base[q + 1, x] - (lean + level)

    def edge(x, toward):
        around = {c: pull.faces(x + c) for c in (0, -toward)}
        pulled = []
        for q in range(Q):
            cx = velocity[q][0]
            if cx == toward:
                at = u_at + Y * (PLUS if cx > 0 else MINUS)[0].index(q)
                both = sides(px, x_even[at : at + Y, :], None if x_odd is None else x_odd[at : at + Y, :])
                pulled.append(both[int(cx > 0)])
            else:
                pulled.append(pull.both(q, x + cx, around[cx]))
        vel = [flow_ref[a, x] for a in range(3)]

        def store(q, value):
            out[q, x] = value

        relax(pulled, vel, square(vel), mask[x], damp[x] * flow_ref[3, x], store)

    last = X // step - 1
    copies = []
    for part in [1, 0, 2, last, *range(3, last)]:
        for x in range(part * step, (part + 1) * step):
            if x == 0:
                edge(x, -1)
            elif x == X - 1:
                edge(x, 1)
            else:
                layer(x)
        here = pl.ds(part * step, step)
        copies.append(pltpu.make_async_copy(out.at[:, here], target.at[:, here], sems.at[part]))
        copies[-1].start()
    for c in copies:
        c.wait()


def local(counts, forward, adjoint, design, mask):
    many_x, many_y, many_z = (int(n > 2) for n in counts)
    nx, ny, nz = counts
    dims = design.shape
    X, Y, Z = dims
    weights = jnp.asarray(np.concatenate([band(Z), packed_band(dims), packed_band_z(dims)]))
    hbm = pl.BlockSpec(memory_space=pltpu.HBM)
    cells = X * Y * Z
    some = lambda pair: [v for v in pair if v is not None]
    pair = lambda items: (items[0], items[1] if len(items) > 1 else None)
    dma = pltpu.SemaphoreType.DMA

    y_rows = X * R + 5 * X
    *to_y, design = call(
        functools.partial(pack_y, dims, many_y),
        [f32(y_rows, Z)] * (1 + many_y) + [f32(X, Y, Z)],
        (in_hbm(adjoint), in_hbm(design)),
        [hbm, hbm],
        [pltpu.VMEM((1 + many_y, 5, X, R, Z), jnp.float32), dma((1 + many_y, 5)), dma],
        limit=4,
        name="pack_y",
    )
    got_y = some(exchange("gy", ny, *pair(to_y)))

    flow_values, factor, *faces = call(
        functools.partial(prepare, dims, many_z),
        [f32(4, X, Y, Z)] + [f32(X, Y, Z)] * (2 + many_z),
        (to_y[0], in_hbm(forward), adjoint),
        vmem(1) + [hbm] + vmem(1),
        [pltpu.VMEM((3, X + 2, Y, Z), jnp.float32)] * 2
        + [pltpu.VMEM((2, X, Y, Z), jnp.float32), pltpu.VMEM((Q, X, Y, Z), jnp.float32), dma((4,))],
        limit=16,
        flops=200 * cells,
        moved=44 * 4 * cells,
        name="prepare",
    )

    filtered_y, *to_z = call(
        functools.partial(design_y, dims, many_y, many_z),
        [f32(X, Y, Z)] * (2 + many_z),
        (design, *faces, *got_y),
        None,
        [pltpu.VMEM((X, Y + 2 * R, Z), jnp.float32), pltpu.VMEM((2, X, Z), jnp.float32)],
        limit=8,
        name="design_y",
    )
    got_z = some(exchange("gz", nz, *pair(to_z)))

    smooth, factor = call(
        functools.partial(factor_y, dims, many_y),
        [f32(X * Y, Z), f32(X, Y, Z)],
        (weights, filtered_y, flow_values, factor, *got_y),
        limit=8,
        flops=200 * cells,
        name="factor_y",
    )
    beyond = swap(smooth, "gx", nx, 0)

    x_rows = R * Y + 8 * Y
    even, smooth, factor = call(
        functools.partial(pack_x, dims, many_y, many_z),
        [f32(x_rows + (1 + many_z) * Y, Z), f32(X * Y, Z), f32(X, Y, Z)],
        (adjoint, weights, smooth, factor, flow_values, *got_y, *got_z),
        limit=16,
        name="pack_x",
    )
    to_x = [even]
    if many_x:
        to_x += call(
            functools.partial(pack_odd, dims, many_y, many_z),
            [f32(x_rows + (1 + many_z) * Y, Z)],
            (adjoint, even, factor, flow_values, *got_y, *got_z),
            limit=16,
            name="pack_odd",
        )
    got_x = some(exchange("gx", nx, *pair(to_x)))

    partial, base = call(
        functools.partial(beside_x, dims, many_y, many_z),
        [f32(X + 2 * R, Y, Z), f32(Q, X, Y, Z)],
        (adjoint, flow_values, mask, smooth, *got_y, *got_z),
        limit=16,
        flops=100000 * cells,
        moved=1000,
        name="beside_x",
    )
    (partial,) = call(
        functools.partial(far_x, dims),
        [f32(X + 2 * R, Y, Z)],
        (partial, beyond),
        limit=8,
        flops=1000,
        moved=1000,
        name="far_x",
    )
    relayed = [relay(beyond, "gx", nx)] if many_x else []

    extended = pltpu.VMEM((X + 2 * R, Y, Z), jnp.float32)
    near, near_damp = call(
        functools.partial(near_x, dims, many_z),
        [f32(X, Y, Z), f32(X, Y, Z)],
        (weights, partial, factor, flow_values, to_x[0], got_x[0]),
        None,
        [extended] * 2,
        limit=8,
        flops=1000,
        moved=1000,
        name="near_x",
    )
    result, damp, *to_y = call(
        functools.partial(source, dims, many_x, many_y, many_z),
        [f32(X, Y, Z), f32(X, Y, Z)] + [f32(X, R, Z)] * (1 + many_y),
        (weights, partial, factor, flow_values, near, near_damp, *to_x[1:], *got_x[1:], *relayed),
        None,
        [extended] * 2,
        limit=8,
        name="source",
    )
    got_y2 = some(exchange("gy", ny, *pair(to_y)))

    step = 2
    (adjoint_next,) = call(
        functools.partial(collide, dims, many_x, many_y, many_z, step),
        [f32(Q, X, Y, Z)],
        (adjoint, base, flow_values, damp, mask, *got_y, *got_z, *got_x),
        None,
        [pltpu.VMEM((Q, X, Y, Z), jnp.float32), dma((X // step,))],
        out_specs=(hbm,),
        limit=8,
        flops=300 * cells,
        moved=44 * 4 * cells,
        name="collide",
    )

    packs = call(
        functools.partial(pack_corner, dims, many_y, many_z),
        [f32(Y, Z)] * (1 + many_z) + [f32(R, Z)] * ((1 + many_y) * (1 + many_z)),
        (result,),
        limit=4,
        flops=1000,
        moved=1000,
        name="pack_corner",
    )
    got_z2 = some(exchange("gz", nz, *pair(packs[: 1 + many_z])))
    corners = [
        swap_corner(packs[(1 + m) * (1 + many_z) + n], (ny, nz), m, n)
        for m in range(1 + many_y)
        for n in range(1 + many_z)
    ]
    (own,) = call(
        functools.partial(own_z, dims),
        [f32(X * Y, Z)],
        (weights, result),
        limit=4,
        flops=1000,
        moved=1000,
        name="own_z",
    )
    (smooth,) = call(
        functools.partial(smooth_yz, dims, many_y),
        [f32(X, Y, Z)],
        (in_hbm(adjoint_next), weights, own, *got_y2),
        [hbm] + vmem(2 + len(got_y2)),
        [pltpu.VMEM((X, Y + 2 * R, Z), jnp.float32)],
        limit=4,
        name="smooth_yz",
    )
    (sensitivity,) = call(
        functools.partial(add_halo, dims, many_y, many_z),
        [f32(X, Y, Z)],
        (weights, smooth, *got_z2, *corners),
        None,
        [pltpu.VMEM((Y + 2 * R, Z), jnp.float32), pltpu.VMEM((X, Y, Z), jnp.float32), dma((4,))],
        out_specs=(hbm,),
        limit=4,
        name="add_halo",
    )
    return adjoint_next, sensitivity


def solution(mesh):
    counts = tuple(mesh.shape[a] for a in ("gx", "gy", "gz"))
    populations, field = P(None, "gx", "gy", "gz"), P("gx", "gy", "gz")
    return jax.shard_map(
        functools.partial(local, counts),
        mesh=mesh,
        in_specs=(populations, populations, field, field),
        out_specs=(populations, field),
        check_vma=False,
    )
```

```python
import functools
import math

import jax
import jax.numpy as jnp
import numpy as np
from jax import lax
from jax.experimental import pallas as pl
from jax.experimental.pallas import tpu as pltpu
from jax.sharding import PartitionSpec as P

Q = 19
R = 8

velocity = [
    (0, 0, 0),
    (1, 0, 0),
    (-1, 0, 0),
    (0, 1, 0),
    (0, -1, 0),
    (0, 0, 1),
    (0, 0, -1),
    (1, 1, 0),
    (-1, -1, 0),
    (1, -1, 0),
    (-1, 1, 0),
    (1, 0, 1),
    (-1, 0, -1),
    (1, 0, -1),
    (-1, 0, 1),
    (0, 1, 1),
    (0, -1, -1),
    (0, 1, -1),
    (0, -1, 1),
]
relax_rate = 1.25
sharpness = 64.0
threshold = 0.5
damping_max = 10.0
ramp_shape = 0.1


def fields_of(axis, sign):
    plus = [q for q in range(Q) if velocity[q][axis] == 1]
    return plus if sign > 0 else [q + 1 if q % 2 else q - 1 for q in plus]


PLUS = [fields_of(a, 1) for a in range(3)]
MINUS = [fields_of(a, -1) for a in range(3)]


def tap_weights():
    spread_width = R / 2.0
    unscaled = [math.exp(-((k - R) ** 2) / (2.0 * spread_width * spread_width)) for k in range(2 * R + 1)]
    summed = sum(unscaled)
    return [v / summed for v in unscaled]


TAPS = tap_weights()


def band(length):
    out = np.zeros((3, length, length), np.float32)
    for i in range(length):
        for k in range(-R, R + 1):
            j = i + k
            if j < 0:
                out[1, j + length, i] = TAPS[k + R]
            elif j >= length:
                out[2, j - length, i] = TAPS[k + R]
            else:
                out[0, j, i] = TAPS[k + R]
    return out


def packed_band(dims):
    X, Y, Z = dims
    out = np.zeros((2, 2, Z, Z), np.float32)
    for above_x in range(2):
        for above_z in range(2):
            for e in range(X):
                for i in range(X):
                    for z in range(R):
                        for j in range(R):
                            kx = i - e + 2 * R * above_x
                            kz = j - z + 2 * R * above_z
                            if 0 <= kx <= 2 * R and 0 <= kz <= 2 * R:
                                out[above_x, above_z, i * R + j, e * R + z] = TAPS[kx] * TAPS[kz]
    return out.reshape(4, Z, Z)


def packed_band_z(dims):
    X, Y, Z = dims
    out = np.zeros((2, Z, Z), np.float32)
    for above in range(2):
        for i in range(X):
            for z in range(R):
                for j in range(R):
                    k = j - z + 2 * R * above
                    if 0 <= k <= 2 * R:
                        out[above, i * R + j, i * R + z] = TAPS[k]
    return out


def sides(parity, even, odd):
    zero = jnp.zeros_like(even)
    if odd is None:
        return jnp.where(parity == 0, zero, even), jnp.where(parity == 0, even, zero)
    return jnp.where(parity == 0, odd, even), jnp.where(parity == 0, even, odd)


def parity_of(axis):
    return lax.rem(lax.axis_index(axis), 2)


def swap(array, axis, count, first):
    pairs = [(i, i + 1) for i in range(first, count - 1, 2)]
    return lax.ppermute(array, axis, pairs + [(b, a) for a, b in pairs])


def relay(array, axis, count):
    pairs = [(i + 2, i) for i in range(1, count - 2, 2)] + [(i - 2, i) for i in range(2, count, 2)]
    return lax.ppermute(array, axis, pairs)


def swap_corner(array, counts, first_y, first_z):
    ny, nz = counts
    pairs = []
    for a in range(first_y, ny - 1, 2):
        for c in range(first_z, nz - 1, 2):
            for d, e in ((c, c + 1), (c + 1, c)):
                pairs += [(a * nz + d, (a + 1) * nz + e), ((a + 1) * nz + e, a * nz + d)]
    return lax.ppermute(array, ("gy", "gz"), pairs)


def exchange(axis, count, even, odd):
    return swap(even, axis, count, 0), (None if odd is None else swap(odd, axis, count, 1))


def vmem(count):
    return [pl.BlockSpec(memory_space=pltpu.VMEM)] * count


def in_hbm(array):
    return pltpu.with_memory_space_constraint(array, pltpu.HBM)


def f32(*shape):
    return jax.ShapeDtypeStruct(shape, jnp.float32)


def call(body, outs, args, specs=None, scratch=(), limit=16, flops=1e6, moved=1e6, **rest):
    return pl.pallas_call(
        body,
        out_shape=outs,
        in_specs=specs or vmem(len(args)),
        out_specs=rest.pop("out_specs", tuple(vmem(len(outs)))),
        scratch_shapes=list(scratch),
        compiler_params=pltpu.CompilerParams(vmem_limit_bytes=limit * 2**20),
        cost_estimate=pl.CostEstimate(flops=int(flops), bytes_accessed=int(moved), transcendentals=0),
        **rest,
    )(*args)


def filter_rows(load):
    total = TAPS[R] * load(R)
    for k in range(R):
        total = total + TAPS[k] * (load(k) + load(2 * R - k))
    return total


def dot(a, b):
    return jnp.dot(a, b, preferred_element_type=jnp.float32, precision=lax.Precision.HIGHEST)


def row_of(ref, at):
    return ref[pl.ds(at, 1), :]


class Pull:
    def __init__(self, adj, dims, py, y_even, y_odd, pz=None, z_even=None, z_odd=None):
        self.adj, self.dims = adj, dims
        self.py, self.y_even, self.y_odd = py, y_even, y_odd
        self.pz, self.z_even, self.z_odd = pz, z_even, z_odd
        X, Y, Z = dims
        self.row = lax.broadcasted_iota(jnp.int32, (Y, Z), 0)
        self.lane = lax.broadcasted_iota(jnp.int32, (Y, Z), 1)

    def along_y(self, q, x):
        X, Y, Z = self.dims
        here = self.adj[q, x]
        cy = velocity[q][1]
        if cy == 0:
            return here
        at = X * R + X * (PLUS if cy > 0 else MINUS)[1].index(q) + x
        even = row_of(self.y_even, at)
        odd = None if self.y_odd is None else row_of(self.y_odd, at)
        below, above = sides(self.py, even, odd)
        if cy > 0:
            return jnp.where(self.row == Y - 1, above, pltpu.roll(here, Y - 1, 0))
        return jnp.where(self.row == 0, below, pltpu.roll(here, 1, 0))

    def faces(self, x):
        even = self.z_even[x]
        odd = None if self.z_odd is None else self.z_odd[x]
        return sides(self.pz, even, odd)

    def both(self, q, x, faces):
        X, Y, Z = self.dims
        here = self.along_y(q, x)
        cz = velocity[q][2]
        if cz == 0:
            return here
        below, above = faces
        if cz > 0:
            j = PLUS[2].index(q)
            face = pltpu.roll(above, 4 - j, 1) if j != 4 else above
            return jnp.where(self.lane == Z - 1, face, pltpu.roll(here, Z - 1, 1))
        j = MINUS[2].index(q)
        face = pltpu.roll(below, Z - j, 1) if j else below
        return jnp.where(self.lane == 0, face, pltpu.roll(here, 1, 1))


def refs_of(refs, odd):
    even = next(refs)
    return even, (next(refs) if odd else None)


def pack_y(dims, many, adj, design, *rest):
    X, Y, Z = dims
    outs = rest[: 1 + many]
    kept, tiles, sems, kept_sem = rest[1 + many :]
    py = parity_of("gy")
    keep = pltpu.make_async_copy(design, kept, kept_sem)
    keep.start()

    def copies(n, up):
        names = (MINUS if up else PLUS)[1]
        first = Y - R if up else 0
        return [
            pltpu.make_async_copy(adj.at[q, :, pl.ds(first, R), :], tiles.at[n, j], sems.at[n, j])
            for j, q in enumerate(names)
        ]

    def start(n, out, up):
        for c in copies(n, up):
            c.start()

    def fill(n, out, up):
        first = Y - R if up else 0
        out[: X * R, :] = kept[:, first : first + R, :].reshape(X * R, Z)
        for c in copies(n, up):
            c.wait()
        for j in range(5):
            out[X * R + X * j : X * R + X * (j + 1), :] = tiles[n, j, :, R - 1 if up else 0, :]

    def each(act):
        for n, out in enumerate(outs):
            pl.when(py == n)(functools.partial(act, n, out, True))
            pl.when(py != n)(functools.partial(act, n, out, False))

    each(start)
    keep.wait()
    each(fill)


def prepare(dims, many_z, ahead, forward, adj, *rest):
    X, Y, Z = dims
    rest = iter(rest)
    flow_ref, factor = next(rest), next(rest)
    outs = [next(rest) for _ in range(1 + many_z)]
    rising, falling, straight, members_ref, sems = rest
    pz = parity_of("gz")
    part = X // 4
    copies = [
        pltpu.make_async_copy(
            forward.at[:, pl.ds(i * part, part)], members_ref.at[:, pl.ds(i * part, part)], sems.at[i]
        )
        for i in range(4)
    ]
    for c in copies:
        c.start()
    row = lax.broadcasted_iota(jnp.int32, (Y, Z), 0)
    lane = lax.broadcasted_iota(jnp.int32, (Y, Z), 1)
    zero = jnp.zeros((Y, Z), jnp.float32)

    def along_y(q, x):
        here, cy = adj[q, x], velocity[q][1]
        if cy == 0:
            return here
        return jnp.where(row == (Y - 1 if cy > 0 else 0), zero, pltpu.roll(here, (-cy) % Y, 0))

    def both(q, x):
        here, cz = along_y(q, x), velocity[q][2]
        if cz == 0:
            return here
        return jnp.where(lane == (Z - 1 if cz > 0 else 0), zero, pltpu.roll(here, (-cz) % Z, 1))

    for a in range(3):
        rising[a, X] = zero
        falling[a, 1] = zero

    def moments(x, _):
        groups = {}
        for q in range(1, Q):
            groups.setdefault(velocity[q][0], {})[q] = both(q, x)
        level, up, down = moment_of(groups[0]), moment_of(groups[1]), moment_of(groups[-1])
        for a in range(3):
            rising[a, x] = up[a]
            falling[a, x + 2] = down[a]
        for a in range(1, 3):
            straight[a - 1, x] = level[a]
        return 0

    def layer(x, _):
        members = [members_ref[q, x] for q in range(Q)]
        inverse = 1.0 / sum(members[1:], members[0])
        total = None
        for a in range(3):
            terms = [(velocity[q][a], members[q] - members[q + 1]) for q in range(1, Q, 2) if velocity[q][a] != 0]
            vel = signed(terms) * inverse
            flow_ref[a, x] = vel
            moment = rising[a, x + 1] + falling[a, x + 1]
            if a > 0:
                moment = moment + straight[a - 1, x]
            term = vel * (vel - moment)
            total = term if total is None else total + term
        flow_ref[3, x] = inverse
        factor[x] = total
        return 0

    def fill(out, up):
        names = (MINUS if up else PLUS)[2]

        def face(x, _):
            value = zero
            for j, q in enumerate(names):
                slot = slot_of(Z, up, j)
                value = jnp.where(lane == slot, pltpu.roll(along_y(q, x), shift_of(Z, up, j), 1), value)
            out[x] = value
            return 0

        lax.fori_loop(0, X, face, 0, unroll=2)

    lax.fori_loop(0, X, moments, 0, unroll=2)
    for n, out in enumerate(outs):
        pl.when(pz == n)(functools.partial(fill, out, True))
        pl.when(pz != n)(functools.partial(fill, out, False))
    for i, c in enumerate(copies):
        c.wait()
        lax.fori_loop(i * part, (i + 1) * part, layer, 0, unroll=2)


def slot_of(Z, up, j):
    return j if up else Z - 5 + j


def shift_of(Z, up, j):
    return (slot_of(Z, up, j) - (Z - 1 if up else 0)) % Z


def extend_y(dims, pad, own, py, even, odd):
    X, Y, Z = dims
    below, above = sides(py, even, odd)
    pad[:, :R, :] = below
    pad[:, R : R + Y, :] = own
    pad[:, R + Y :, :] = above


def filter_y(dims, pad, store, step=2):
    X, Y, Z = dims
    for x in range(0, X, step):
        store(x, filter_rows(lambda k: pad[x : x + step, k : k + Y, :]))


def design_y(dims, many_y, many_z, design, *rest):
    X, Y, Z = dims
    rest = iter(rest)
    faces = [next(rest) for _ in range(1 + many_z)]
    y_even, y_odd = refs_of(rest, many_y)
    filtered = next(rest)
    outs = [next(rest) for _ in range(1 + many_z)]
    pad, edges = rest
    pz = parity_of("gz")
    py = parity_of("gy")

    def halo(ref):
        return ref[: X * R, :].reshape(X, R, Z)

    extend_y(dims, pad, design[...], py, halo(y_even), None if y_odd is None else halo(y_odd))

    def store(x, value):
        filtered[x : x + value.shape[0]] = value

    filter_y(dims, pad, store)
    row = lax.broadcasted_iota(jnp.int32, (Y, Z), 0)
    lane = lax.broadcasted_iota(jnp.int32, (Y, Z), 1)

    def fill(out, face, up):
        names = (MINUS if up else PLUS)[2]
        slanted = [(j, q) for j, q in enumerate(names) if velocity[q][1] != 0]
        for i, (j, q) in enumerate(slanted):
            edges[i] = pltpu.roll(rows_of(dims, py, y_even, y_odd, q), shift_of(Z, up, j), 1)
        first, last = slot_of(Z, up, 0), slot_of(Z, up, 4)

        def layer(x, _):
            value = jnp.where((lane >= first) & (lane <= last), face[x], filtered[x])
            for i, (j, q) in enumerate(slanted):
                at = (row == (Y - 1 if velocity[q][1] > 0 else 0)) & (lane == slot_of(Z, up, j))
                value = jnp.where(at, edges[i, pl.ds(x, 1), :], value)
            out[x] = value
            return 0

        lax.fori_loop(0, X, layer, 0, unroll=True)

    for n, (out, face) in enumerate(zip(outs, faces)):
        pl.when(pz == n)(functools.partial(fill, out, face, True))
        pl.when(pz != n)(functools.partial(fill, out, face, False))


def rows_of(dims, py, even, odd, q):
    X, Y, Z = dims
    above = velocity[q][1] > 0
    at = X * R + X * (PLUS if above else MINUS)[1].index(q)
    return sides(py, even[at : at + X, :], None if odd is None else odd[at : at + X, :])[int(above)]


def signed(terms):
    total = None
    for sign, value in terms:
        value = value if sign > 0 else -value
        total = value if total is None else total + value
    return total


def moment_of(values):
    return [
        signed([(velocity[q][a], v) for q, v in values.items() if velocity[q][a] != 0]) for a in range(3)
    ]


def halo_z(weights, pz, even, odd):
    value = dot(even, jnp.where(pz == 0, weights[2], weights[1]))
    if odd is not None:
        value = value + dot(odd, jnp.where(pz == 0, weights[1], weights[2]))
    return value


def flat(dims, ref):
    X, Y, Z = dims
    return None if ref is None else ref[...].reshape(X * Y, Z)


def own_z(dims, weights, field, out):
    out[...] = dot(flat(dims, field), weights[0])


def factor_y(dims, many_y, weights, filtered_y, flow_ref, factor, *rest):
    X, Y, Z = dims
    rest = iter(rest)
    y_even, y_odd = refs_of(rest, many_y)
    smooth, out = rest
    smooth[...] = dot(flat(dims, filtered_y), weights[0])
    out[...] = factor[...]
    py = parity_of("gy")
    row = lax.broadcasted_iota(jnp.int32, (X, Z), 0)
    lane = lax.broadcasted_iota(jnp.int32, (X, Z), 1)
    for edge, names in ((0, MINUS[1]), (Y - 1, PLUS[1])):
        values = {}
        for q in names:
            value = rows_of(dims, py, y_even, y_odd, q)
            cx, _, cz = velocity[q]
            if cx != 0:
                value = jnp.where(row == (X - 1 if cx > 0 else 0), 0.0, pltpu.roll(value, (-cx) % X, 0))
            if cz != 0:
                value = jnp.where(lane == (Z - 1 if cz > 0 else 0), 0.0, pltpu.roll(value, (-cz) % Z, 1))
            values[q] = value
        moment = moment_of(values)
        total = factor[:, edge, :]
        for a in range(3):
            total = total - flow_ref[a, :, edge, :] * moment[a]
        out[:, edge, :] = total


def faces_x(dims, out, up, factor, flow_ref, pull):
    X, Y, Z = dims
    names = (MINUS if up else PLUS)[0]
    edge = X - 1 if up else 0
    first = X - R if up else 0
    at = R * Y
    out[:at, :] = factor[first : first + R].reshape(R * Y, Z)
    faces = pull.faces(edge)
    for q in names:
        out[at : at + Y, :] = pull.both(q, edge, faces)
        at += Y
    for a in range(3):
        out[at : at + Y, :] = flow_ref[a, edge]
        at += Y


def pack_halo(dims, pz, refs, out):
    X, Y, Z = dims
    lane = lax.broadcasted_iota(jnp.int32, (Y, Z), 1)
    for n, ref in enumerate(refs):
        value = jnp.zeros((Y, Z), jnp.float32)
        for x in range(X):
            there = (lane >= R * x) & (lane < R * (x + 1))
            value = jnp.where(there, pltpu.roll(ref[x], lanes_x(dims, pz, n, x), 1), value)
        out[(R + 8 + n) * Y : (R + 9 + n) * Y, :] = value


def pack_odd(dims, many_y, many_z, adj, ahead, factor, flow_ref, *rest):
    X, Y, Z = dims
    rest = iter(rest)
    y_even, y_odd = refs_of(rest, many_y)
    z_even, z_odd = refs_of(rest, many_z)
    (out,) = rest
    px = parity_of("gx")
    pz = parity_of("gz")
    out[(R + 8) * Y :, :] = ahead[(R + 8) * Y :, :]
    pull = Pull(adj, dims, parity_of("gy"), y_even, y_odd, pz, z_even, z_odd)
    pl.when(px == 1)(lambda: faces_x(dims, out, True, factor, flow_ref, pull))
    pl.when(px != 1)(lambda: faces_x(dims, out, False, factor, flow_ref, pull))


def pack_x(dims, many_y, many_z, adj, factor_in, flow_ref, *rest):
    X, Y, Z = dims
    rest = iter(rest)
    y_even, y_odd = refs_of(rest, many_y)
    z_even, z_odd = refs_of(rest, many_z)
    out, factor = rest
    px, py, pz = parity_of("gx"), parity_of("gy"), parity_of("gz")
    pack_halo(dims, pz, [z_even, z_odd][: 1 + many_z], out)
    lane = lax.broadcasted_iota(jnp.int32, (Y, Z), 1)
    factor[...] = factor_in[...]

    def correct(ref, above):
        names = (PLUS if above else MINUS)[2]
        edge = Z - 1 if above else 0
        zero = jnp.zeros((Y, Z), jnp.float32)

        def layer(x, _):
            values = {}
            for j, q in enumerate(names):
                cx = velocity[q][0]
                face = ref[jnp.clip(x + cx, 0, X - 1)] if cx else ref[x]
                shift = (edge - slot_of(Z, not above, j)) % Z
                face = pltpu.roll(face, shift, 1) if shift else face
                if cx != 0:
                    face = jnp.where(x == (X - 1 if cx > 0 else 0), zero, face)
                values[q] = face
            moment = moment_of(values)
            change = flow_ref[0, x] * moment[0] + flow_ref[1, x] * moment[1] + flow_ref[2, x] * moment[2]
            factor[x] = factor[x] - jnp.where(lane == edge, change, zero)
            return 0

        lax.fori_loop(0, X, layer, 0, unroll=True)

    for n, ref in enumerate([z_even, z_odd][: 1 + many_z]):
        pl.when(pz == n)(functools.partial(correct, ref, True))
        pl.when(pz != n)(functools.partial(correct, ref, False))

    pull = Pull(adj, dims, py, y_even, y_odd, pz, z_even, z_odd)

    pl.when(px == 0)(lambda: faces_x(dims, out, True, factor, flow_ref, pull))
    pl.when(px != 0)(lambda: faces_x(dims, out, False, factor, flow_ref, pull))


def project(filtered):
    base = math.tanh(sharpness * threshold)
    denominator = base + math.tanh(sharpness * (1.0 - threshold))
    inner = jnp.tanh(sharpness * (filtered - threshold))
    physical = (base + inner) * (1.0 / denominator)
    steep = (sharpness / denominator) * (1.0 - inner * inner)
    inverse = 1.0 / (ramp_shape + physical)
    return physical, steep, inverse


def taps_of(X, above, e):
    shift = 2 * R + (X if above else -X) - e
    return [(TAPS[i + shift], i) for i in range(X) if 0 <= i + shift <= 2 * R]


def add_side(dims, base, layers, at, out, above):
    X, Y, Z = dims
    for e in range(X + 2 * R):
        total = base[e]
        for tap, i in taps_of(X, above, e):
            total = total + tap * layers[at + i * Y : at + (i + 1) * Y, :]
        out[e] = total


def lanes_x(dims, pz, n, x):
    Z = dims[2]
    return jnp.where(pz == n, (R * x) % Z, (R * x + R) % Z)


def layers_toward(dims, above, near):
    X = dims[0]
    if near:
        return range(2 * R, X + 2 * R) if above else range(X)
    return range(X, X + 2 * R) if above else range(2 * R)


def complete(dims, above, layers, many_z, pz, weights, partial, factor, flow_ref, own, got, smooth, ext):
    X, Y, Z = dims
    u_at, v_at, d_at = R * Y, R * Y + 5 * Y, R * Y + 8 * Y
    for e in layers:
        smooth[e] = partial[e]
        if R <= e < R + X:
            ext[e] = factor[e - R]
        elif got is None:
            ext[e] = jnp.zeros((Y, Z), jnp.float32)
        else:
            at = (e - R - X if above else e) * Y
            ext[e] = got[at : at + Y, :]
    if got is None:
        return
    lane = lax.broadcasted_iota(jnp.int32, (Y, Z), 1)
    for n in range(1 + many_z):
        above_z = jnp.where(pz == n, 1, 0)
        value = dot(got[d_at + n * Y : d_at + (n + 1) * Y, :], weights[3 + 2 * int(above) + above_z])
        first = (Z - R) * above_z
        there = (lane >= first) & (lane < first + R)
        for i in range(X):
            e = i + X * int(above)
            moved = pltpu.roll(value, lax.rem(first + Z - R * i, Z), 1)
            smooth[e] = smooth[e] + jnp.where(there, moved, 0.0)

    def moment(ref, names):
        return moment_of({q: ref[u_at + j * Y : u_at + (j + 1) * Y, :] for j, q in enumerate(names)})

    def less(e, vel, m):
        ext[e] = ext[e] - (vel[0] * m[0] + vel[1] * m[1] + vel[2] * m[2])

    inner, outer = (R + X - 1, R + X) if above else (R, R - 1)
    there, here = (PLUS[0], MINUS[0]) if above else (MINUS[0], PLUS[0])
    less(inner, [flow_ref[a, inner - R] for a in range(3)], moment(got, there))
    less(outer, [got[v_at + a * Y : v_at + (a + 1) * Y, :] for a in range(3)], moment(own, here))


def half_source(dims, above, layers, smooth, relayed, ext, new, damp, base, result):
    X, Y, Z = dims
    slope = -damping_max * ramp_shape * (1.0 + ramp_shape)
    for e in layers:
        total = smooth[e]
        if relayed is not None:
            for tap, i in taps_of(X, above, e):
                total = total + tap * relayed[i * Y : (i + 1) * Y, :]
        physical, steep, inverse = project(total)
        new[e] = (slope * steep) * (inverse * inverse) * ext[e]
        if R <= e < R + X:
            damp[e - R] = (2.0 * damping_max * ramp_shape) * (1.0 - physical) * inverse
    for x in range(X):
        terms = [TAPS[e - x] * new[e] for e in layers if 0 <= e - x <= 2 * R]
        if base is not None:
            terms = [base[x]] + terms
        result[x] = sum(terms[1:], terms[0]) if terms else jnp.zeros((Y, Z), jnp.float32)


def near_x(dims, many_z, weights, partial, factor, flow_ref, own, got, result, damp, smooth, ext):
    px, pz = parity_of("gx"), parity_of("gz")

    def act(above):
        layers = layers_toward(dims, above, True)
        complete(dims, above, layers, many_z, pz, weights, partial, factor, flow_ref, own, got, smooth, ext)
        half_source(dims, above, layers, smooth, None, ext, ext, damp, None, result)

    pl.when(px == 0)(lambda: act(True))
    pl.when(px != 0)(lambda: act(False))


def far_ready(dims, many_x, many_z, ahead, weights, partial, factor, flow_ref, *rest):
    own, got = rest[:2] if many_x else (None, None)
    smooth, ext = rest[-2:]
    px, pz = parity_of("gx"), parity_of("gz")

    def act(above):
        layers = layers_toward(dims, above, False)
        complete(dims, above, layers, many_z, pz, weights, partial, factor, flow_ref, own, got, smooth, ext)

    pl.when(px == 1)(lambda: act(True))
    pl.when(px != 1)(lambda: act(False))


def source(dims, many_x, many_y, many_z, smooth, ext, near, near_damp, *rest):
    X, Y, Z = dims
    rest = iter(rest)
    relayed = next(rest) if many_x else None
    result, damp = next(rest), next(rest)
    rows = [next(rest) for _ in range(1 + many_y)]
    to_z = [next(rest) for _ in range(1 + many_z)]
    corners = [[next(rest) for _ in range(1 + many_z)] for _ in range(1 + many_y)]
    (new,) = rest
    px, py, pz = parity_of("gx"), parity_of("gy"), parity_of("gz")
    damp[...] = near_damp[...]

    def act(above):
        layers = layers_toward(dims, above, False)
        half_source(dims, above, layers, smooth, relayed, ext, new, damp, near, result)

    pl.when(px == 1)(lambda: act(True))
    pl.when(px != 1)(lambda: act(False))
    for n, out in enumerate(rows):

        @pl.when(py == n)
        def _(out=out):
            out[...] = result[:, Y - R :, :]

        @pl.when(py != n)
        def _(out=out):
            out[...] = result[:, :R, :]

    pack_corner(dims, py, pz, result, to_z, corners)


def pack_corner(dims, py, pz, own, to_z, corners):
    X, Y, Z = dims
    lane = lax.broadcasted_iota(jnp.int32, (Y, Z), 1)
    for n, out in enumerate(to_z):
        value = jnp.zeros((Y, Z), jnp.float32)
        for x in range(X):
            shift = jnp.where(pz == n, (R * x + R) % Z, (R * x) % Z)
            there = (lane >= R * x) & (lane < R * (x + 1))
            value = jnp.where(there, pltpu.roll(own[x], shift, 1), value)
        out[...] = value
        for m, row in enumerate(corners):
            row[n][...] = jnp.where(py == m, value[Y - R :], value[:R])


def smooth_yz(dims, many_y, ahead, weights, own, *rest):
    X, Y, Z = dims
    rest = iter(rest)
    rows = [next(rest) for _ in range(1 + many_y)]
    result, pad = rest
    rows = [dot(ref[...].reshape(X * R, Z), weights[0]).reshape(X, R, Z) for ref in rows]
    extend_y(dims, pad, own[...].reshape(X, Y, Z), parity_of("gy"), rows[0], rows[1] if many_y else None)

    def store(x, value):
        result[x : x + value.shape[0]] = value

    filter_y(dims, pad, store)


def add_halo(dims, many_y, many_z, weights, own, *rest):
    X, Y, Z = dims
    rest = iter(rest)
    sides_z = [next(rest) for _ in range(1 + many_z)]
    corners = [[next(rest) for _ in range(1 + many_z)] for _ in range(1 + many_y)]
    out, pad, result, sems = rest
    py, pz = parity_of("gy"), parity_of("gz")
    lane = lax.broadcasted_iota(jnp.int32, (Y, Z), 1)
    moved = []
    for n in range(1 + many_z):
        below, above = sides(py, corners[0][n][...], corners[1][n][...] if many_y else None)
        pad[:R, :] = below
        pad[R : R + Y, :] = sides_z[n][...]
        pad[R + Y :, :] = above
        side = jnp.where(pz == n, 1, 0)
        first = (Z - R) * side
        extra = dot(filter_rows(lambda k: pad[k : k + Y, :]), weights[7 + side])
        moved.append((extra, first, (lane >= first) & (lane < first + R)))
    part = X // 4
    copies = []
    for i in range(4):
        for x in range(i * part, (i + 1) * part):
            value = own[x]
            for extra, first, there in moved:
                value = value + jnp.where(there, pltpu.roll(extra, lax.rem(first + Z - R * x, Z), 1), 0.0)
            result[x] = value
        here = pl.ds(i * part, part)
        copies.append(pltpu.make_async_copy(result.at[here], out.at[here], sems.at[i]))
        copies[-1].start()
    for c in copies:
        c.wait()


def relax(pulled, vel, speed_sq, label, drag, store):
    plus = {q: pulled[q] + pulled[q + 1] for q in range(1, Q, 2)}
    minus = {q: pulled[q] - pulled[q + 1] for q in range(1, Q, 2)}
    axes = (1, 3, 5)
    straight = plus[1] + plus[3] + plus[5]
    slanted = plus[7] + plus[9] + plus[11] + plus[13] + plus[15] + plus[17]
    zeroth = (1.0 / 3.0) * pulled[0] + (1.0 / 18.0) * straight + (1.0 / 36.0) * slanted
    first, diagonal = [], []
    for a in range(3):
        terms = [(velocity[q][a], minus[q]) for q in range(7, Q, 2) if velocity[q][a] != 0]
        first.append((1.0 / 18.0) * minus[axes[a]] + (1.0 / 36.0) * signed(terms))
        both = [(1, plus[q]) for q in range(7, Q, 2) if velocity[q][a] != 0]
        diagonal.append((1.0 / 18.0) * plus[axes[a]] + (1.0 / 36.0) * signed(both))
    xy = (1.0 / 36.0) * (plus[7] - plus[9])
    xz = (1.0 / 36.0) * (plus[11] - plus[13])
    yz = (1.0 / 36.0) * (plus[15] - plus[17])
    turned = [
        diagonal[0] * vel[0] + xy * vel[1] + xz * vel[2],
        xy * vel[0] + diagonal[1] * vel[1] + yz * vel[2],
        xz * vel[0] + yz * vel[1] + diagonal[2] * vel[2],
    ]
    quadric = vel[0] * turned[0] + vel[1] * turned[1] + vel[2] * turned[2]
    eq_scalar = zeroth * (1.0 + 1.5 * speed_sq) - 4.5 * quadric
    eq_vector = [3.0 * first[a] + 9.0 * turned[a] - 3.0 * zeroth * vel[a] for a in range(3)]
    fluid, solid, inlet = label == 0, label == 1, label == 2
    zero = jnp.zeros_like(eq_scalar)
    keep = jnp.where(fluid, 1.0 - relax_rate, zero)
    bounce = jnp.where(solid, 1.0, zero)
    level = relax_rate * eq_scalar
    tilt = [relax_rate * v for v in eq_vector]
    if drag is not None:
        level = level - drag * speed_sq
        tilt = [t + drag * v for t, v in zip(tilt, vel)]
    level = jnp.where(fluid, level, jnp.where(solid, zero, eq_scalar))
    tilt = [jnp.where(fluid, t, jnp.where(inlet, v, zero)) for t, v in zip(tilt, eq_vector)]
    store(0, (keep + bounce) * pulled[0] + level)
    for q in range(1, Q, 2):
        lean = lean_of(q, tilt)
        store(q, keep * pulled[q] + bounce * pulled[q + 1] + (level + lean))
        store(q + 1, keep * pulled[q + 1] + bounce * pulled[q] + (level - lean))


def lean_of(q, vector):
    return signed([(velocity[q][a], vector[a]) for a in range(3) if velocity[q][a] != 0])


def square(vel):
    return vel[0] * vel[0] + vel[1] * vel[1] + vel[2] * vel[2]


def far_x(dims, partial, beyond, out):
    px = parity_of("gx")
    pl.when(px == 0)(lambda: add_side(dims, partial, beyond, 0, out, True))
    pl.when(px != 0)(lambda: add_side(dims, partial, beyond, 0, out, False))


def beside_x(dims, many_y, many_z, ahead, weights, adj, flow_ref, mask, smooth, *rest):
    X, Y, Z = dims
    rest = iter(rest)
    y_even, y_odd = refs_of(rest, many_y)
    z_even, z_odd = refs_of(rest, many_z)
    partial, base, own = rest
    own[...] = smooth[...] + halo_z(weights, parity_of("gz"), flat(dims, z_even), flat(dims, z_odd))
    for e in range(X + 2 * R):
        terms = [(i - e + 2 * R, i * Y) for i in range(X) if 0 <= i - e + 2 * R <= 2 * R]
        partial[e] = sum(TAPS[k] * own[at : at + Y, :] for k, at in terms)
    pull = Pull(adj, dims, parity_of("gy"), y_even, y_odd, parity_of("gz"), z_even, z_odd)

    def layer(x, _):
        around = {c: pull.faces(x + c) for c in (-1, 0, 1)}
        pulled = [pull.both(q, x + velocity[q][0], around[velocity[q][0]]) for q in range(Q)]
        vel = [flow_ref[a, x] for a in range(3)]

        def store(q, value):
            base[q, x] = value

        relax(pulled, vel, square(vel), mask[x], None, store)
        return 0

    lax.fori_loop(1, X - 1, layer, 0, unroll=7)


def collide(dims, many_x, many_y, many_z, step, adj, base, flow_ref, damp, mask, *rest):
    X, Y, Z = dims
    rest = iter(rest)
    y_even, y_odd = refs_of(rest, many_y)
    z_even, z_odd = refs_of(rest, many_z)
    x_even, x_odd = refs_of(rest, many_x)
    target, out, sems = rest
    px, py, pz = parity_of("gx"), parity_of("gy"), parity_of("gz")
    pull = Pull(adj, dims, py, y_even, y_odd, pz, z_even, z_odd)
    u_at = R * Y

    def layer(x):
        vel = [flow_ref[a, x] for a in range(3)]
        drag = jnp.where(mask[x] == 0, damp[x] * flow_ref[3, x], 0.0)
        level = drag * square(vel)
        tilt = [drag * v for v in vel]
        out[0, x] = base[0, x] - level
        for q in range(1, Q, 2):
            lean = lean_of(q, tilt)
            out[q, x] = base[q, x] + (lean - level)
            out[q + 1, x] = base[q + 1, x] - (lean + level)

    def edge(x, toward):
        around = {c: pull.faces(x + c) for c in (0, -toward)}
        pulled = []
        for q in range(Q):
            cx = velocity[q][0]
            if cx == toward:
                at = u_at + Y * (PLUS if cx > 0 else MINUS)[0].index(q)
                both = sides(px, x_even[at : at + Y, :], None if x_odd is None else x_odd[at : at + Y, :])
                pulled.append(both[int(cx > 0)])
            else:
                pulled.append(pull.both(q, x + cx, around[cx]))
        vel = [flow_ref[a, x] for a in range(3)]

        def store(q, value):
            out[q, x] = value

        relax(pulled, vel, square(vel), mask[x], damp[x] * flow_ref[3, x], store)

    last = X // step - 1
    copies = []
    for part in [1, 0, 2, last, *range(3, last)]:
        for x in range(part * step, (part + 1) * step):
            if x == 0:
                edge(x, -1)
            elif x == X - 1:
                edge(x, 1)
            else:
                layer(x)
        here = pl.ds(part * step, step)
        copies.append(pltpu.make_async_copy(out.at[:, here], target.at[:, here], sems.at[part]))
        copies[-1].start()
    for c in copies:
        c.wait()


def local(counts, forward, adjoint, design, mask):
    many_x, many_y, many_z = (int(n > 2) for n in counts)
    nx, ny, nz = counts
    dims = design.shape
    X, Y, Z = dims
    weights = jnp.asarray(np.concatenate([band(Z), packed_band(dims), packed_band_z(dims)]))
    hbm = pl.BlockSpec(memory_space=pltpu.HBM)
    cells = X * Y * Z
    some = lambda pair: [v for v in pair if v is not None]
    pair = lambda items: (items[0], items[1] if len(items) > 1 else None)
    dma = pltpu.SemaphoreType.DMA

    y_rows = X * R + 5 * X
    *to_y, design = call(
        functools.partial(pack_y, dims, many_y),
        [f32(y_rows, Z)] * (1 + many_y) + [f32(X, Y, Z)],
        (in_hbm(adjoint), in_hbm(design)),
        [hbm, hbm],
        [pltpu.VMEM((1 + many_y, 5, X, R, Z), jnp.float32), dma((1 + many_y, 5)), dma],
        limit=4,
        name="pack_y",
    )
    got_y = some(exchange("gy", ny, *pair(to_y)))

    flow_values, factor, *faces = call(
        functools.partial(prepare, dims, many_z),
        [f32(4, X, Y, Z)] + [f32(X, Y, Z)] * (2 + many_z),
        (to_y[0], in_hbm(forward), adjoint),
        vmem(1) + [hbm] + vmem(1),
        [pltpu.VMEM((3, X + 2, Y, Z), jnp.float32)] * 2
        + [pltpu.VMEM((2, X, Y, Z), jnp.float32), pltpu.VMEM((Q, X, Y, Z), jnp.float32), dma((4,))],
        limit=16,
        flops=200 * cells,
        moved=44 * 4 * cells,
        name="prepare",
    )

    filtered_y, *to_z = call(
        functools.partial(design_y, dims, many_y, many_z),
        [f32(X, Y, Z)] * (2 + many_z),
        (design, *faces, *got_y),
        None,
        [pltpu.VMEM((X, Y + 2 * R, Z), jnp.float32), pltpu.VMEM((2, X, Z), jnp.float32)],
        limit=8,
        name="design_y",
    )
    got_z = some(exchange("gz", nz, *pair(to_z)))

    smooth, factor = call(
        functools.partial(factor_y, dims, many_y),
        [f32(X * Y, Z), f32(X, Y, Z)],
        (weights, filtered_y, flow_values, factor, *got_y),
        limit=8,
        flops=200 * cells,
        name="factor_y",
    )
    beyond = swap(smooth, "gx", nx, 0)

    x_rows = R * Y + 8 * Y
    even, factor = call(
        functools.partial(pack_x, dims, many_y, many_z),
        [f32(x_rows + (1 + many_z) * Y, Z), f32(X, Y, Z)],
        (adjoint, factor, flow_values, *got_y, *got_z),
        limit=16,
        name="pack_x",
    )
    to_x = [even]
    if many_x:
        to_x += call(
            functools.partial(pack_odd, dims, many_y, many_z),
            [f32(x_rows + (1 + many_z) * Y, Z)],
            (adjoint, even, factor, flow_values, *got_y, *got_z),
            limit=16,
            name="pack_odd",
        )
    got_x = some(exchange("gx", nx, *pair(to_x)))

    partial, base = call(
        functools.partial(beside_x, dims, many_y, many_z),
        [f32(X + 2 * R, Y, Z), f32(Q, X, Y, Z)],
        (to_x[-1], weights, adjoint, flow_values, mask, smooth, *got_y, *got_z),
        None,
        [pltpu.VMEM((X * Y, Z), jnp.float32)],
        limit=16,
        flops=100000 * cells,
        moved=1000,
        name="beside_x",
    )
    (partial,) = call(
        functools.partial(far_x, dims),
        [f32(X + 2 * R, Y, Z)],
        (partial, beyond),
        limit=8,
        flops=1000,
        moved=1000,
        name="far_x",
    )
    relayed = [relay(beyond, "gx", nx)] if many_x else []

    extended = pltpu.VMEM((X + 2 * R, Y, Z), jnp.float32)
    near, near_damp = call(
        functools.partial(near_x, dims, many_z),
        [f32(X, Y, Z), f32(X, Y, Z)],
        (weights, partial, factor, flow_values, to_x[0], got_x[0]),
        None,
        [extended] * 2,
        limit=8,
        flops=1000,
        moved=1000,
        name="near_x",
    )
    smooth, ext = call(
        functools.partial(far_ready, dims, many_x, many_z),
        [f32(X + 2 * R, Y, Z)] * 2,
        (near, weights, partial, factor, flow_values, *to_x[1:], *got_x[1:]),
        limit=8,
        flops=1000,
        moved=1000,
        name="far_ready",
    )
    n_corners = (1 + many_y) * (1 + many_z)
    result, damp, *packs = call(
        functools.partial(source, dims, many_x, many_y, many_z),
        [f32(X, Y, Z), f32(X, Y, Z)]
        + [f32(X, R, Z)] * (1 + many_y)
        + [f32(Y, Z)] * (1 + many_z)
        + [f32(R, Z)] * n_corners,
        (smooth, ext, near, near_damp, *relayed),
        None,
        [extended],
        limit=8,
        name="source",
    )
    to_y, to_z, to_corner = packs[: 1 + many_y], packs[1 + many_y : -n_corners], packs[-n_corners:]
    got_y2 = some(exchange("gy", ny, *pair(to_y)))

    step = 2
    (adjoint_next,) = call(
        functools.partial(collide, dims, many_x, many_y, many_z, step),
        [f32(Q, X, Y, Z)],
        (adjoint, base, flow_values, damp, mask, *got_y, *got_z, *got_x),
        None,
        [pltpu.VMEM((Q, X, Y, Z), jnp.float32), dma((X // step,))],
        out_specs=(hbm,),
        limit=8,
        flops=300 * cells,
        moved=44 * 4 * cells,
        name="collide",
    )

    corners = [
        swap_corner(to_corner[m * (1 + many_z) + n], (ny, nz), m, n)
        for m in range(1 + many_y)
        for n in range(1 + many_z)
    ]
    got_z2 = some(exchange("gz", nz, *pair(to_z)))
    (own,) = call(
        functools.partial(own_z, dims),
        [f32(X * Y, Z)],
        (weights, result),
        limit=4,
        flops=1000,
        moved=1000,
        name="own_z",
    )
    (smooth,) = call(
        functools.partial(smooth_yz, dims, many_y),
        [f32(X, Y, Z)],
        (in_hbm(adjoint_next), weights, own, *got_y2),
        [hbm] + vmem(2 + len(got_y2)),
        [pltpu.VMEM((X, Y + 2 * R, Z), jnp.float32)],
        limit=4,
        name="smooth_yz",
    )
    (sensitivity,) = call(
        functools.partial(add_halo, dims, many_y, many_z),
        [f32(X, Y, Z)],
        (weights, smooth, *got_z2, *corners),
        None,
        [pltpu.VMEM((Y + 2 * R, Z), jnp.float32), pltpu.VMEM((X, Y, Z), jnp.float32), dma((4,))],
        out_specs=(hbm,),
        limit=4,
        name="add_halo",
    )
    return adjoint_next, sensitivity


def solution(mesh):
    counts = tuple(mesh.shape[a] for a in ("gx", "gy", "gz"))
    populations, field = P(None, "gx", "gy", "gz"), P("gx", "gy", "gz")
    return jax.shard_map(
        functools.partial(local, counts),
        mesh=mesh,
        in_specs=(populations, populations, field, field),
        out_specs=(populations, field),
        check_vma=False,
    )
```

```python
import functools
import math

import jax
import jax.numpy as jnp
import numpy as np
from jax import lax
from jax.experimental import pallas as pl
from jax.experimental.pallas import tpu as pltpu
from jax.sharding import PartitionSpec as P

Q = 19
R = 8

velocity = [
    (0, 0, 0),
    (1, 0, 0),
    (-1, 0, 0),
    (0, 1, 0),
    (0, -1, 0),
    (0, 0, 1),
    (0, 0, -1),
    (1, 1, 0),
    (-1, -1, 0),
    (1, -1, 0),
    (-1, 1, 0),
    (1, 0, 1),
    (-1, 0, -1),
    (1, 0, -1),
    (-1, 0, 1),
    (0, 1, 1),
    (0, -1, -1),
    (0, 1, -1),
    (0, -1, 1),
]
relax_rate = 1.25
sharpness = 64.0
threshold = 0.5
damping_max = 10.0
ramp_shape = 0.1


def fields_of(axis, sign):
    plus = [q for q in range(Q) if velocity[q][axis] == 1]
    return plus if sign > 0 else [q + 1 if q % 2 else q - 1 for q in plus]


PLUS = [fields_of(a, 1) for a in range(3)]
MINUS = [fields_of(a, -1) for a in range(3)]


def tap_weights():
    spread_width = R / 2.0
    unscaled = [math.exp(-((k - R) ** 2) / (2.0 * spread_width * spread_width)) for k in range(2 * R + 1)]
    summed = sum(unscaled)
    return [v / summed for v in unscaled]


TAPS = tap_weights()


def band(length):
    out = np.zeros((3, length, length), np.float32)
    for i in range(length):
        for k in range(-R, R + 1):
            j = i + k
            if j < 0:
                out[1, j + length, i] = TAPS[k + R]
            elif j >= length:
                out[2, j - length, i] = TAPS[k + R]
            else:
                out[0, j, i] = TAPS[k + R]
    return out


def packed_band(dims):
    X, Y, Z = dims
    out = np.zeros((2, 2, Z, Z), np.float32)
    for above_x in range(2):
        for above_z in range(2):
            for e in range(X):
                for i in range(X):
                    for z in range(R):
                        for j in range(R):
                            kx = i - e + 2 * R * above_x
                            kz = j - z + 2 * R * above_z
                            if 0 <= kx <= 2 * R and 0 <= kz <= 2 * R:
                                out[above_x, above_z, i * R + j, e * R + z] = TAPS[kx] * TAPS[kz]
    return out.reshape(4, Z, Z)


def packed_band_z(dims):
    X, Y, Z = dims
    out = np.zeros((2, Z, Z), np.float32)
    for above in range(2):
        for i in range(X):
            for z in range(R):
                for j in range(R):
                    k = j - z + 2 * R * above
                    if 0 <= k <= 2 * R:
                        out[above, i * R + j, i * R + z] = TAPS[k]
    return out


def sides(parity, even, odd):
    zero = jnp.zeros_like(even)
    if odd is None:
        return jnp.where(parity == 0, zero, even), jnp.where(parity == 0, even, zero)
    return jnp.where(parity == 0, odd, even), jnp.where(parity == 0, even, odd)


def parity_of(axis):
    return lax.rem(lax.axis_index(axis), 2)


def swap(array, axis, count, first):
    pairs = [(i, i + 1) for i in range(first, count - 1, 2)]
    return lax.ppermute(array, axis, pairs + [(b, a) for a, b in pairs])


def relay(array, axis, count):
    pairs = [(i + 2, i) for i in range(1, count - 2, 2)] + [(i - 2, i) for i in range(2, count, 2)]
    return lax.ppermute(array, axis, pairs)


def swap_corner(array, counts, first_y, first_z):
    ny, nz = counts
    pairs = []
    for a in range(first_y, ny - 1, 2):
        for c in range(first_z, nz - 1, 2):
            for d, e in ((c, c + 1), (c + 1, c)):
                pairs += [(a * nz + d, (a + 1) * nz + e), ((a + 1) * nz + e, a * nz + d)]
    return lax.ppermute(array, ("gy", "gz"), pairs)


def exchange(axis, count, even, odd):
    return swap(even, axis, count, 0), (None if odd is None else swap(odd, axis, count, 1))


def vmem(count):
    return [pl.BlockSpec(memory_space=pltpu.VMEM)] * count


def in_hbm(array):
    return pltpu.with_memory_space_constraint(array, pltpu.HBM)


def f32(*shape):
    return jax.ShapeDtypeStruct(shape, jnp.float32)


def call(body, outs, args, specs=None, scratch=(), limit=16, flops=1e6, moved=1e6, **rest):
    return pl.pallas_call(
        body,
        out_shape=outs,
        in_specs=specs or vmem(len(args)),
        out_specs=rest.pop("out_specs", tuple(vmem(len(outs)))),
        scratch_shapes=list(scratch),
        compiler_params=pltpu.CompilerParams(vmem_limit_bytes=limit * 2**20),
        cost_estimate=pl.CostEstimate(flops=int(flops), bytes_accessed=int(moved), transcendentals=0),
        **rest,
    )(*args)


def filter_rows(load):
    total = TAPS[R] * load(R)
    for k in range(R):
        total = total + TAPS[k] * (load(k) + load(2 * R - k))
    return total


def dot(a, b):
    return jnp.dot(a, b, preferred_element_type=jnp.float32, precision=lax.Precision.HIGHEST)


def row_of(ref, at):
    return ref[pl.ds(at, 1), :]


class Pull:
    def __init__(self, adj, dims, py, y_even, y_odd, pz=None, z_even=None, z_odd=None):
        self.adj, self.dims = adj, dims
        self.py, self.y_even, self.y_odd = py, y_even, y_odd
        self.pz, self.z_even, self.z_odd = pz, z_even, z_odd
        X, Y, Z = dims
        self.row = lax.broadcasted_iota(jnp.int32, (Y, Z), 0)
        self.lane = lax.broadcasted_iota(jnp.int32, (Y, Z), 1)

    def along_y(self, q, x):
        X, Y, Z = self.dims
        here = self.adj[q, x]
        cy = velocity[q][1]
        if cy == 0:
            return here
        at = X * R + X * (PLUS if cy > 0 else MINUS)[1].index(q) + x
        even = row_of(self.y_even, at)
        odd = None if self.y_odd is None else row_of(self.y_odd, at)
        below, above = sides(self.py, even, odd)
        if cy > 0:
            return jnp.where(self.row == Y - 1, above, pltpu.roll(here, Y - 1, 0))
        return jnp.where(self.row == 0, below, pltpu.roll(here, 1, 0))

    def faces(self, x):
        even = self.z_even[x]
        odd = None if self.z_odd is None else self.z_odd[x]
        return sides(self.pz, even, odd)

    def both(self, q, x, faces):
        X, Y, Z = self.dims
        here = self.along_y(q, x)
        cz = velocity[q][2]
        if cz == 0:
            return here
        below, above = faces
        if cz > 0:
            j = PLUS[2].index(q)
            face = pltpu.roll(above, 4 - j, 1) if j != 4 else above
            return jnp.where(self.lane == Z - 1, face, pltpu.roll(here, Z - 1, 1))
        j = MINUS[2].index(q)
        face = pltpu.roll(below, Z - j, 1) if j else below
        return jnp.where(self.lane == 0, face, pltpu.roll(here, 1, 1))


def refs_of(refs, odd):
    even = next(refs)
    return even, (next(refs) if odd else None)


def pack_y(dims, many, adj, design, *rest):
    X, Y, Z = dims
    outs = rest[: 1 + many]
    kept, tiles, sems, kept_sem = rest[1 + many :]
    py = parity_of("gy")
    keep = pltpu.make_async_copy(design, kept, kept_sem)
    keep.start()

    def copies(n, up):
        names = (MINUS if up else PLUS)[1]
        first = Y - R if up else 0
        return [
            pltpu.make_async_copy(adj.at[q, :, pl.ds(first, R), :], tiles.at[n, j], sems.at[n, j])
            for j, q in enumerate(names)
        ]

    def start(n, out, up):
        for c in copies(n, up):
            c.start()

    def fill(n, out, up):
        first = Y - R if up else 0
        out[: X * R, :] = kept[:, first : first + R, :].reshape(X * R, Z)
        for c in copies(n, up):
            c.wait()
        for j in range(5):
            out[X * R + X * j : X * R + X * (j + 1), :] = tiles[n, j, :, R - 1 if up else 0, :]

    def each(act):
        for n, out in enumerate(outs):
            pl.when(py == n)(functools.partial(act, n, out, True))
            pl.when(py != n)(functools.partial(act, n, out, False))

    each(start)
    keep.wait()
    each(fill)


def prepare(dims, many_z, ahead, forward, adj, *rest):
    X, Y, Z = dims
    rest = iter(rest)
    flow_ref, factor = next(rest), next(rest)
    outs = [next(rest) for _ in range(1 + many_z)]
    rising, falling, straight, members_ref, sems = rest
    pz = parity_of("gz")
    part = X // 4
    copies = [
        pltpu.make_async_copy(
            forward.at[:, pl.ds(i * part, part)], members_ref.at[:, pl.ds(i * part, part)], sems.at[i]
        )
        for i in range(4)
    ]
    for c in copies:
        c.start()
    row = lax.broadcasted_iota(jnp.int32, (Y, Z), 0)
    lane = lax.broadcasted_iota(jnp.int32, (Y, Z), 1)
    zero = jnp.zeros((Y, Z), jnp.float32)

    def along_y(q, x):
        here, cy = adj[q, x], velocity[q][1]
        if cy == 0:
            return here
        return jnp.where(row == (Y - 1 if cy > 0 else 0), zero, pltpu.roll(here, (-cy) % Y, 0))

    def both(q, x):
        here, cz = along_y(q, x), velocity[q][2]
        if cz == 0:
            return here
        return jnp.where(lane == (Z - 1 if cz > 0 else 0), zero, pltpu.roll(here, (-cz) % Z, 1))

    for a in range(3):
        rising[a, X] = zero
        falling[a, 1] = zero

    def moments(x, _):
        groups = {}
        for q in range(1, Q):
            groups.setdefault(velocity[q][0], {})[q] = both(q, x)
        level, up, down = moment_of(groups[0]), moment_of(groups[1]), moment_of(groups[-1])
        for a in range(3):
            rising[a, x] = up[a]
            falling[a, x + 2] = down[a]
        for a in range(1, 3):
            straight[a - 1, x] = level[a]
        return 0

    def layer(x, _):
        members = [members_ref[q, x] for q in range(Q)]
        inverse = 1.0 / sum(members[1:], members[0])
        total = None
        for a in range(3):
            terms = [(velocity[q][a], members[q] - members[q + 1]) for q in range(1, Q, 2) if velocity[q][a] != 0]
            vel = signed(terms) * inverse
            flow_ref[a, x] = vel
            moment = rising[a, x + 1] + falling[a, x + 1]
            if a > 0:
                moment = moment + straight[a - 1, x]
            term = vel * (vel - moment)
            total = term if total is None else total + term
        flow_ref[3, x] = inverse
        factor[x] = total
        return 0

    def fill(out, up):
        names = (MINUS if up else PLUS)[2]

        def face(x, _):
            value = zero
            for j, q in enumerate(names):
                slot = slot_of(Z, up, j)
                value = jnp.where(lane == slot, pltpu.roll(along_y(q, x), shift_of(Z, up, j), 1), value)
            out[x] = value
            return 0

        lax.fori_loop(0, X, face, 0, unroll=2)

    lax.fori_loop(0, X, moments, 0, unroll=2)
    for n, out in enumerate(outs):
        pl.when(pz == n)(functools.partial(fill, out, True))
        pl.when(pz != n)(functools.partial(fill, out, False))
    for i, c in enumerate(copies):
        c.wait()
        lax.fori_loop(i * part, (i + 1) * part, layer, 0, unroll=2)


def slot_of(Z, up, j):
    return j if up else Z - 5 + j


def shift_of(Z, up, j):
    return (slot_of(Z, up, j) - (Z - 1 if up else 0)) % Z


def extend_y(dims, pad, own, py, even, odd):
    X, Y, Z = dims
    below, above = sides(py, even, odd)
    pad[:, :R, :] = below
    pad[:, R : R + Y, :] = own
    pad[:, R + Y :, :] = above


def filter_y(dims, pad, store, step=2):
    X, Y, Z = dims
    for x in range(0, X, step):
        store(x, filter_rows(lambda k: pad[x : x + step, k : k + Y, :]))


def design_y(dims, many_y, many_z, design, *rest):
    X, Y, Z = dims
    rest = iter(rest)
    faces = [next(rest) for _ in range(1 + many_z)]
    y_even, y_odd = refs_of(rest, many_y)
    filtered = next(rest)
    outs = [next(rest) for _ in range(1 + many_z)]
    pad, edges = rest
    pz = parity_of("gz")
    py = parity_of("gy")

    def halo(ref):
        return ref[: X * R, :].reshape(X, R, Z)

    extend_y(dims, pad, design[...], py, halo(y_even), None if y_odd is None else halo(y_odd))

    def store(x, value):
        filtered[x : x + value.shape[0]] = value

    filter_y(dims, pad, store)
    row = lax.broadcasted_iota(jnp.int32, (Y, Z), 0)
    lane = lax.broadcasted_iota(jnp.int32, (Y, Z), 1)

    def fill(out, face, up):
        names = (MINUS if up else PLUS)[2]
        slanted = [(j, q) for j, q in enumerate(names) if velocity[q][1] != 0]
        for i, (j, q) in enumerate(slanted):
            edges[i] = pltpu.roll(rows_of(dims, py, y_even, y_odd, q), shift_of(Z, up, j), 1)
        first, last = slot_of(Z, up, 0), slot_of(Z, up, 4)

        def layer(x, _):
            value = jnp.where((lane >= first) & (lane <= last), face[x], filtered[x])
            for i, (j, q) in enumerate(slanted):
                at = (row == (Y - 1 if velocity[q][1] > 0 else 0)) & (lane == slot_of(Z, up, j))
                value = jnp.where(at, edges[i, pl.ds(x, 1), :], value)
            out[x] = value
            return 0

        lax.fori_loop(0, X, layer, 0, unroll=True)

    for n, (out, face) in enumerate(zip(outs, faces)):
        pl.when(pz == n)(functools.partial(fill, out, face, True))
        pl.when(pz != n)(functools.partial(fill, out, face, False))


def rows_of(dims, py, even, odd, q):
    X, Y, Z = dims
    above = velocity[q][1] > 0
    at = X * R + X * (PLUS if above else MINUS)[1].index(q)
    return sides(py, even[at : at + X, :], None if odd is None else odd[at : at + X, :])[int(above)]


def signed(terms):
    total = None
    for sign, value in terms:
        value = value if sign > 0 else -value
        total = value if total is None else total + value
    return total


def moment_of(values):
    return [
        signed([(velocity[q][a], v) for q, v in values.items() if velocity[q][a] != 0]) for a in range(3)
    ]


def halo_z(weights, pz, even, odd):
    value = dot(even, jnp.where(pz == 0, weights[2], weights[1]))
    if odd is not None:
        value = value + dot(odd, jnp.where(pz == 0, weights[1], weights[2]))
    return value


def flat(dims, ref):
    X, Y, Z = dims
    return None if ref is None else ref[...].reshape(X * Y, Z)


def own_z(dims, weights, field, out):
    out[...] = dot(flat(dims, field), weights[0])


def factor_y(dims, many_y, weights, filtered_y, flow_ref, factor, *rest):
    X, Y, Z = dims
    rest = iter(rest)
    y_even, y_odd = refs_of(rest, many_y)
    smooth, out = rest
    smooth[...] = dot(flat(dims, filtered_y), weights[0])
    out[...] = factor[...]
    py = parity_of("gy")
    row = lax.broadcasted_iota(jnp.int32, (X, Z), 0)
    lane = lax.broadcasted_iota(jnp.int32, (X, Z), 1)
    for edge, names in ((0, MINUS[1]), (Y - 1, PLUS[1])):
        values = {}
        for q in names:
            value = rows_of(dims, py, y_even, y_odd, q)
            cx, _, cz = velocity[q]
            if cx != 0:
                value = jnp.where(row == (X - 1 if cx > 0 else 0), 0.0, pltpu.roll(value, (-cx) % X, 0))
            if cz != 0:
                value = jnp.where(lane == (Z - 1 if cz > 0 else 0), 0.0, pltpu.roll(value, (-cz) % Z, 1))
            values[q] = value
        moment = moment_of(values)
        total = factor[:, edge, :]
        for a in range(3):
            total = total - flow_ref[a, :, edge, :] * moment[a]
        out[:, edge, :] = total


def faces_x(dims, out, up, factor, flow_ref, pull):
    X, Y, Z = dims
    names = (MINUS if up else PLUS)[0]
    edge = X - 1 if up else 0
    first = X - R if up else 0
    at = R * Y
    out[:at, :] = factor[first : first + R].reshape(R * Y, Z)
    faces = pull.faces(edge)
    for q in names:
        out[at : at + Y, :] = pull.both(q, edge, faces)
        at += Y
    for a in range(3):
        out[at : at + Y, :] = flow_ref[a, edge]
        at += Y


def pack_halo(dims, pz, refs, out):
    X, Y, Z = dims
    lane = lax.broadcasted_iota(jnp.int32, (Y, Z), 1)
    for n, ref in enumerate(refs):
        value = jnp.zeros((Y, Z), jnp.float32)
        for x in range(X):
            there = (lane >= R * x) & (lane < R * (x + 1))
            value = jnp.where(there, pltpu.roll(ref[x], lanes_x(dims, pz, n, x), 1), value)
        out[(R + 8 + n) * Y : (R + 9 + n) * Y, :] = value


def pack_odd(dims, many_y, many_z, adj, ahead, factor, flow_ref, *rest):
    X, Y, Z = dims
    rest = iter(rest)
    y_even, y_odd = refs_of(rest, many_y)
    z_even, z_odd = refs_of(rest, many_z)
    (out,) = rest
    px = parity_of("gx")
    pz = parity_of("gz")
    out[(R + 8) * Y :, :] = ahead[(R + 8) * Y :, :]
    pull = Pull(adj, dims, parity_of("gy"), y_even, y_odd, pz, z_even, z_odd)
    pl.when(px == 1)(lambda: faces_x(dims, out, True, factor, flow_ref, pull))
    pl.when(px != 1)(lambda: faces_x(dims, out, False, factor, flow_ref, pull))


def pack_x(dims, many_y, many_z, adj, factor_in, flow_ref, *rest):
    X, Y, Z = dims
    rest = iter(rest)
    y_even, y_odd = refs_of(rest, many_y)
    z_even, z_odd = refs_of(rest, many_z)
    out, factor = rest
    px, py, pz = parity_of("gx"), parity_of("gy"), parity_of("gz")
    pack_halo(dims, pz, [z_even, z_odd][: 1 + many_z], out)
    lane = lax.broadcasted_iota(jnp.int32, (Y, Z), 1)
    factor[...] = factor_in[...]

    def correct(ref, above):
        names = (PLUS if above else MINUS)[2]
        edge = Z - 1 if above else 0
        zero = jnp.zeros((Y, Z), jnp.float32)

        def layer(x, _):
            values = {}
            for j, q in enumerate(names):
                cx = velocity[q][0]
                face = ref[jnp.clip(x + cx, 0, X - 1)] if cx else ref[x]
                shift = (edge - slot_of(Z, not above, j)) % Z
                face = pltpu.roll(face, shift, 1) if shift else face
                if cx != 0:
                    face = jnp.where(x == (X - 1 if cx > 0 else 0), zero, face)
                values[q] = face
            moment = moment_of(values)
            change = flow_ref[0, x] * moment[0] + flow_ref[1, x] * moment[1] + flow_ref[2, x] * moment[2]
            factor[x] = factor[x] - jnp.where(lane == edge, change, zero)
            return 0

        lax.fori_loop(0, X, layer, 0, unroll=True)

    for n, ref in enumerate([z_even, z_odd][: 1 + many_z]):
        pl.when(pz == n)(functools.partial(correct, ref, True))
        pl.when(pz != n)(functools.partial(correct, ref, False))

    pull = Pull(adj, dims, py, y_even, y_odd, pz, z_even, z_odd)

    pl.when(px == 0)(lambda: faces_x(dims, out, True, factor, flow_ref, pull))
    pl.when(px != 0)(lambda: faces_x(dims, out, False, factor, flow_ref, pull))


def project(filtered):
    base = math.tanh(sharpness * threshold)
    denominator = base + math.tanh(sharpness * (1.0 - threshold))
    inner = jnp.tanh(sharpness * (filtered - threshold))
    physical = (base + inner) * (1.0 / denominator)
    steep = (sharpness / denominator) * (1.0 - inner * inner)
    inverse = 1.0 / (ramp_shape + physical)
    return physical, steep, inverse


def taps_of(X, above, e):
    shift = 2 * R + (X if above else -X) - e
    return [(TAPS[i + shift], i) for i in range(X) if 0 <= i + shift <= 2 * R]


def add_side(dims, base, layers, at, out, above):
    X, Y, Z = dims
    for e in range(X + 2 * R):
        total = base[e]
        for tap, i in taps_of(X, above, e):
            total = total + tap * layers[at + i * Y : at + (i + 1) * Y, :]
        out[e] = total


def lanes_x(dims, pz, n, x):
    Z = dims[2]
    return jnp.where(pz == n, (R * x) % Z, (R * x + R) % Z)


def layers_toward(dims, above, near):
    X = dims[0]
    if near:
        return range(2 * R, X + 2 * R) if above else range(X)
    return range(X, X + 2 * R) if above else range(2 * R)


def complete(dims, above, layers, many_z, pz, weights, partial, factor, flow_ref, own, got, smooth, ext):
    X, Y, Z = dims
    u_at, v_at, d_at = R * Y, R * Y + 5 * Y, R * Y + 8 * Y
    for e in layers:
        smooth[e] = partial[e]
        if R <= e < R + X:
            ext[e] = factor[e - R]
        elif got is None:
            ext[e] = jnp.zeros((Y, Z), jnp.float32)
        else:
            at = (e - R - X if above else e) * Y
            ext[e] = got[at : at + Y, :]
    if got is None:
        return
    lane = lax.broadcasted_iota(jnp.int32, (Y, Z), 1)
    for n in range(1 + many_z):
        above_z = jnp.where(pz == n, 1, 0)
        value = dot(got[d_at + n * Y : d_at + (n + 1) * Y, :], weights[3 + 2 * int(above) + above_z])
        first = (Z - R) * above_z
        there = (lane >= first) & (lane < first + R)
        for i in range(X):
            e = i + X * int(above)
            moved = pltpu.roll(value, lax.rem(first + Z - R * i, Z), 1)
            smooth[e] = smooth[e] + jnp.where(there, moved, 0.0)

    def moment(ref, names):
        return moment_of({q: ref[u_at + j * Y : u_at + (j + 1) * Y, :] for j, q in enumerate(names)})

    def less(e, vel, m):
        ext[e] = ext[e] - (vel[0] * m[0] + vel[1] * m[1] + vel[2] * m[2])

    inner, outer = (R + X - 1, R + X) if above else (R, R - 1)
    there, here = (PLUS[0], MINUS[0]) if above else (MINUS[0], PLUS[0])
    less(inner, [flow_ref[a, inner - R] for a in range(3)], moment(got, there))
    less(outer, [got[v_at + a * Y : v_at + (a + 1) * Y, :] for a in range(3)], moment(own, here))


def half_source(dims, above, layers, smooth, relayed, ext, new, damp, base, result):
    X, Y, Z = dims
    slope = -damping_max * ramp_shape * (1.0 + ramp_shape)
    for e in layers:
        total = smooth[e]
        if relayed is not None:
            for tap, i in taps_of(X, above, e):
                total = total + tap * relayed[i * Y : (i + 1) * Y, :]
        physical, steep, inverse = project(total)
        new[e] = (slope * steep) * (inverse * inverse) * ext[e]
        if R <= e < R + X:
            damp[e - R] = (2.0 * damping_max * ramp_shape) * (1.0 - physical) * inverse
    for x in range(X):
        terms = [TAPS[e - x] * new[e] for e in layers if 0 <= e - x <= 2 * R]
        if base is not None:
            terms = [base[x]] + terms
        result[x] = sum(terms[1:], terms[0]) if terms else jnp.zeros((Y, Z), jnp.float32)


def near_x(dims, many_z, weights, partial, factor, flow_ref, own, got, result, damp, smooth, ext):
    px, pz = parity_of("gx"), parity_of("gz")

    def act(above):
        layers = layers_toward(dims, above, True)
        complete(dims, above, layers, many_z, pz, weights, partial, factor, flow_ref, own, got, smooth, ext)
        half_source(dims, above, layers, smooth, None, ext, ext, damp, None, result)

    pl.when(px == 0)(lambda: act(True))
    pl.when(px != 0)(lambda: act(False))


def far_ready(dims, many_x, many_z, ahead, weights, partial, factor, flow_ref, *rest):
    own, got = rest[:2] if many_x else (None, None)
    smooth, ext = rest[-2:]
    px, pz = parity_of("gx"), parity_of("gz")

    def act(above):
        layers = layers_toward(dims, above, False)
        complete(dims, above, layers, many_z, pz, weights, partial, factor, flow_ref, own, got, smooth, ext)

    pl.when(px == 1)(lambda: act(True))
    pl.when(px != 1)(lambda: act(False))


def source(dims, many_x, many_y, many_z, smooth, ext, near, near_damp, *rest):
    X, Y, Z = dims
    rest = iter(rest)
    relayed = next(rest) if many_x else None
    result, damp = next(rest), next(rest)
    rows = [next(rest) for _ in range(1 + many_y)]
    to_z = [next(rest) for _ in range(1 + many_z)]
    corners = [[next(rest) for _ in range(1 + many_z)] for _ in range(1 + many_y)]
    (new,) = rest
    px, py, pz = parity_of("gx"), parity_of("gy"), parity_of("gz")
    damp[...] = near_damp[...]

    def act(above):
        layers = layers_toward(dims, above, False)
        half_source(dims, above, layers, smooth, relayed, ext, new, damp, near, result)

    pl.when(px == 1)(lambda: act(True))
    pl.when(px != 1)(lambda: act(False))
    for n, out in enumerate(rows):

        @pl.when(py == n)
        def _(out=out):
            out[...] = result[:, Y - R :, :]

        @pl.when(py != n)
        def _(out=out):
            out[...] = result[:, :R, :]

    pack_corner(dims, py, pz, result, to_z, corners)


def pack_corner(dims, py, pz, own, to_z, corners):
    X, Y, Z = dims
    lane = lax.broadcasted_iota(jnp.int32, (Y, Z), 1)
    for n, out in enumerate(to_z):
        value = jnp.zeros((Y, Z), jnp.float32)
        for x in range(X):
            shift = jnp.where(pz == n, (R * x + R) % Z, (R * x) % Z)
            there = (lane >= R * x) & (lane < R * (x + 1))
            value = jnp.where(there, pltpu.roll(own[x], shift, 1), value)
        out[...] = value
        for m, row in enumerate(corners):
            row[n][:R, :] = jnp.where(py == m, value[Y - R :], value[:R])
            row[n][R:, :] = jnp.zeros((3 * R, Z), jnp.float32)


def smooth_yz(dims, many_y, ahead, weights, own, *rest):
    X, Y, Z = dims
    rest = iter(rest)
    rows = [next(rest) for _ in range(1 + many_y)]
    result, pad = rest
    rows = [dot(ref[...].reshape(X * R, Z), weights[0]).reshape(X, R, Z) for ref in rows]
    extend_y(dims, pad, own[...].reshape(X, Y, Z), parity_of("gy"), rows[0], rows[1] if many_y else None)

    def store(x, value):
        result[x : x + value.shape[0]] = value

    filter_y(dims, pad, store)


def add_halo(dims, many_y, many_z, weights, own, *rest):
    X, Y, Z = dims
    rest = iter(rest)
    sides_z = [next(rest) for _ in range(1 + many_z)]
    corners = [[next(rest) for _ in range(1 + many_z)] for _ in range(1 + many_y)]
    out, pad, result, sems = rest
    py, pz = parity_of("gy"), parity_of("gz")
    lane = lax.broadcasted_iota(jnp.int32, (Y, Z), 1)
    moved = []
    for n in range(1 + many_z):
        below, above = sides(py, corners[0][n][:R, :], corners[1][n][:R, :] if many_y else None)
        pad[:R, :] = below
        pad[R : R + Y, :] = sides_z[n][...]
        pad[R + Y :, :] = above
        side = jnp.where(pz == n, 1, 0)
        first = (Z - R) * side
        extra = dot(filter_rows(lambda k: pad[k : k + Y, :]), weights[7 + side])
        moved.append((extra, first, (lane >= first) & (lane < first + R)))
    part = X // 4
    copies = []
    for i in range(4):
        for x in range(i * part, (i + 1) * part):
            value = own[x]
            for extra, first, there in moved:
                value = value + jnp.where(there, pltpu.roll(extra, lax.rem(first + Z - R * x, Z), 1), 0.0)
            result[x] = value
        here = pl.ds(i * part, part)
        copies.append(pltpu.make_async_copy(result.at[here], out.at[here], sems.at[i]))
        copies[-1].start()
    for c in copies:
        c.wait()


def relax(pulled, vel, speed_sq, label, drag, store):
    plus = {q: pulled[q] + pulled[q + 1] for q in range(1, Q, 2)}
    minus = {q: pulled[q] - pulled[q + 1] for q in range(1, Q, 2)}
    axes = (1, 3, 5)
    straight = plus[1] + plus[3] + plus[5]
    slanted = plus[7] + plus[9] + plus[11] + plus[13] + plus[15] + plus[17]
    zeroth = (1.0 / 3.0) * pulled[0] + (1.0 / 18.0) * straight + (1.0 / 36.0) * slanted
    first, diagonal = [], []
    for a in range(3):
        terms = [(velocity[q][a], minus[q]) for q in range(7, Q, 2) if velocity[q][a] != 0]
        first.append((1.0 / 18.0) * minus[axes[a]] + (1.0 / 36.0) * signed(terms))
        both = [(1, plus[q]) for q in range(7, Q, 2) if velocity[q][a] != 0]
        diagonal.append((1.0 / 18.0) * plus[axes[a]] + (1.0 / 36.0) * signed(both))
    xy = (1.0 / 36.0) * (plus[7] - plus[9])
    xz = (1.0 / 36.0) * (plus[11] - plus[13])
    yz = (1.0 / 36.0) * (plus[15] - plus[17])
    turned = [
        diagonal[0] * vel[0] + xy * vel[1] + xz * vel[2],
        xy * vel[0] + diagonal[1] * vel[1] + yz * vel[2],
        xz * vel[0] + yz * vel[1] + diagonal[2] * vel[2],
    ]
    quadric = vel[0] * turned[0] + vel[1] * turned[1] + vel[2] * turned[2]
    eq_scalar = zeroth * (1.0 + 1.5 * speed_sq) - 4.5 * quadric
    eq_vector = [3.0 * first[a] + 9.0 * turned[a] - 3.0 * zeroth * vel[a] for a in range(3)]
    fluid, solid, inlet = label == 0, label == 1, label == 2
    zero = jnp.zeros_like(eq_scalar)
    keep = jnp.where(fluid, 1.0 - relax_rate, zero)
    bounce = jnp.where(solid, 1.0, zero)
    level = relax_rate * eq_scalar
    tilt = [relax_rate * v for v in eq_vector]
    if drag is not None:
        level = level - drag * speed_sq
        tilt = [t + drag * v for t, v in zip(tilt, vel)]
    level = jnp.where(fluid, level, jnp.where(solid, zero, eq_scalar))
    tilt = [jnp.where(fluid, t, jnp.where(inlet, v, zero)) for t, v in zip(tilt, eq_vector)]
    store(0, (keep + bounce) * pulled[0] + level)
    for q in range(1, Q, 2):
        lean = lean_of(q, tilt)
        store(q, keep * pulled[q] + bounce * pulled[q + 1] + (level + lean))
        store(q + 1, keep * pulled[q + 1] + bounce * pulled[q] + (level - lean))


def lean_of(q, vector):
    return signed([(velocity[q][a], vector[a]) for a in range(3) if velocity[q][a] != 0])


def square(vel):
    return vel[0] * vel[0] + vel[1] * vel[1] + vel[2] * vel[2]


def far_x(dims, partial, beyond, out):
    px = parity_of("gx")
    pl.when(px == 0)(lambda: add_side(dims, partial, beyond, 0, out, True))
    pl.when(px != 0)(lambda: add_side(dims, partial, beyond, 0, out, False))


def beside_x(dims, many_y, many_z, ahead, weights, adj, flow_ref, mask, smooth, *rest):
    X, Y, Z = dims
    rest = iter(rest)
    y_even, y_odd = refs_of(rest, many_y)
    z_even, z_odd = refs_of(rest, many_z)
    partial, base, own = rest
    own[...] = smooth[...] + halo_z(weights, parity_of("gz"), flat(dims, z_even), flat(dims, z_odd))
    for e in range(X + 2 * R):
        terms = [(i - e + 2 * R, i * Y) for i in range(X) if 0 <= i - e + 2 * R <= 2 * R]
        partial[e] = sum(TAPS[k] * own[at : at + Y, :] for k, at in terms)
    pull = Pull(adj, dims, parity_of("gy"), y_even, y_odd, parity_of("gz"), z_even, z_odd)

    def layer(x, _):
        around = {c: pull.faces(x + c) for c in (-1, 0, 1)}
        pulled = [pull.both(q, x + velocity[q][0], around[velocity[q][0]]) for q in range(Q)]
        vel = [flow_ref[a, x] for a in range(3)]

        def store(q, value):
            base[q, x] = value

        relax(pulled, vel, square(vel), mask[x], None, store)
        return 0

    lax.fori_loop(1, X - 1, layer, 0, unroll=7)


def collide(dims, many_x, many_y, many_z, step, adj, base, flow_ref, damp, mask, *rest):
    X, Y, Z = dims
    rest = iter(rest)
    y_even, y_odd = refs_of(rest, many_y)
    z_even, z_odd = refs_of(rest, many_z)
    x_even, x_odd = refs_of(rest, many_x)
    target, out, sems = rest
    px, py, pz = parity_of("gx"), parity_of("gy"), parity_of("gz")
    pull = Pull(adj, dims, py, y_even, y_odd, pz, z_even, z_odd)
    u_at = R * Y

    def layer(x):
        vel = [flow_ref[a, x] for a in range(3)]
        drag = jnp.where(mask[x] == 0, damp[x] * flow_ref[3, x], 0.0)
        level = drag * square(vel)
        tilt = [drag * v for v in vel]
        out[0, x] = base[0, x] - level
        for q in range(1, Q, 2):
            lean = lean_of(q, tilt)
            out[q, x] = base[q, x] + (lean - level)
            out[q + 1, x] = base[q + 1, x] - (lean + level)

    def edge(x, toward):
        around = {c: pull.faces(x + c) for c in (0, -toward)}
        pulled = []
        for q in range(Q):
            cx = velocity[q][0]
            if cx == toward:
                at = u_at + Y * (PLUS if cx > 0 else MINUS)[0].index(q)
                both = sides(px, x_even[at : at + Y, :], None if x_odd is None else x_odd[at : at + Y, :])
                pulled.append(both[int(cx > 0)])
            else:
                pulled.append(pull.both(q, x + cx, around[cx]))
        vel = [flow_ref[a, x] for a in range(3)]

        def store(q, value):
            out[q, x] = value

        relax(pulled, vel, square(vel), mask[x], damp[x] * flow_ref[3, x], store)

    last = X // step - 1
    copies = []
    for part in [1, 0, 2, last, *range(3, last)]:
        for x in range(part * step, (part + 1) * step):
            if x == 0:
                edge(x, -1)
            elif x == X - 1:
                edge(x, 1)
            else:
                layer(x)
        here = pl.ds(part * step, step)
        copies.append(pltpu.make_async_copy(out.at[:, here], target.at[:, here], sems.at[part]))
        copies[-1].start()
    for c in copies:
        c.wait()


def local(counts, forward, adjoint, design, mask):
    many_x, many_y, many_z = (int(n > 2) for n in counts)
    nx, ny, nz = counts
    dims = design.shape
    X, Y, Z = dims
    weights = jnp.asarray(np.concatenate([band(Z), packed_band(dims), packed_band_z(dims)]))
    hbm = pl.BlockSpec(memory_space=pltpu.HBM)
    cells = X * Y * Z
    some = lambda pair: [v for v in pair if v is not None]
    pair = lambda items: (items[0], items[1] if len(items) > 1 else None)
    dma = pltpu.SemaphoreType.DMA

    y_rows = X * R + 5 * X
    *to_y, design = call(
        functools.partial(pack_y, dims, many_y),
        [f32(y_rows, Z)] * (1 + many_y) + [f32(X, Y, Z)],
        (in_hbm(adjoint), in_hbm(design)),
        [hbm, hbm],
        [pltpu.VMEM((1 + many_y, 5, X, R, Z), jnp.float32), dma((1 + many_y, 5)), dma],
        limit=4,
        name="pack_y",
    )
    got_y = some(exchange("gy", ny, *pair(to_y)))

    flow_values, factor, *faces = call(
        functools.partial(prepare, dims, many_z),
        [f32(4, X, Y, Z)] + [f32(X, Y, Z)] * (2 + many_z),
        (to_y[0], in_hbm(forward), adjoint),
        vmem(1) + [hbm] + vmem(1),
        [pltpu.VMEM((3, X + 2, Y, Z), jnp.float32)] * 2
        + [pltpu.VMEM((2, X, Y, Z), jnp.float32), pltpu.VMEM((Q, X, Y, Z), jnp.float32), dma((4,))],
        limit=16,
        flops=200 * cells,
        moved=44 * 4 * cells,
        name="prepare",
    )

    filtered_y, *to_z = call(
        functools.partial(design_y, dims, many_y, many_z),
        [f32(X, Y, Z)] * (2 + many_z),
        (design, *faces, *got_y),
        None,
        [pltpu.VMEM((X, Y + 2 * R, Z), jnp.float32), pltpu.VMEM((2, X, Z), jnp.float32)],
        limit=8,
        name="design_y",
    )
    got_z = some(exchange("gz", nz, *pair(to_z)))

    smooth, factor = call(
        functools.partial(factor_y, dims, many_y),
        [f32(X * Y, Z), f32(X, Y, Z)],
        (weights, filtered_y, flow_values, factor, *got_y),
        limit=8,
        flops=200 * cells,
        name="factor_y",
    )
    beyond = swap(smooth, "gx", nx, 0)

    x_rows = R * Y + 8 * Y
    even, factor = call(
        functools.partial(pack_x, dims, many_y, many_z),
        [f32(x_rows + (1 + many_z) * Y, Z), f32(X, Y, Z)],
        (adjoint, factor, flow_values, *got_y, *got_z),
        limit=16,
        name="pack_x",
    )
    to_x = [even]
    if many_x:
        to_x += call(
            functools.partial(pack_odd, dims, many_y, many_z),
            [f32(x_rows + (1 + many_z) * Y, Z)],
            (adjoint, even, factor, flow_values, *got_y, *got_z),
            limit=16,
            name="pack_odd",
        )
    got_x = some(exchange("gx", nx, *pair(to_x)))

    partial, base = call(
        functools.partial(beside_x, dims, many_y, many_z),
        [f32(X + 2 * R, Y, Z), f32(Q, X, Y, Z)],
        (to_x[-1], weights, adjoint, flow_values, mask, smooth, *got_y, *got_z),
        None,
        [pltpu.VMEM((X * Y, Z), jnp.float32)],
        limit=16,
        flops=100000 * cells,
        moved=1000,
        name="beside_x",
    )
    (partial,) = call(
        functools.partial(far_x, dims),
        [f32(X + 2 * R, Y, Z)],
        (partial, beyond),
        limit=8,
        flops=1000,
        moved=1000,
        name="far_x",
    )
    relayed = [relay(beyond, "gx", nx)] if many_x else []

    extended = pltpu.VMEM((X + 2 * R, Y, Z), jnp.float32)
    near, near_damp = call(
        functools.partial(near_x, dims, many_z),
        [f32(X, Y, Z), f32(X, Y, Z)],
        (weights, partial, factor, flow_values, to_x[0], got_x[0]),
        None,
        [extended] * 2,
        limit=8,
        flops=1000,
        moved=1000,
        name="near_x",
    )
    smooth, ext = call(
        functools.partial(far_ready, dims, many_x, many_z),
        [f32(X + 2 * R, Y, Z)] * 2,
        (near, weights, partial, factor, flow_values, *to_x[1:], *got_x[1:]),
        limit=8,
        flops=1000,
        moved=1000,
        name="far_ready",
    )
    n_corners = (1 + many_y) * (1 + many_z)
    result, damp, *packs = call(
        functools.partial(source, dims, many_x, many_y, many_z),
        [f32(X, Y, Z), f32(X, Y, Z)]
        + [f32(X, R, Z)] * (1 + many_y)
        + [f32(Y, Z)] * (1 + many_z)
        + [f32(4 * R, Z)] * n_corners,
        (smooth, ext, near, near_damp, *relayed),
        None,
        [extended],
        limit=8,
        name="source",
    )
    to_y, to_z, to_corner = packs[: 1 + many_y], packs[1 + many_y : -n_corners], packs[-n_corners:]
    got_y2 = some(exchange("gy", ny, *pair(to_y)))

    step = 2
    (adjoint_next,) = call(
        functools.partial(collide, dims, many_x, many_y, many_z, step),
        [f32(Q, X, Y, Z)],
        (adjoint, base, flow_values, damp, mask, *got_y, *got_z, *got_x),
        None,
        [pltpu.VMEM((Q, X, Y, Z), jnp.float32), dma((X // step,))],
        out_specs=(hbm,),
        limit=8,
        flops=300 * cells,
        moved=44 * 4 * cells,
        name="collide",
    )

    corners = [
        swap_corner(to_corner[m * (1 + many_z) + n], (ny, nz), m, n)
        for m in range(1 + many_y)
        for n in range(1 + many_z)
    ]
    got_z2 = some(exchange("gz", nz, *pair(to_z)))
    (own,) = call(
        functools.partial(own_z, dims),
        [f32(X * Y, Z)],
        (weights, result),
        limit=4,
        flops=1000,
        moved=1000,
        name="own_z",
    )
    (smooth,) = call(
        functools.partial(smooth_yz, dims, many_y),
        [f32(X, Y, Z)],
        (in_hbm(adjoint_next), weights, own, *got_y2),
        [hbm] + vmem(2 + len(got_y2)),
        [pltpu.VMEM((X, Y + 2 * R, Z), jnp.float32)],
        limit=4,
        name="smooth_yz",
    )
    (sensitivity,) = call(
        functools.partial(add_halo, dims, many_y, many_z),
        [f32(X, Y, Z)],
        (weights, smooth, *got_z2, *corners),
        None,
        [pltpu.VMEM((Y + 2 * R, Z), jnp.float32), pltpu.VMEM((X, Y, Z), jnp.float32), dma((4,))],
        out_specs=(hbm,),
        limit=4,
        name="add_halo",
    )
    return adjoint_next, sensitivity


def solution(mesh):
    counts = tuple(mesh.shape[a] for a in ("gx", "gy", "gz"))
    populations, field = P(None, "gx", "gy", "gz"), P("gx", "gy", "gz")
    return jax.shard_map(
        functools.partial(local, counts),
        mesh=mesh,
        in_specs=(populations, populations, field, field),
        out_specs=(populations, field),
        check_vma=False,
    )
```

```python
import functools
import math

import jax
import jax.numpy as jnp
import numpy as np
from jax import lax
from jax.experimental import pallas as pl
from jax.experimental.pallas import tpu as pltpu
from jax.sharding import PartitionSpec as P

Q = 19
R = 8

velocity = [
    (0, 0, 0),
    (1, 0, 0),
    (-1, 0, 0),
    (0, 1, 0),
    (0, -1, 0),
    (0, 0, 1),
    (0, 0, -1),
    (1, 1, 0),
    (-1, -1, 0),
    (1, -1, 0),
    (-1, 1, 0),
    (1, 0, 1),
    (-1, 0, -1),
    (1, 0, -1),
    (-1, 0, 1),
    (0, 1, 1),
    (0, -1, -1),
    (0, 1, -1),
    (0, -1, 1),
]
relax_rate = 1.25
sharpness = 64.0
threshold = 0.5
damping_max = 10.0
ramp_shape = 0.1


def fields_of(axis, sign):
    plus = [q for q in range(Q) if velocity[q][axis] == 1]
    return plus if sign > 0 else [q + 1 if q % 2 else q - 1 for q in plus]


PLUS = [fields_of(a, 1) for a in range(3)]
MINUS = [fields_of(a, -1) for a in range(3)]


def tap_weights():
    spread_width = R / 2.0
    unscaled = [math.exp(-((k - R) ** 2) / (2.0 * spread_width * spread_width)) for k in range(2 * R + 1)]
    summed = sum(unscaled)
    return [v / summed for v in unscaled]


TAPS = tap_weights()


def band(length):
    out = np.zeros((3, length, length), np.float32)
    for i in range(length):
        for k in range(-R, R + 1):
            j = i + k
            if j < 0:
                out[1, j + length, i] = TAPS[k + R]
            elif j >= length:
                out[2, j - length, i] = TAPS[k + R]
            else:
                out[0, j, i] = TAPS[k + R]
    return out


def packed_band(dims):
    X, Y, Z = dims
    out = np.zeros((2, 2, Z, Z), np.float32)
    for above_x in range(2):
        for above_z in range(2):
            for e in range(X):
                for i in range(X):
                    for z in range(R):
                        for j in range(R):
                            kx = i - e + 2 * R * above_x
                            kz = j - z + 2 * R * above_z
                            if 0 <= kx <= 2 * R and 0 <= kz <= 2 * R:
                                out[above_x, above_z, i * R + j, e * R + z] = TAPS[kx] * TAPS[kz]
    return out.reshape(4, Z, Z)


def packed_band_z(dims):
    X, Y, Z = dims
    out = np.zeros((2, Z, Z), np.float32)
    for above in range(2):
        for i in range(X):
            for z in range(R):
                for j in range(R):
                    k = j - z + 2 * R * above
                    if 0 <= k <= 2 * R:
                        out[above, i * R + j, i * R + z] = TAPS[k]
    return out


def sides(parity, even, odd):
    zero = jnp.zeros_like(even)
    if odd is None:
        return jnp.where(parity == 0, zero, even), jnp.where(parity == 0, even, zero)
    return jnp.where(parity == 0, odd, even), jnp.where(parity == 0, even, odd)


def parity_of(axis):
    return lax.rem(lax.axis_index(axis), 2)


def swap(array, axis, count, first):
    pairs = [(i, i + 1) for i in range(first, count - 1, 2)]
    return lax.ppermute(array, axis, pairs + [(b, a) for a, b in pairs])


def relay(array, axis, count):
    pairs = [(i + 2, i) for i in range(1, count - 2, 2)] + [(i - 2, i) for i in range(2, count, 2)]
    return lax.ppermute(array, axis, pairs)


def swap_corner(array, counts, first_y, first_z):
    ny, nz = counts
    pairs = []
    for a in range(first_y, ny - 1, 2):
        for c in range(first_z, nz - 1, 2):
            for d, e in ((c, c + 1), (c + 1, c)):
                pairs += [(a * nz + d, (a + 1) * nz + e), ((a + 1) * nz + e, a * nz + d)]
    return lax.ppermute(array, ("gy", "gz"), pairs)


def exchange(axis, count, even, odd):
    return swap(even, axis, count, 0), (None if odd is None else swap(odd, axis, count, 1))


def vmem(count):
    return [pl.BlockSpec(memory_space=pltpu.VMEM)] * count


def in_hbm(array):
    return pltpu.with_memory_space_constraint(array, pltpu.HBM)


def f32(*shape):
    return jax.ShapeDtypeStruct(shape, jnp.float32)


def call(body, outs, args, specs=None, scratch=(), limit=16, flops=1e6, moved=1e6, **rest):
    return pl.pallas_call(
        body,
        out_shape=outs,
        in_specs=specs or vmem(len(args)),
        out_specs=rest.pop("out_specs", tuple(vmem(len(outs)))),
        scratch_shapes=list(scratch),
        compiler_params=pltpu.CompilerParams(vmem_limit_bytes=limit * 2**20),
        cost_estimate=pl.CostEstimate(flops=int(flops), bytes_accessed=int(moved), transcendentals=0),
        **rest,
    )(*args)


def filter_rows(load):
    total = TAPS[R] * load(R)
    for k in range(R):
        total = total + TAPS[k] * (load(k) + load(2 * R - k))
    return total


def dot(a, b):
    return jnp.dot(a, b, preferred_element_type=jnp.float32, precision=lax.Precision.HIGHEST)


def row_of(ref, at):
    return ref[pl.ds(at, 1), :]


class Pull:
    def __init__(self, adj, dims, py, y_even, y_odd, pz=None, z_even=None, z_odd=None):
        self.adj, self.dims = adj, dims
        self.py, self.y_even, self.y_odd = py, y_even, y_odd
        self.pz, self.z_even, self.z_odd = pz, z_even, z_odd
        X, Y, Z = dims
        self.row = lax.broadcasted_iota(jnp.int32, (Y, Z), 0)
        self.lane = lax.broadcasted_iota(jnp.int32, (Y, Z), 1)

    def along_y(self, q, x):
        X, Y, Z = self.dims
        here = self.adj[q, x]
        cy = velocity[q][1]
        if cy == 0:
            return here
        at = X * R + X * (PLUS if cy > 0 else MINUS)[1].index(q) + x
        even = row_of(self.y_even, at)
        odd = None if self.y_odd is None else row_of(self.y_odd, at)
        below, above = sides(self.py, even, odd)
        if cy > 0:
            return jnp.where(self.row == Y - 1, above, pltpu.roll(here, Y - 1, 0))
        return jnp.where(self.row == 0, below, pltpu.roll(here, 1, 0))

    def faces(self, x):
        even = self.z_even[x]
        odd = None if self.z_odd is None else self.z_odd[x]
        return sides(self.pz, even, odd)

    def both(self, q, x, faces):
        X, Y, Z = self.dims
        here = self.along_y(q, x)
        cz = velocity[q][2]
        if cz == 0:
            return here
        below, above = faces
        if cz > 0:
            j = PLUS[2].index(q)
            face = pltpu.roll(above, 4 - j, 1) if j != 4 else above
            return jnp.where(self.lane == Z - 1, face, pltpu.roll(here, Z - 1, 1))
        j = MINUS[2].index(q)
        face = pltpu.roll(below, Z - j, 1) if j else below
        return jnp.where(self.lane == 0, face, pltpu.roll(here, 1, 1))


def refs_of(refs, odd):
    even = next(refs)
    return even, (next(refs) if odd else None)


def pack_y(dims, many, adj, design, *rest):
    X, Y, Z = dims
    outs = rest[: 1 + many]
    kept, tiles, sems, kept_sem = rest[1 + many :]
    py = parity_of("gy")
    keep = pltpu.make_async_copy(design, kept, kept_sem)
    keep.start()

    def copies(n, up):
        names = (MINUS if up else PLUS)[1]
        first = Y - R if up else 0
        return [
            pltpu.make_async_copy(adj.at[q, :, pl.ds(first, R), :], tiles.at[n, j], sems.at[n, j])
            for j, q in enumerate(names)
        ]

    def start(n, out, up):
        for c in copies(n, up):
            c.start()

    def fill(n, out, up):
        first = Y - R if up else 0
        out[: X * R, :] = kept[:, first : first + R, :].reshape(X * R, Z)
        for c in copies(n, up):
            c.wait()
        for j in range(5):
            out[X * R + X * j : X * R + X * (j + 1), :] = tiles[n, j, :, R - 1 if up else 0, :]

    def each(act):
        for n, out in enumerate(outs):
            pl.when(py == n)(functools.partial(act, n, out, True))
            pl.when(py != n)(functools.partial(act, n, out, False))

    each(start)
    keep.wait()
    each(fill)


def prepare(dims, many_z, ahead, forward, adj, *rest):
    X, Y, Z = dims
    rest = iter(rest)
    flow_ref, factor = next(rest), next(rest)
    outs = [next(rest) for _ in range(1 + many_z)]
    rising, falling, straight, members_ref, sems = rest
    pz = parity_of("gz")
    part = X // 4
    copies = [
        pltpu.make_async_copy(
            forward.at[:, pl.ds(i * part, part)], members_ref.at[:, pl.ds(i * part, part)], sems.at[i]
        )
        for i in range(4)
    ]
    for c in copies:
        c.start()
    row = lax.broadcasted_iota(jnp.int32, (Y, Z), 0)
    lane = lax.broadcasted_iota(jnp.int32, (Y, Z), 1)
    zero = jnp.zeros((Y, Z), jnp.float32)

    def along_y(q, x):
        here, cy = adj[q, x], velocity[q][1]
        if cy == 0:
            return here
        return jnp.where(row == (Y - 1 if cy > 0 else 0), zero, pltpu.roll(here, (-cy) % Y, 0))

    def both(q, x):
        here, cz = along_y(q, x), velocity[q][2]
        if cz == 0:
            return here
        return jnp.where(lane == (Z - 1 if cz > 0 else 0), zero, pltpu.roll(here, (-cz) % Z, 1))

    for a in range(3):
        rising[a, X] = zero
        falling[a, 1] = zero

    def moments(x, _):
        groups = {}
        for q in range(1, Q):
            groups.setdefault(velocity[q][0], {})[q] = both(q, x)
        level, up, down = moment_of(groups[0]), moment_of(groups[1]), moment_of(groups[-1])
        for a in range(3):
            rising[a, x] = up[a]
            falling[a, x + 2] = down[a]
        for a in range(1, 3):
            straight[a - 1, x] = level[a]
        return 0

    def layer(x, _):
        members = [members_ref[q, x] for q in range(Q)]
        inverse = 1.0 / sum(members[1:], members[0])
        total = None
        for a in range(3):
            terms = [(velocity[q][a], members[q] - members[q + 1]) for q in range(1, Q, 2) if velocity[q][a] != 0]
            vel = signed(terms) * inverse
            flow_ref[a, x] = vel
            moment = rising[a, x + 1] + falling[a, x + 1]
            if a > 0:
                moment = moment + straight[a - 1, x]
            term = vel * (vel - moment)
            total = term if total is None else total + term
        flow_ref[3, x] = inverse
        factor[x] = total
        return 0

    def fill(out, up):
        names = (MINUS if up else PLUS)[2]

        def face(x, _):
            value = zero
            for j, q in enumerate(names):
                slot = slot_of(Z, up, j)
                value = jnp.where(lane == slot, pltpu.roll(along_y(q, x), shift_of(Z, up, j), 1), value)
            out[x] = value
            return 0

        lax.fori_loop(0, X, face, 0, unroll=2)

    lax.fori_loop(0, X, moments, 0, unroll=2)
    for n, out in enumerate(outs):
        pl.when(pz == n)(functools.partial(fill, out, True))
        pl.when(pz != n)(functools.partial(fill, out, False))
    for i, c in enumerate(copies):
        c.wait()
        lax.fori_loop(i * part, (i + 1) * part, layer, 0, unroll=2)


def slot_of(Z, up, j):
    return j if up else Z - 5 + j


def shift_of(Z, up, j):
    return (slot_of(Z, up, j) - (Z - 1 if up else 0)) % Z


def extend_y(dims, pad, own, py, even, odd):
    X, Y, Z = dims
    below, above = sides(py, even, odd)
    pad[:, :R, :] = below
    pad[:, R : R + Y, :] = own
    pad[:, R + Y :, :] = above


def filter_y(dims, pad, store, step=2):
    X, Y, Z = dims
    for x in range(0, X, step):
        store(x, filter_rows(lambda k: pad[x : x + step, k : k + Y, :]))


def design_y(dims, many_y, many_z, design, *rest):
    X, Y, Z = dims
    rest = iter(rest)
    faces = [next(rest) for _ in range(1 + many_z)]
    y_even, y_odd = refs_of(rest, many_y)
    filtered = next(rest)
    outs = [next(rest) for _ in range(1 + many_z)]
    pad, edges = rest
    pz = parity_of("gz")
    py = parity_of("gy")

    def halo(ref):
        return ref[: X * R, :].reshape(X, R, Z)

    extend_y(dims, pad, design[...], py, halo(y_even), None if y_odd is None else halo(y_odd))

    def store(x, value):
        filtered[x : x + value.shape[0]] = value

    filter_y(dims, pad, store)
    row = lax.broadcasted_iota(jnp.int32, (Y, Z), 0)
    lane = lax.broadcasted_iota(jnp.int32, (Y, Z), 1)

    def fill(out, face, up):
        names = (MINUS if up else PLUS)[2]
        slanted = [(j, q) for j, q in enumerate(names) if velocity[q][1] != 0]
        for i, (j, q) in enumerate(slanted):
            edges[i] = pltpu.roll(rows_of(dims, py, y_even, y_odd, q), shift_of(Z, up, j), 1)
        first, last = slot_of(Z, up, 0), slot_of(Z, up, 4)

        def layer(x, _):
            value = jnp.where((lane >= first) & (lane <= last), face[x], filtered[x])
            for i, (j, q) in enumerate(slanted):
                at = (row == (Y - 1 if velocity[q][1] > 0 else 0)) & (lane == slot_of(Z, up, j))
                value = jnp.where(at, edges[i, pl.ds(x, 1), :], value)
            out[x] = value
            return 0

        lax.fori_loop(0, X, layer, 0, unroll=True)

    for n, (out, face) in enumerate(zip(outs, faces)):
        pl.when(pz == n)(functools.partial(fill, out, face, True))
        pl.when(pz != n)(functools.partial(fill, out, face, False))


def rows_of(dims, py, even, odd, q):
    X, Y, Z = dims
    above = velocity[q][1] > 0
    at = X * R + X * (PLUS if above else MINUS)[1].index(q)
    return sides(py, even[at : at + X, :], None if odd is None else odd[at : at + X, :])[int(above)]


def signed(terms):
    total = None
    for sign, value in terms:
        value = value if sign > 0 else -value
        total = value if total is None else total + value
    return total


def moment_of(values):
    return [
        signed([(velocity[q][a], v) for q, v in values.items() if velocity[q][a] != 0]) for a in range(3)
    ]


def halo_z(weights, pz, even, odd):
    value = dot(even, jnp.where(pz == 0, weights[2], weights[1]))
    if odd is not None:
        value = value + dot(odd, jnp.where(pz == 0, weights[1], weights[2]))
    return value


def flat(dims, ref):
    X, Y, Z = dims
    return None if ref is None else ref[...].reshape(X * Y, Z)


def own_z(dims, weights, field, out):
    out[...] = dot(flat(dims, field), weights[0])


def factor_y(dims, many_y, weights, filtered_y, flow_ref, factor, *rest):
    X, Y, Z = dims
    rest = iter(rest)
    y_even, y_odd = refs_of(rest, many_y)
    smooth, out = rest
    smooth[...] = dot(flat(dims, filtered_y), weights[0])
    out[...] = factor[...]
    py = parity_of("gy")
    row = lax.broadcasted_iota(jnp.int32, (X, Z), 0)
    lane = lax.broadcasted_iota(jnp.int32, (X, Z), 1)
    for edge, names in ((0, MINUS[1]), (Y - 1, PLUS[1])):
        values = {}
        for q in names:
            value = rows_of(dims, py, y_even, y_odd, q)
            cx, _, cz = velocity[q]
            if cx != 0:
                value = jnp.where(row == (X - 1 if cx > 0 else 0), 0.0, pltpu.roll(value, (-cx) % X, 0))
            if cz != 0:
                value = jnp.where(lane == (Z - 1 if cz > 0 else 0), 0.0, pltpu.roll(value, (-cz) % Z, 1))
            values[q] = value
        moment = moment_of(values)
        total = factor[:, edge, :]
        for a in range(3):
            total = total - flow_ref[a, :, edge, :] * moment[a]
        out[:, edge, :] = total


def faces_x(dims, out, up, factor, flow_ref, pull):
    X, Y, Z = dims
    names = (MINUS if up else PLUS)[0]
    edge = X - 1 if up else 0
    first = X - R if up else 0
    at = R * Y
    out[:at, :] = factor[first : first + R].reshape(R * Y, Z)
    faces = pull.faces(edge)
    for q in names:
        out[at : at + Y, :] = pull.both(q, edge, faces)
        at += Y
    for a in range(3):
        out[at : at + Y, :] = flow_ref[a, edge]
        at += Y


def pack_halo(dims, pz, refs, out):
    X, Y, Z = dims
    lane = lax.broadcasted_iota(jnp.int32, (Y, Z), 1)
    for n, ref in enumerate(refs):
        value = jnp.zeros((Y, Z), jnp.float32)
        for x in range(X):
            there = (lane >= R * x) & (lane < R * (x + 1))
            value = jnp.where(there, pltpu.roll(ref[x], lanes_x(dims, pz, n, x), 1), value)
        out[(R + 8 + n) * Y : (R + 9 + n) * Y, :] = value


def pack_odd(dims, many_y, many_z, adj, ahead, factor, flow_ref, *rest):
    X, Y, Z = dims
    rest = iter(rest)
    y_even, y_odd = refs_of(rest, many_y)
    z_even, z_odd = refs_of(rest, many_z)
    (out,) = rest
    px = parity_of("gx")
    pz = parity_of("gz")
    out[(R + 8) * Y :, :] = ahead[(R + 8) * Y :, :]
    pull = Pull(adj, dims, parity_of("gy"), y_even, y_odd, pz, z_even, z_odd)
    pl.when(px == 1)(lambda: faces_x(dims, out, True, factor, flow_ref, pull))
    pl.when(px != 1)(lambda: faces_x(dims, out, False, factor, flow_ref, pull))


def pack_x(dims, many_y, many_z, adj, factor_in, flow_ref, *rest):
    X, Y, Z = dims
    rest = iter(rest)
    y_even, y_odd = refs_of(rest, many_y)
    z_even, z_odd = refs_of(rest, many_z)
    out, factor = rest
    px, py, pz = parity_of("gx"), parity_of("gy"), parity_of("gz")
    pack_halo(dims, pz, [z_even, z_odd][: 1 + many_z], out)
    lane = lax.broadcasted_iota(jnp.int32, (Y, Z), 1)
    factor[...] = factor_in[...]

    def correct(ref, above):
        names = (PLUS if above else MINUS)[2]
        edge = Z - 1 if above else 0
        zero = jnp.zeros((Y, Z), jnp.float32)

        def layer(x, _):
            values = {}
            for j, q in enumerate(names):
                cx = velocity[q][0]
                face = ref[jnp.clip(x + cx, 0, X - 1)] if cx else ref[x]
                shift = (edge - slot_of(Z, not above, j)) % Z
                face = pltpu.roll(face, shift, 1) if shift else face
                if cx != 0:
                    face = jnp.where(x == (X - 1 if cx > 0 else 0), zero, face)
                values[q] = face
            moment = moment_of(values)
            change = flow_ref[0, x] * moment[0] + flow_ref[1, x] * moment[1] + flow_ref[2, x] * moment[2]
            factor[x] = factor[x] - jnp.where(lane == edge, change, zero)
            return 0

        lax.fori_loop(0, X, layer, 0, unroll=True)

    for n, ref in enumerate([z_even, z_odd][: 1 + many_z]):
        pl.when(pz == n)(functools.partial(correct, ref, True))
        pl.when(pz != n)(functools.partial(correct, ref, False))

    pull = Pull(adj, dims, py, y_even, y_odd, pz, z_even, z_odd)

    pl.when(px == 0)(lambda: faces_x(dims, out, True, factor, flow_ref, pull))
    pl.when(px != 0)(lambda: faces_x(dims, out, False, factor, flow_ref, pull))


def project(filtered):
    base = math.tanh(sharpness * threshold)
    denominator = base + math.tanh(sharpness * (1.0 - threshold))
    inner = jnp.tanh(sharpness * (filtered - threshold))
    physical = (base + inner) * (1.0 / denominator)
    steep = (sharpness / denominator) * (1.0 - inner * inner)
    inverse = 1.0 / (ramp_shape + physical)
    return physical, steep, inverse


def taps_of(X, above, e):
    shift = 2 * R + (X if above else -X) - e
    return [(TAPS[i + shift], i) for i in range(X) if 0 <= i + shift <= 2 * R]


def add_side(dims, base, layers, at, out, above):
    X, Y, Z = dims
    for e in range(X + 2 * R):
        total = base[e]
        for tap, i in taps_of(X, above, e):
            total = total + tap * layers[at + i * Y : at + (i + 1) * Y, :]
        out[e] = total


def lanes_x(dims, pz, n, x):
    Z = dims[2]
    return jnp.where(pz == n, (R * x) % Z, (R * x + R) % Z)


def layers_toward(dims, above, near):
    X = dims[0]
    if near:
        return range(2 * R, X + 2 * R) if above else range(X)
    return range(X, X + 2 * R) if above else range(2 * R)


def complete(dims, above, layers, many_z, pz, weights, partial, factor, flow_ref, own, got, smooth, ext):
    X, Y, Z = dims
    u_at, v_at, d_at = R * Y, R * Y + 5 * Y, R * Y + 8 * Y
    for e in layers:
        smooth[e] = partial[e]
        if R <= e < R + X:
            ext[e] = factor[e - R]
        elif got is None:
            ext[e] = jnp.zeros((Y, Z), jnp.float32)
        else:
            at = (e - R - X if above else e) * Y
            ext[e] = got[at : at + Y, :]
    if got is None:
        return
    lane = lax.broadcasted_iota(jnp.int32, (Y, Z), 1)
    for n in range(1 + many_z):
        above_z = jnp.where(pz == n, 1, 0)
        value = dot(got[d_at + n * Y : d_at + (n + 1) * Y, :], weights[3 + 2 * int(above) + above_z])
        first = (Z - R) * above_z
        there = (lane >= first) & (lane < first + R)
        for i in range(X):
            e = i + X * int(above)
            moved = pltpu.roll(value, lax.rem(first + Z - R * i, Z), 1)
            smooth[e] = smooth[e] + jnp.where(there, moved, 0.0)

    def moment(ref, names):
        return moment_of({q: ref[u_at + j * Y : u_at + (j + 1) * Y, :] for j, q in enumerate(names)})

    def less(e, vel, m):
        ext[e] = ext[e] - (vel[0] * m[0] + vel[1] * m[1] + vel[2] * m[2])

    inner, outer = (R + X - 1, R + X) if above else (R, R - 1)
    there, here = (PLUS[0], MINUS[0]) if above else (MINUS[0], PLUS[0])
    less(inner, [flow_ref[a, inner - R] for a in range(3)], moment(got, there))
    less(outer, [got[v_at + a * Y : v_at + (a + 1) * Y, :] for a in range(3)], moment(own, here))


def half_source(dims, above, layers, smooth, relayed, ext, new, damp, base, result):
    X, Y, Z = dims
    slope = -damping_max * ramp_shape * (1.0 + ramp_shape)
    for e in layers:
        total = smooth[e]
        if relayed is not None:
            for tap, i in taps_of(X, above, e):
                total = total + tap * relayed[i * Y : (i + 1) * Y, :]
        physical, steep, inverse = project(total)
        new[e] = (slope * steep) * (inverse * inverse) * ext[e]
        if R <= e < R + X:
            damp[e - R] = (2.0 * damping_max * ramp_shape) * (1.0 - physical) * inverse
    for x in range(X):
        terms = [TAPS[e - x] * new[e] for e in layers if 0 <= e - x <= 2 * R]
        if base is not None:
            terms = [base[x]] + terms
        result[x] = sum(terms[1:], terms[0]) if terms else jnp.zeros((Y, Z), jnp.float32)


def near_x(dims, many_z, weights, partial, factor, flow_ref, own, got, result, damp, smooth, ext):
    px, pz = parity_of("gx"), parity_of("gz")

    def act(above):
        layers = layers_toward(dims, above, True)
        complete(dims, above, layers, many_z, pz, weights, partial, factor, flow_ref, own, got, smooth, ext)
        half_source(dims, above, layers, smooth, None, ext, ext, damp, None, result)

    pl.when(px == 0)(lambda: act(True))
    pl.when(px != 0)(lambda: act(False))


def far_ready(dims, many_x, many_z, ahead, weights, partial, factor, flow_ref, *rest):
    own, got = rest[:2] if many_x else (None, None)
    smooth, ext = rest[-2:]
    px, pz = parity_of("gx"), parity_of("gz")

    def act(above):
        layers = layers_toward(dims, above, False)
        complete(dims, above, layers, many_z, pz, weights, partial, factor, flow_ref, own, got, smooth, ext)

    pl.when(px == 1)(lambda: act(True))
    pl.when(px != 1)(lambda: act(False))


def source(dims, many_x, many_y, many_z, ahead, smooth, ext, near, near_damp, *rest):
    X, Y, Z = dims
    rest = iter(rest)
    relayed = next(rest) if many_x else None
    result, damp = next(rest), next(rest)
    rows = [next(rest) for _ in range(1 + many_y)]
    to_z = [next(rest) for _ in range(1 + many_z)]
    corners = [[next(rest) for _ in range(1 + many_z)] for _ in range(1 + many_y)]
    (new,) = rest
    px, py, pz = parity_of("gx"), parity_of("gy"), parity_of("gz")
    damp[...] = near_damp[...]

    def act(above):
        layers = layers_toward(dims, above, False)
        half_source(dims, above, layers, smooth, relayed, ext, new, damp, near, result)

    pl.when(px == 1)(lambda: act(True))
    pl.when(px != 1)(lambda: act(False))
    for n, out in enumerate(rows):

        @pl.when(py == n)
        def _(out=out):
            out[...] = result[:, Y - R :, :]

        @pl.when(py != n)
        def _(out=out):
            out[...] = result[:, :R, :]

    pack_corner(dims, py, pz, result, to_z, corners)


def pack_corner(dims, py, pz, own, to_z, corners):
    X, Y, Z = dims
    lane = lax.broadcasted_iota(jnp.int32, (Y, Z), 1)
    for n, out in enumerate(to_z):
        value = jnp.zeros((Y, Z), jnp.float32)
        for x in range(X):
            shift = jnp.where(pz == n, (R * x + R) % Z, (R * x) % Z)
            there = (lane >= R * x) & (lane < R * (x + 1))
            value = jnp.where(there, pltpu.roll(own[x], shift, 1), value)
        out[...] = value
        for m, row in enumerate(corners):
            row[n][:R, :] = jnp.where(py == m, value[Y - R :], value[:R])
            row[n][R:, :] = jnp.zeros((3 * R, Z), jnp.float32)


def smooth_yz(dims, many_y, ahead, weights, own, *rest):
    X, Y, Z = dims
    rest = iter(rest)
    rows = [next(rest) for _ in range(1 + many_y)]
    result, pad = rest
    rows = [dot(ref[...].reshape(X * R, Z), weights[0]).reshape(X, R, Z) for ref in rows]
    extend_y(dims, pad, own[...].reshape(X, Y, Z), parity_of("gy"), rows[0], rows[1] if many_y else None)

    def store(x, value):
        result[x : x + value.shape[0]] = value

    filter_y(dims, pad, store)


def add_halo(dims, many_y, many_z, weights, own, *rest):
    X, Y, Z = dims
    rest = iter(rest)
    sides_z = [next(rest) for _ in range(1 + many_z)]
    corners = [[next(rest) for _ in range(1 + many_z)] for _ in range(1 + many_y)]
    out, pad, result, sems = rest
    py, pz = parity_of("gy"), parity_of("gz")
    lane = lax.broadcasted_iota(jnp.int32, (Y, Z), 1)
    moved = []
    for n in range(1 + many_z):
        below, above = sides(py, corners[0][n][:R, :], corners[1][n][:R, :] if many_y else None)
        pad[:R, :] = below
        pad[R : R + Y, :] = sides_z[n][...]
        pad[R + Y :, :] = above
        side = jnp.where(pz == n, 1, 0)
        first = (Z - R) * side
        extra = dot(filter_rows(lambda k: pad[k : k + Y, :]), weights[7 + side])
        moved.append((extra, first, (lane >= first) & (lane < first + R)))
    part = X // 4
    copies = []
    for i in range(4):
        for x in range(i * part, (i + 1) * part):
            value = own[x]
            for extra, first, there in moved:
                value = value + jnp.where(there, pltpu.roll(extra, lax.rem(first + Z - R * x, Z), 1), 0.0)
            result[x] = value
        here = pl.ds(i * part, part)
        copies.append(pltpu.make_async_copy(result.at[here], out.at[here], sems.at[i]))
        copies[-1].start()
    for c in copies:
        c.wait()


def relax(pulled, vel, speed_sq, label, drag, store):
    plus = {q: pulled[q] + pulled[q + 1] for q in range(1, Q, 2)}
    minus = {q: pulled[q] - pulled[q + 1] for q in range(1, Q, 2)}
    axes = (1, 3, 5)
    straight = plus[1] + plus[3] + plus[5]
    slanted = plus[7] + plus[9] + plus[11] + plus[13] + plus[15] + plus[17]
    zeroth = (1.0 / 3.0) * pulled[0] + (1.0 / 18.0) * straight + (1.0 / 36.0) * slanted
    first, diagonal = [], []
    for a in range(3):
        terms = [(velocity[q][a], minus[q]) for q in range(7, Q, 2) if velocity[q][a] != 0]
        first.append((1.0 / 18.0) * minus[axes[a]] + (1.0 / 36.0) * signed(terms))
        both = [(1, plus[q]) for q in range(7, Q, 2) if velocity[q][a] != 0]
        diagonal.append((1.0 / 18.0) * plus[axes[a]] + (1.0 / 36.0) * signed(both))
    xy = (1.0 / 36.0) * (plus[7] - plus[9])
    xz = (1.0 / 36.0) * (plus[11] - plus[13])
    yz = (1.0 / 36.0) * (plus[15] - plus[17])
    turned = [
        diagonal[0] * vel[0] + xy * vel[1] + xz * vel[2],
        xy * vel[0] + diagonal[1] * vel[1] + yz * vel[2],
        xz * vel[0] + yz * vel[1] + diagonal[2] * vel[2],
    ]
    quadric = vel[0] * turned[0] + vel[1] * turned[1] + vel[2] * turned[2]
    eq_scalar = zeroth * (1.0 + 1.5 * speed_sq) - 4.5 * quadric
    eq_vector = [3.0 * first[a] + 9.0 * turned[a] - 3.0 * zeroth * vel[a] for a in range(3)]
    fluid, solid, inlet = label == 0, label == 1, label == 2
    zero = jnp.zeros_like(eq_scalar)
    keep = jnp.where(fluid, 1.0 - relax_rate, zero)
    bounce = jnp.where(solid, 1.0, zero)
    level = relax_rate * eq_scalar
    tilt = [relax_rate * v for v in eq_vector]
    if drag is not None:
        level = level - drag * speed_sq
        tilt = [t + drag * v for t, v in zip(tilt, vel)]
    level = jnp.where(fluid, level, jnp.where(solid, zero, eq_scalar))
    tilt = [jnp.where(fluid, t, jnp.where(inlet, v, zero)) for t, v in zip(tilt, eq_vector)]
    store(0, (keep + bounce) * pulled[0] + level)
    for q in range(1, Q, 2):
        lean = lean_of(q, tilt)
        store(q, keep * pulled[q] + bounce * pulled[q + 1] + (level + lean))
        store(q + 1, keep * pulled[q + 1] + bounce * pulled[q] + (level - lean))


def lean_of(q, vector):
    return signed([(velocity[q][a], vector[a]) for a in range(3) if velocity[q][a] != 0])


def square(vel):
    return vel[0] * vel[0] + vel[1] * vel[1] + vel[2] * vel[2]


def far_x(dims, partial, beyond, out):
    px = parity_of("gx")
    pl.when(px == 0)(lambda: add_side(dims, partial, beyond, 0, out, True))
    pl.when(px != 0)(lambda: add_side(dims, partial, beyond, 0, out, False))


def beside_x(dims, many_y, many_z, ahead, weights, adj, flow_ref, mask, smooth, *rest):
    X, Y, Z = dims
    rest = iter(rest)
    y_even, y_odd = refs_of(rest, many_y)
    z_even, z_odd = refs_of(rest, many_z)
    partial, base, own = rest
    own[...] = smooth[...] + halo_z(weights, parity_of("gz"), flat(dims, z_even), flat(dims, z_odd))
    for e in range(X + 2 * R):
        terms = [(i - e + 2 * R, i * Y) for i in range(X) if 0 <= i - e + 2 * R <= 2 * R]
        partial[e] = sum(TAPS[k] * own[at : at + Y, :] for k, at in terms)
    pull = Pull(adj, dims, parity_of("gy"), y_even, y_odd, parity_of("gz"), z_even, z_odd)

    def layer(x, _):
        around = {c: pull.faces(x + c) for c in (-1, 0, 1)}
        pulled = [pull.both(q, x + velocity[q][0], around[velocity[q][0]]) for q in range(Q)]
        vel = [flow_ref[a, x] for a in range(3)]

        def store(q, value):
            base[q, x] = value

        relax(pulled, vel, square(vel), mask[x], None, store)
        return 0

    lax.fori_loop(1, X - 1, layer, 0, unroll=True)


def edges_x(dims, many_x, many_y, many_z, ahead, adj, flow_ref, mask, *rest):
    X, Y, Z = dims
    rest = iter(rest)
    y_even, y_odd = refs_of(rest, many_y)
    z_even, z_odd = refs_of(rest, many_z)
    x_even, x_odd = refs_of(rest, many_x)
    (out,) = rest
    px, py, pz = parity_of("gx"), parity_of("gy"), parity_of("gz")
    pull = Pull(adj, dims, py, y_even, y_odd, pz, z_even, z_odd)
    u_at = R * Y

    def edge(x, toward):
        around = {c: pull.faces(x + c) for c in (0, -toward)}
        pulled = []
        for q in range(Q):
            cx = velocity[q][0]
            if cx == toward:
                at = u_at + Y * (PLUS if cx > 0 else MINUS)[0].index(q)
                both = sides(px, x_even[at : at + Y, :], None if x_odd is None else x_odd[at : at + Y, :])
                pulled.append(both[int(cx > 0)])
            else:
                pulled.append(pull.both(q, x + cx, around[cx]))
        vel = [flow_ref[a, x] for a in range(3)]

        def store(q, value):
            out[int(x > 0), q] = value

        relax(pulled, vel, square(vel), mask[x], None, store)

    edge(0, -1)
    edge(X - 1, 1)


def collide(dims, step, edges, base, flow_ref, damp, mask, target, out, sems):
    X, Y, Z = dims

    def layer(x):
        vel = [flow_ref[a, x] for a in range(3)]
        drag = jnp.where(mask[x] == 0, damp[x] * flow_ref[3, x], 0.0)
        level = drag * square(vel)
        tilt = [drag * v for v in vel]
        here = {0: edges.at[0], X - 1: edges.at[1]}.get(x, base.at[:, x])
        out[0, x] = here[0] - level
        for q in range(1, Q, 2):
            lean = lean_of(q, tilt)
            out[q, x] = here[q] + (lean - level)
            out[q + 1, x] = here[q + 1] - (lean + level)

    last = X // step - 1
    copies = []
    for part in [1, 0, 2, last, *range(3, last)]:
        for x in range(part * step, (part + 1) * step):
            layer(x)
        here = pl.ds(part * step, step)
        copies.append(pltpu.make_async_copy(out.at[:, here], target.at[:, here], sems.at[part]))
        copies[-1].start()
    for c in copies:
        c.wait()


def local(counts, forward, adjoint, design, mask):
    many_x, many_y, many_z = (int(n > 2) for n in counts)
    nx, ny, nz = counts
    dims = design.shape
    X, Y, Z = dims
    weights = jnp.asarray(np.concatenate([band(Z), packed_band(dims), packed_band_z(dims)]))
    hbm = pl.BlockSpec(memory_space=pltpu.HBM)
    cells = X * Y * Z
    some = lambda pair: [v for v in pair if v is not None]
    pair = lambda items: (items[0], items[1] if len(items) > 1 else None)
    dma = pltpu.SemaphoreType.DMA

    y_rows = X * R + 5 * X
    *to_y, design = call(
        functools.partial(pack_y, dims, many_y),
        [f32(y_rows, Z)] * (1 + many_y) + [f32(X, Y, Z)],
        (in_hbm(adjoint), in_hbm(design)),
        [hbm, hbm],
        [pltpu.VMEM((1 + many_y, 5, X, R, Z), jnp.float32), dma((1 + many_y, 5)), dma],
        limit=4,
        name="pack_y",
    )
    got_y = some(exchange("gy", ny, *pair(to_y)))

    flow_values, factor, *faces = call(
        functools.partial(prepare, dims, many_z),
        [f32(4, X, Y, Z)] + [f32(X, Y, Z)] * (2 + many_z),
        (to_y[0], in_hbm(forward), adjoint),
        vmem(1) + [hbm] + vmem(1),
        [pltpu.VMEM((3, X + 2, Y, Z), jnp.float32)] * 2
        + [pltpu.VMEM((2, X, Y, Z), jnp.float32), pltpu.VMEM((Q, X, Y, Z), jnp.float32), dma((4,))],
        limit=16,
        flops=200 * cells,
        moved=44 * 4 * cells,
        name="prepare",
    )

    filtered_y, *to_z = call(
        functools.partial(design_y, dims, many_y, many_z),
        [f32(X, Y, Z)] * (2 + many_z),
        (design, *faces, *got_y),
        None,
        [pltpu.VMEM((X, Y + 2 * R, Z), jnp.float32), pltpu.VMEM((2, X, Z), jnp.float32)],
        limit=8,
        name="design_y",
    )
    got_z = some(exchange("gz", nz, *pair(to_z)))

    smooth, factor = call(
        functools.partial(factor_y, dims, many_y),
        [f32(X * Y, Z), f32(X, Y, Z)],
        (weights, filtered_y, flow_values, factor, *got_y),
        limit=8,
        flops=200 * cells,
        name="factor_y",
    )
    beyond = swap(smooth, "gx", nx, 0)

    x_rows = R * Y + 8 * Y
    even, factor = call(
        functools.partial(pack_x, dims, many_y, many_z),
        [f32(x_rows + (1 + many_z) * Y, Z), f32(X, Y, Z)],
        (adjoint, factor, flow_values, *got_y, *got_z),
        limit=16,
        name="pack_x",
    )
    to_x = [even]
    if many_x:
        to_x += call(
            functools.partial(pack_odd, dims, many_y, many_z),
            [f32(x_rows + (1 + many_z) * Y, Z)],
            (adjoint, even, factor, flow_values, *got_y, *got_z),
            limit=16,
            name="pack_odd",
        )
    got_x = some(exchange("gx", nx, *pair(to_x)))

    partial, base = call(
        functools.partial(beside_x, dims, many_y, many_z),
        [f32(X + 2 * R, Y, Z), f32(Q, X, Y, Z)],
        (to_x[-1], weights, adjoint, flow_values, mask, smooth, *got_y, *got_z),
        None,
        [pltpu.VMEM((X * Y, Z), jnp.float32)],
        limit=16,
        flops=100000 * cells,
        moved=1000,
        name="beside_x",
    )
    (partial,) = call(
        functools.partial(far_x, dims),
        [f32(X + 2 * R, Y, Z)],
        (partial, beyond),
        limit=8,
        flops=1000,
        moved=1000,
        name="far_x",
    )
    relayed = [relay(beyond, "gx", nx)] if many_x else []

    extended = pltpu.VMEM((X + 2 * R, Y, Z), jnp.float32)
    near, near_damp = call(
        functools.partial(near_x, dims, many_z),
        [f32(X, Y, Z), f32(X, Y, Z)],
        (weights, partial, factor, flow_values, to_x[0], got_x[0]),
        None,
        [extended] * 2,
        limit=8,
        flops=1000,
        moved=1000,
        name="near_x",
    )
    smooth, ext = call(
        functools.partial(far_ready, dims, many_x, many_z),
        [f32(X + 2 * R, Y, Z)] * 2,
        (near, weights, partial, factor, flow_values, *to_x[1:], *got_x[1:]),
        limit=8,
        flops=1000,
        moved=1000,
        name="far_ready",
    )
    (edges,) = call(
        functools.partial(edges_x, dims, many_x, many_y, many_z),
        [f32(2, Q, Y, Z)],
        (smooth, adjoint, flow_values, mask, *got_y, *got_z, *got_x),
        limit=8,
        flops=1000,
        moved=1000,
        name="edges_x",
    )
    n_corners = (1 + many_y) * (1 + many_z)
    result, damp, *packs = call(
        functools.partial(source, dims, many_x, many_y, many_z),
        [f32(X, Y, Z), f32(X, Y, Z)]
        + [f32(X, R, Z)] * (1 + many_y)
        + [f32(Y, Z)] * (1 + many_z)
        + [f32(4 * R, Z)] * n_corners,
        (edges, smooth, ext, near, near_damp, *relayed),
        None,
        [extended],
        limit=8,
        name="source",
    )
    to_y, to_z, to_corner = packs[: 1 + many_y], packs[1 + many_y : -n_corners], packs[-n_corners:]
    got_y2 = some(exchange("gy", ny, *pair(to_y)))

    step = 2
    (adjoint_next,) = call(
        functools.partial(collide, dims, step),
        [f32(Q, X, Y, Z)],
        (edges, base, flow_values, damp, mask),
        None,
        [pltpu.VMEM((Q, X, Y, Z), jnp.float32), dma((X // step,))],
        out_specs=(hbm,),
        limit=8,
        flops=300 * cells,
        moved=44 * 4 * cells,
        name="collide",
    )

    corners = [
        swap_corner(to_corner[m * (1 + many_z) + n], (ny, nz), m, n)
        for m in range(1 + many_y)
        for n in range(1 + many_z)
    ]
    got_z2 = some(exchange("gz", nz, *pair(to_z)))
    (own,) = call(
        functools.partial(own_z, dims),
        [f32(X * Y, Z)],
        (weights, result),
        limit=4,
        flops=1000,
        moved=1000,
        name="own_z",
    )
    (smooth,) = call(
        functools.partial(smooth_yz, dims, many_y),
        [f32(X, Y, Z)],
        (in_hbm(adjoint_next), weights, own, *got_y2),
        [hbm] + vmem(2 + len(got_y2)),
        [pltpu.VMEM((X, Y + 2 * R, Z), jnp.float32)],
        limit=4,
        name="smooth_yz",
    )
    (sensitivity,) = call(
        functools.partial(add_halo, dims, many_y, many_z),
        [f32(X, Y, Z)],
        (weights, smooth, *got_z2, *corners),
        None,
        [pltpu.VMEM((Y + 2 * R, Z), jnp.float32), pltpu.VMEM((X, Y, Z), jnp.float32), dma((4,))],
        out_specs=(hbm,),
        limit=4,
        name="add_halo",
    )
    return adjoint_next, sensitivity


def solution(mesh):
    counts = tuple(mesh.shape[a] for a in ("gx", "gy", "gz"))
    populations, field = P(None, "gx", "gy", "gz"), P("gx", "gy", "gz")
    return jax.shard_map(
        functools.partial(local, counts),
        mesh=mesh,
        in_specs=(populations, populations, field, field),
        out_specs=(populations, field),
        check_vma=False,
    )
```
